32 devices in a mesh: cell: 2 (over y), seq: 4 (over z), tensor: 4 (over x, core).
Axes of the slice: x: 2, y: 2, z: 4, core: 2. Of those that a mesh axis runs over, the one named last changes fastest.
Arguments:
- tokens: bfloat16 [4, 2048, 1120], P('cell', 'seq'), may hold values from -6 to 6
- out_grad: bfloat16 [4, 2048, 1120], P('cell', 'seq'), may hold values from -6 to 6
- group_order: int32 [4, 8], P('cell'), may hold values from 0 to 7, as said below
- lengths: int32 [4], P('cell'), may hold values from 1024 to 2048, as said below
- qkv_weight: bfloat16 [2, 3, 1120, 1120], P(None, None, None, 'tensor'), may hold values from -0.1875 to 0.1875
- qv_bias: bfloat16 [2, 2, 1120], P(None, None, 'tensor'), may hold values from -0.19921875 to 0.19921875
- out_weight: bfloat16 [2, 1120, 1120], P(None, 'tensor'), may hold values from -4 to 4
- out_bias: bfloat16 [2, 1120], replicated, may hold values from -0.3984375 to 0.3984375
- up_weight: bfloat16 [2, 1120, 4480], P(None, None, 'tensor'), may hold values from -0.1875 to 0.1875
- up_bias: bfloat16 [2, 4480], P(None, 'tensor'), may hold values from -0.796875 to 0.796875
- down_weight: bfloat16 [2, 4480, 1120], P(None, 'tensor'), may hold values from -0.09375 to 0.09375
- down_bias: bfloat16 [2, 1120], replicated, may hold values from -0.3984375 to 0.3984375
- norm_gain: bfloat16 [2, 2, 1120], replicated, may hold values from 0.099609375 to 1.8984375
- norm_shift: bfloat16 [2, 2, 1120], replicated, may hold values from -0.3984375 to 0.3984375
Outputs:
- block_out: bfloat16 [4, 2048, 1120], P('cell', 'seq')
- tokens_grad: bfloat16 [4, 2048, 1120], P('cell', 'seq')
- qkv_weight_grad: float32 [2, 3, 1120, 1120], P(None, None, None, 'tensor')
- qv_bias_grad: float32 [2, 2, 1120], P(None, None, 'tensor')
- out_weight_grad: float32 [2, 1120, 1120], P(None, 'tensor')
- out_bias_grad: float32 [2, 1120], replicated
- up_weight_grad: float32 [2, 1120, 4480], P(None, None, 'tensor')
- up_bias_grad: float32 [2, 4480], P(None, 'tensor')
- down_weight_grad: float32 [2, 4480, 1120], P(None, 'tensor')
- down_bias_grad: float32 [2, 1120], replicated
- norm_gain_grad: float32 [2, 2, 1120], replicated
- norm_shift_grad: float32 [2, 2, 1120], replicated
The draws below stay inside these ranges and needn't reach their ends.
Inputs may be any that keep to these rules, and one draw needn't show every extreme that they name: `group_order`: each row is a permutation of 0 to 7 in which entries 2s and 2s + 1 are j and 7 - j for some j. tokens at places from lengths onward are padding, which no query attends to.
All inputs are finite; a program needn't handle non-finite values.
Results may differ from the reference program's by a relative error of at most 0.024.
Values may be sent and summed in bfloat16 or wider, within the bound.
A program may use at most 384 MiB of HBM per device.

```python
import jax
import jax.numpy as jnp
from jax import lax

D = 1120
HEADS = 20
HEAD = 56
FF = 4480
LAYERS = 2
TOK_DEV = 512
LENGTH = 2048
CELLS = 4
SLOTS = 8
N_SEQ = 4


def draw_group_order(key, part):
    key = jax.random.fold_in(key, 11)

    def one_row(row_key):
        pair_key, flip_key = jax.random.split(row_key)
        pairs = jax.random.permutation(pair_key, N_SEQ).astype(jnp.int32)
        flips = jax.random.randint(flip_key, (N_SEQ,), 0, 2)
        lower = pairs
        upper = SLOTS - 1 - pairs
        first = jnp.where(flips == 1, upper, lower)
        second = jnp.where(flips == 1, lower, upper)
        return jnp.stack([first, second], axis=1).reshape(SLOTS)
    return jax.vmap(one_row)(jax.random.split(key, CELLS)).astype(jnp.int32)


def draw_lengths(key, part):
    key = jax.random.fold_in(key, 23)
    base_key, order_key = jax.random.split(key)
    drawn = jax.random.randint(base_key, (CELLS,), LENGTH // 2, LENGTH + 1)
    picked = jax.random.permutation(order_key, CELLS)
    drawn = drawn.at[picked[0]].set(LENGTH)
    drawn = drawn.at[picked[1]].set(LENGTH // 2)
    return drawn.astype(jnp.int32)


def block_scale(own_key, shape, cuts, least, high):
    factor_of, own = 1.0, jax.random.fold_in(own_key, 6)
    for dim, parts in cuts:
        draws = jnp.exp(jax.random.uniform(jax.random.fold_in(own, dim), (parts,), jnp.float32, least / len(cuts), high / len(cuts)))
        factor_of = factor_of * jnp.repeat(draws, shape[dim] // parts).reshape([-1 if axis == dim else 1 for axis in range(len(shape))])
    return factor_of


def normal_values(key, extent, width, reach, cuts=(), held_as=jnp.bfloat16):
    values = jax.random.normal(key, extent, jnp.float32) * width
    if len(cuts) > 0:
        values = block_scale(key, extent, cuts, -0.22, 0.18) * values
    return jnp.clip(values, min=-reach, max=reach).astype(held_as)


def setup_inputs(seed: int = 0) -> dict:
    splits = jax.random.split(jax.random.key(seed), 15)
    return {
        "tokens": normal_values(splits[0], (CELLS, LENGTH, D), 1.0, 6.0, ((0, 2), (1, 4))),
        "out_grad": normal_values(splits[1], (CELLS, LENGTH, D), 1.0, 6.0, ((0, 2), (1, 4))),
        "group_order": draw_group_order(jax.random.fold_in(splits[14], 71), 0),
        "lengths": draw_lengths(jax.random.fold_in(splits[14], 71), 0),
        "qkv_weight": normal_values(splits[4], (LAYERS, 3, D, D), D ** -0.5, 0.1875, ((3, 4),)),
        "qv_bias": normal_values(splits[5], (LAYERS, 2, D), 0.05, 0.19921875, ((2, 4),)),
        "out_weight": normal_values(splits[6], (LAYERS, D, D), (max(D // 512, 1)) ** -0.5, 4.0, ((1, 4),)),
        "out_bias": normal_values(splits[7], (LAYERS, D), 0.1, 0.3984375),
        "up_weight": normal_values(splits[8], (LAYERS, D, FF), D ** -0.5, 0.1875, ((2, 4),)),
        "up_bias": normal_values(splits[9], (LAYERS, FF), 0.2, 0.796875, ((1, 4),)),
        "down_weight": normal_values(splits[10], (LAYERS, FF, D), FF ** -0.5, 0.09375, ((1, 4),)),
        "down_bias": normal_values(splits[11], (LAYERS, D), 0.1, 0.3984375),
        "norm_gain": jnp.clip(1.0 + 0.18 * jax.random.normal(splits[12], (LAYERS, 2, D), jnp.float32), 0.099609375, 1.8984375).astype(jnp.bfloat16),
        "norm_shift": normal_values(splits[13], (LAYERS, 2, D), 0.1, 0.3984375),
    }


@jax.custom_vjp
def low(v):
    return lax.optimization_barrier(v.astype(jnp.bfloat16)).astype(jnp.float32)

@jax.custom_vjp
def low_back(v):
    return v

def low_keep(v):
    return (low(v), None)

def low_pass(kept, grad):
    return (grad,)

def back_keep(v):
    return (v, None)

def back_low(kept, grad):
    return (low(grad),)
low.defvjp(low_keep, low_pass)
low_back.defvjp(back_keep, back_low)
EPSILON = 1e-05
MASKED = -1e+30
ROOT_TWO_PI = 0.7978845608028654
CUBIC = 0.044715
HIGHEST = lax.Precision.HIGHEST

def layer_norm(values, gain_row, offset_row):
    centred = values - lax.optimization_barrier(jnp.mean(values, axis=-1, keepdims=True))
    spread = lax.optimization_barrier(jnp.mean(centred * centred, axis=-1, keepdims=True))
    return centred * lax.rsqrt(spread + EPSILON) * gain_row + offset_row

def gelu_tanh(values):
    return 0.5 * values * (1.0 + jnp.tanh(ROOT_TWO_PI * (values + CUBIC * values * values * values)))

def cell_places(order_row):
    half_rows = TOK_DEV // 2
    stored = jnp.arange(LENGTH, dtype=jnp.int32)
    return order_row[stored // half_rows] * half_rows + stored % half_rows

def attention(queries, keys_all, values_all, places, length_cell):
    block_rows = 512 if LENGTH % 512 == 0 else LENGTH
    block_count = LENGTH // block_rows
    score_scale = HEAD ** (-0.5)

    def one_block(pieces):
        query_block, place_block = pieces
        scores = jnp.einsum('qhe,khe->hqk', query_block, keys_all, precision=HIGHEST) * score_scale
        scores = low_back(scores)
        allowed = (places[None, :] <= place_block[:, None]) & (places[None, :] < length_cell)
        scores = jnp.where(allowed[None], scores, MASKED)
        row_max = lax.optimization_barrier(jnp.max(scores, axis=-1, keepdims=True))
        weights = jnp.exp(scores - row_max)
        softmax_rows = weights / lax.optimization_barrier(jnp.sum(weights, axis=-1, keepdims=True))
        return jnp.einsum('hqk,khe->qhe', low(softmax_rows), values_all, precision=HIGHEST)
    query_blocks = queries.reshape(block_count, block_rows, HEADS, HEAD)
    place_blocks = places.reshape(block_count, block_rows)
    mixed_rows = lax.map(jax.checkpoint(one_block), (query_blocks, place_blocks))
    return mixed_rows.reshape(LENGTH, HEADS * HEAD)

def forward(stream, qkv_weight, qv_bias, out_weight, out_bias, up_weight, up_bias, down_weight, down_bias, norm_gain, norm_shift, places, length_cell):
    head_shape = (LENGTH, HEADS, HEAD)
    for layer_index in range(LAYERS):
        normed = low(layer_norm(stream, norm_gain[layer_index, 0], norm_shift[layer_index, 0]))
        projected = jnp.einsum('td,jde->jte', normed, qkv_weight[layer_index], precision=HIGHEST)
        queries = low(low_back(projected[0] + qv_bias[layer_index, 0]))
        keys_all = low(low_back(projected[1]))
        values_all = low(low_back(projected[2] + qv_bias[layer_index, 1]))
        mixed_rows = attention(queries.reshape(head_shape), keys_all.reshape(head_shape), values_all.reshape(head_shape), places, length_cell)
        mixed_rows = low(low_back(mixed_rows))
        stream = stream + low_back(jnp.dot(mixed_rows, out_weight[layer_index], precision=HIGHEST)) + out_bias[layer_index]
        normed = low(layer_norm(stream, norm_gain[layer_index, 1], norm_shift[layer_index, 1]))
        hidden = low_back(jnp.dot(normed, up_weight[layer_index], precision=HIGHEST) + up_bias[layer_index])
        hidden = low(low_back(gelu_tanh(hidden)))
        stream = stream + low_back(jnp.dot(hidden, down_weight[layer_index], precision=HIGHEST)) + down_bias[layer_index]
    return stream

def reference(tokens, out_grad, group_order, lengths, qkv_weight, qv_bias, out_weight, out_bias, up_weight, up_bias, down_weight, down_bias, norm_gain, norm_shift):
    params = tuple((member.astype(jnp.float32) for member in (qkv_weight, qv_bias, out_weight, out_bias, up_weight, up_bias, down_weight, down_bias, norm_gain, norm_shift)))

    def one_cell(totals, inputs):
        cell_tokens, cell_grad, order_row, length_cell = inputs
        places = cell_places(order_row)

        def run(stream, *weights):
            return forward(stream, *weights, places, length_cell)
        result, pull_back = jax.vjp(run, cell_tokens.astype(jnp.float32), *params)
        gradients = pull_back(cell_grad.astype(jnp.float32))
        totals = tuple((running + gradient for running, gradient in zip(totals, gradients[1:])))
        return (totals, (result.astype(jnp.bfloat16), gradients[0].astype(jnp.bfloat16)))
    zeros = tuple((jnp.zeros_like(member) for member in params))
    totals, (block_out, tokens_grad) = lax.scan(one_cell, zeros, (tokens, out_grad, group_order, lengths))
    return (block_out, tokens_grad, totals[0], totals[1], totals[2], totals[3], totals[4], totals[5], totals[6], totals[7], totals[8], totals[9])
```

```python
import functools

import jax
import jax.numpy as jnp
from jax import lax
from jax.experimental import pallas as pl
from jax.experimental.pallas import tpu as pltpu
from jax.sharding import PartitionSpec as P

HEAD = 56
EPSILON = 1e-05
MASKED = -1e30
ROOT_TWO_PI = 0.7978845608028654
CUBIC = 0.044715
LOG2E = 1.4426950408889634
F32 = jnp.float32
BF16 = jnp.bfloat16


def swap(values, axis, bit):
    size = lax.axis_size(axis)
    return lax.ppermute(values, axis, [(i, i ^ bit) for i in range(size)])


def shift_right(values, axis):
    size = lax.axis_size(axis)
    return lax.ppermute(values, axis, [(i, (i + 1) % size) for i in range(size)])


def normalize(values):
    centred = values - jnp.mean(values, axis=-1, keepdims=True)
    spread = jnp.mean(centred * centred, axis=-1, keepdims=True)
    inverse = lax.rsqrt(spread + EPSILON)
    return (centred * inverse, inverse)


def norm_back(incoming, normed, inverse, gain_row):
    scaled = incoming * gain_row
    first_mean = jnp.mean(scaled, axis=-1, keepdims=True)
    second_mean = jnp.mean(scaled * normed, axis=-1, keepdims=True)
    return inverse * (scaled - first_mean - normed * second_mean)


def gelu_both(values):
    inner = jnp.tanh(ROOT_TWO_PI * (values + CUBIC * values * values * values))
    hidden = 0.5 * values * (1.0 + inner)
    slope = 0.5 * (1.0 + inner) + 0.5 * values * (1.0 - inner * inner) * ROOT_TWO_PI * (
        1.0 + 3.0 * CUBIC * values * values
    )
    return hidden.astype(BF16), slope.astype(BF16)


def contract(left, right, left_dim, right_dim):
    return lax.dot_general(
        left, right, (((left_dim,), (right_dim,)), ((), ())), preferred_element_type=F32
    )


def score_block(info, keys, queries, key_block, query_block, masked):
    scores = contract(keys, queries, 0, 0)
    if masked:
        rows = scores.shape[0]
        key_place = key_block * rows + lax.broadcasted_iota(jnp.int32, scores.shape, 0)
        query_place = query_block * rows + lax.broadcasted_iota(jnp.int32, scores.shape, 1)
        allowed = (key_place <= query_place) & (key_place < info[2])
        scores = jnp.where(allowed, scores, MASKED)
    return scores


def for_blocks(info, ring, block_rows, work):
    def one(step, carry):
        key_half, query_half = step // 2, step % 2
        key_block, query_block = info[3 + 2 * ring + key_half], info[query_half]
        first = key_block * block_rows
        counts = (key_block <= query_block) & (first < info[2])
        partial = (key_block == query_block) | (first + block_rows > info[2])

        @pl.when(counts & partial)
        def _():
            work(key_half, query_half, key_block, query_block, True)

        @pl.when(counts & jnp.logical_not(partial))
        def _():
            work(key_half, query_half, key_block, query_block, False)

        return carry

    lax.fori_loop(0, 4, one, 0)


def attend_kernel(info, queries, *refs):
    rings = len(refs) - 5
    pairs = refs[:rings]
    mixed, log_total, top, total, sums = refs[rings:]
    heads, head_size, tokens = queries.shape
    rows = tokens // 2
    factor = head_size**-0.5 * LOG2E
    top[...] = jnp.full_like(top, MASKED)
    total[...] = jnp.zeros_like(total)
    sums[...] = jnp.zeros_like(sums)
    for ring in range(rings):
        pair = pairs[ring]

        def work(key_half, query_half, key_block, query_block, masked, pair=pair):
            key_at = pl.ds(pl.multiple_of(key_half * rows, rows), rows)
            query_at = pl.ds(pl.multiple_of(query_half * rows, rows), rows)
            for head in range(heads):
                scores = score_block(
                    info,
                    pair[0, head, :, key_at],
                    queries[head, :, query_at],
                    key_block,
                    query_block,
                    masked,
                )
                old = top[head, :, query_at]
                new = jnp.maximum(old, jnp.max(scores, axis=0, keepdims=True) * factor)
                decay = jnp.exp2(old - new)
                weights = jnp.exp2(scores * factor - new)
                top[head, :, query_at] = new
                total[head, :, query_at] = total[head, :, query_at] * decay + jnp.sum(
                    weights, axis=0, keepdims=True
                )
                sums[head, :, query_at] = sums[head, :, query_at] * decay + contract(
                    pair[1, head, :, key_at], weights.astype(BF16), 1, 0
                )

        for_blocks(info, ring, rows, work)
    for head in range(heads):
        mixed[head] = (sums[head] / total[head]).astype(BF16)
        log_total[head] = top[head] + jnp.log2(total[head])


def attend_back_kernel(info, queries, grad_mixed, mixed, log_total, *refs):
    rings = (len(refs) - 4) // 2
    pairs = refs[:rings]
    grad_queries = refs[rings]
    grad_pairs = refs[rings + 1 : 2 * rings + 1]
    inner, sums, pair_sums = refs[2 * rings + 1 :]
    heads, head_size, tokens = queries.shape
    rows = tokens // 2
    scale = head_size**-0.5
    factor = scale * LOG2E
    for head in range(heads):
        inner[head] = jnp.sum(
            grad_mixed[head].astype(F32) * mixed[head].astype(F32), axis=0, keepdims=True
        )
    sums[...] = jnp.zeros_like(sums)
    for ring in range(rings):
        pair = pairs[ring]
        pair_sums[...] = jnp.zeros_like(pair_sums)

        def work(key_half, query_half, key_block, query_block, masked, pair=pair):
            key_at = pl.ds(pl.multiple_of(key_half * rows, rows), rows)
            query_at = pl.ds(pl.multiple_of(query_half * rows, rows), rows)
            for head in range(heads):
                keys, values = pair[0, head, :, key_at], pair[1, head, :, key_at]
                query_part, grad_part = queries[head, :, query_at], grad_mixed[head, :, query_at]
                scores = score_block(info, keys, query_part, key_block, query_block, masked)
                probs = jnp.exp2(scores * factor - log_total[head, :, query_at])
                grad_probs = contract(values, grad_part, 0, 0)
                grad_scores = (probs * (grad_probs - inner[head, :, query_at])).astype(BF16)
                pair_sums[1, head, :, key_at] += contract(grad_part, probs.astype(BF16), 1, 1)
                pair_sums[0, head, :, key_at] += contract(query_part, grad_scores, 1, 1)
                sums[head, :, query_at] += contract(keys, grad_scores, 1, 0)

        for_blocks(info, ring, rows, work)
        grad_pairs[ring][0] = (pair_sums[0] * scale).astype(BF16)
        grad_pairs[ring][1] = pair_sums[1].astype(BF16)
    grad_queries[...] = (sums[...] * scale).astype(BF16)


def kernel_cost(shape, rings, matmuls):
    heads, head_size, tokens = shape
    pairs = heads * tokens * tokens * rings
    return pl.CostEstimate(
        flops=2 * pairs * 256 * matmuls // 2,
        bytes_accessed=2 * heads * head_size * tokens * (2 * rings + 2),
        transcendentals=pairs // 2,
    )


def attend(info, queries, pairs):
    heads, head_size, tokens = queries.shape
    rings = len(pairs)
    vmem = pl.BlockSpec(memory_space=pltpu.VMEM)
    return pl.pallas_call(
        attend_kernel,
        out_shape=(
            jax.ShapeDtypeStruct(queries.shape, BF16),
            jax.ShapeDtypeStruct((heads, 1, tokens), F32),
        ),
        in_specs=[pl.BlockSpec(memory_space=pltpu.SMEM)] + [vmem] * (1 + rings),
        out_specs=(vmem, vmem),
        scratch_shapes=[
            pltpu.VMEM((heads, 1, tokens), F32),
            pltpu.VMEM((heads, 1, tokens), F32),
            pltpu.VMEM((heads, head_size, tokens), F32),
        ],
        compiler_params=pltpu.CompilerParams(vmem_limit_bytes=24 << 20),
        cost_estimate=kernel_cost(queries.shape, rings, 2),
    )(info, queries, *pairs)


def attend_back(info, queries, grad_mixed, mixed, log_total, pairs):
    heads, head_size, tokens = queries.shape
    rings = len(pairs)
    vmem = pl.BlockSpec(memory_space=pltpu.VMEM)
    results = pl.pallas_call(
        attend_back_kernel,
        out_shape=(jax.ShapeDtypeStruct(queries.shape, BF16),)
        + tuple(jax.ShapeDtypeStruct(pair.shape, BF16) for pair in pairs),
        in_specs=[pl.BlockSpec(memory_space=pltpu.SMEM)] + [vmem] * (4 + rings),
        out_specs=(vmem,) * (1 + rings),
        scratch_shapes=[
            pltpu.VMEM((heads, 1, tokens), F32),
            pltpu.VMEM((heads, head_size, tokens), F32),
            pltpu.VMEM((2, heads, head_size, tokens), F32),
        ],
        compiler_params=pltpu.CompilerParams(vmem_limit_bytes=32 << 20),
        cost_estimate=kernel_cost(queries.shape, rings, 5),
    )(info, queries, grad_mixed, mixed, log_total, *pairs)
    return results[0], results[1:]


def pair_order(mine, other, bit):
    return jnp.where(
        bit == 0,
        jnp.concatenate([mine, other], axis=0),
        jnp.concatenate([other, mine], axis=0),
    )


def tensor_sum(partial):
    rows = partial.shape[0] // 2
    near = swap(partial[rows:].astype(BF16), "tensor", 1)
    half = (partial[:rows] + near.astype(F32)).astype(BF16)
    far = swap(half, "tensor", 2)
    return half.astype(F32) + far.astype(F32)


def widen(mine):
    return jnp.concatenate([mine, swap(mine, "tensor", 1)], axis=0)


def add_low(kept, got):
    return (kept.astype(F32) + got.astype(F32)).astype(BF16)


def split_sum(first, second):
    cell_size = lax.axis_size("cell")
    seq_index = lax.axis_index("seq")
    if cell_size == 2:
        cell = lax.axis_index("cell")
        kept = add_low(
            jnp.where(cell == 0, first, second),
            swap(jnp.where(cell == 0, second, first), "cell", 1),
        )
    else:
        kept = lax.psum(jnp.stack([first, second]).astype(F32), "cell").astype(BF16)
        kept = kept.reshape((-1,) + first.shape[1:])
    bits = []
    step = 1
    while step < lax.axis_size("seq"):
        bit = (seq_index // step) % 2
        half = kept.shape[0] // 2
        low, high = kept[:half], kept[half:]
        kept = add_low(
            jnp.where(bit == 0, low, high),
            swap(jnp.where(bit == 0, high, low), "seq", step),
        )
        bits.append((step, bit))
        step *= 2
    for step, bit in reversed(bits):
        kept = pair_order(kept, swap(kept, "seq", step), bit)
    if cell_size == 2:
        other = swap(kept, "cell", 1)
        return jnp.where(cell == 0, kept, other), jnp.where(cell == 0, other, kept)
    kept = kept.reshape((2,) + first.shape)
    return kept[0], kept[1]


def small_sum(values):
    values = lax.psum(values, "cell") if lax.axis_size("cell") != 2 else values + swap(values, "cell", 1)
    step = 1
    while step < lax.axis_size("seq"):
        values = values + swap(values, "seq", step)
        step *= 2
    return values


def mm(left, right):
    return jnp.einsum("ab,bc->ac", left, right, preferred_element_type=F32)


def mm_right(left, right):
    return jnp.einsum("ab,cb->ac", left, right, preferred_element_type=F32)


def mm_left(left, right):
    return jnp.einsum("ab,ac->bc", left, right, preferred_element_type=F32)


def shards(
    tokens,
    out_grad,
    group_order,
    lengths,
    qkv_weight,
    qv_bias,
    out_weight,
    out_bias,
    up_weight,
    up_bias,
    down_weight,
    down_bias,
    norm_gain,
    norm_shift,
):
    cell_count, row_count, model_width = tokens.shape
    layer_count = qkv_weight.shape[0]
    local_width = qkv_weight.shape[3]
    head_count = local_width // HEAD
    rings = lax.axis_size("seq")
    half_rows = row_count // 2
    seq_index = lax.axis_index("seq")
    core = lax.axis_index("tensor") % 2
    gains = norm_gain.astype(F32)
    shifts = norm_shift.astype(F32)

    def own_first(values):
        low, high = values[:half_rows], values[half_rows:]
        return jnp.where(core == 0, low, high), jnp.where(core == 0, high, low)

    def flat(values):
        return values.reshape(values.shape[0] * values.shape[1], values.shape[2])

    infos = []
    for cell in range(cell_count):
        slots = [
            2 * ((seq_index - ring) % rings) + (core + half) % 2
            for ring in range(rings)
            for half in range(2)
        ]
        blocks = [lax.dynamic_index_in_dim(group_order[cell], s, 0, False) for s in slots]
        infos.append(jnp.stack(blocks[:2] + [lengths[cell]] + blocks).astype(jnp.int32))

    cells = range(cell_count)
    stream, wide = [None] * cell_count, [None] * cell_count
    for cell in cells:
        mine, other = own_first(tokens[cell])
        stream[cell] = mine.astype(F32)
        both = jnp.concatenate([mine, other], axis=0).astype(F32)
        wide[cell] = (normalize(both)[0] * gains[0, 0] + shifts[0, 0]).astype(BF16)

    kept = [[None] * cell_count for _ in range(layer_count)]
    block_out = [None] * cell_count
    for layer in range(layer_count):
        flat_qkv = qkv_weight[layer]
        for cell in cells:
            normed_one, inverse_one = normalize(stream[cell])
            if layer > 0:
                wide[cell] = widen(
                    (normed_one * gains[layer, 0] + shifts[layer, 0]).astype(BF16)
                )
            wide_one = wide[cell]
            projected = jnp.einsum("td,jde->jet", wide_one, flat_qkv, preferred_element_type=F32)
            shape = (head_count, HEAD, row_count)
            queries = (projected[0] + qv_bias[layer, 0][:, None]).astype(BF16).reshape(shape)
            keys = projected[1].astype(BF16).reshape(shape)
            values = (projected[2] + qv_bias[layer, 1][:, None]).astype(BF16).reshape(shape)
            pairs = [jnp.stack([keys, values])]
            for _ in range(rings - 1):
                pairs.append(shift_right(pairs[-1], "seq"))
            mixed, log_total = attend(infos[cell], queries, pairs)
            flat_mixed = mixed.reshape(local_width, row_count)
            attended = tensor_sum(mm_left(flat_mixed, out_weight[layer]))
            stream_mid = stream[cell] + attended + out_bias[layer]
            normed_two, inverse_two = normalize(stream_mid)
            wide_two = widen((normed_two * gains[layer, 1] + shifts[layer, 1]).astype(BF16))
            hidden, slope = gelu_both(mm(wide_two, up_weight[layer]) + up_bias[layer])
            lowered = tensor_sum(mm(hidden, down_weight[layer]))
            kept[layer][cell] = (
                normed_one,
                inverse_one,
                wide_one,
                queries,
                pairs,
                mixed,
                log_total,
                normed_two,
                inverse_two,
                wide_two,
                hidden,
                slope,
            )
            stream[cell] = stream_mid + lowered + down_bias[layer]
    for cell in cells:
        low = stream[cell].astype(BF16)
        block_out[cell] = pair_order(low, swap(low, "tensor", 1), core)

    grad_stream, grad_wide = [None] * cell_count, [None] * cell_count
    for cell in cells:
        mine, other = own_first(out_grad[cell])
        grad_stream[cell] = mine.astype(F32)
        grad_wide[cell] = jnp.concatenate([mine, other], axis=0)

    per_layer = [None] * layer_count
    row_vectors = [None] * layer_count
    shard_vectors = [None] * layer_count
    for layer in reversed(range(layer_count)):
        state = [dict() for _ in cells]
        for cell in cells:
            (
                normed_one,
                inverse_one,
                wide_one,
                queries,
                pairs,
                mixed,
                log_total,
                normed_two,
                inverse_two,
                wide_two,
                hidden,
                slope,
            ) = kept[layer][cell]
            now = state[cell]
            if grad_wide[cell] is None:
                grad_wide[cell] = widen(grad_stream[cell].astype(BF16))
            grad_down = grad_wide[cell]
            grad_wide[cell] = None
            now["downb"] = jnp.sum(grad_stream[cell], axis=0)
            now["down"] = mm_left(hidden, grad_down)
            grad_hidden = mm_right(grad_down, down_weight[layer]).astype(BF16)
            grad_pre = (grad_hidden.astype(F32) * slope.astype(F32)).astype(BF16)
            now["upb"] = jnp.sum(grad_pre.astype(F32), axis=0)
            now["up"] = mm_left(wide_two, grad_pre)
            grad_two = tensor_sum(mm_right(grad_pre, up_weight[layer]))
            now["gain_two"] = jnp.sum(grad_two * normed_two, axis=0)
            now["shift_two"] = jnp.sum(grad_two, axis=0)
            grad_mid = grad_stream[cell] + norm_back(
                grad_two, normed_two, inverse_two, gains[layer, 1]
            )
            now["outb"] = jnp.sum(grad_mid, axis=0)
            wide_mid = widen(grad_mid.astype(BF16))
            flat_mixed = mixed.reshape(local_width, row_count)
            now["out"] = mm_left(wide_mid, flat_mixed.T)
            grad_mixed = mm_right(out_weight[layer], wide_mid).astype(BF16)
            grad_queries, grad_pairs = attend_back(
                infos[cell], queries, grad_mixed.reshape(mixed.shape), mixed, log_total, pairs
            )
            moving = grad_pairs[1]
            for ring in range(2, rings):
                moving = add_low(grad_pairs[ring], shift_right(moving, "seq"))
            moving = add_low(grad_pairs[0], shift_right(moving, "seq"))
            grads = jnp.concatenate([grad_queries[None], moving], axis=0)
            grads = grads.reshape(3, local_width, row_count)
            sums = jnp.sum(grads.astype(F32), axis=2)
            now["qv"] = jnp.stack([sums[0], sums[2]])
            now["qkv"] = jnp.einsum("td,jet->jde", wide_one, grads, preferred_element_type=F32)
            grad_one = tensor_sum(
                jnp.einsum("jet,jde->td", grads, qkv_weight[layer], preferred_element_type=F32)
            )
            now["gain_one"] = jnp.sum(grad_one * normed_one, axis=0)
            now["shift_one"] = jnp.sum(grad_one, axis=0)
            grad_stream[cell] = grad_mid + norm_back(
                grad_one, normed_one, inverse_one, gains[layer, 0]
            )

        def over_cells(name, state=state):
            return functools.reduce(jnp.add, [now[name] for now in state])

        up, down = split_sum(over_cells("up").astype(BF16), over_cells("down").astype(BF16))
        qkv = over_cells("qkv").astype(BF16)
        out = over_cells("out").astype(BF16)
        first, second = split_sum(
            jnp.concatenate([qkv[0], qkv[1]], axis=0), jnp.concatenate([qkv[2], out], axis=0)
        )
        per_layer[layer] = (
            jnp.stack([first[:model_width], first[model_width:], second[:model_width]]),
            second[model_width:].T,
            up,
            down,
        )
        row_vectors[layer] = jnp.stack(
            [
                over_cells(name)
                for name in ("gain_one", "gain_two", "shift_one", "shift_two", "outb", "downb")
            ]
        )
        shard_vectors[layer] = jnp.concatenate(
            [over_cells("qv").reshape(-1), over_cells("upb")]
        )
    tokens_grad = [None] * cell_count
    for cell in cells:
        low = grad_stream[cell].astype(BF16)
        tokens_grad[cell] = pair_order(low, swap(low, "tensor", 1), core)

    rows = jnp.stack(row_vectors)
    rows = rows + swap(rows, "tensor", 1)
    shards_low = jnp.stack(shard_vectors)
    vector = small_sum(jnp.concatenate([rows.reshape(-1), shards_low.reshape(-1)]))
    rows = vector[: rows.size].reshape(rows.shape)
    shards_low = vector[rows.size :].reshape(shards_low.shape)
    qkv_grad, out_grad_weight, up_grad, down_grad = (
        jnp.stack([per_layer[layer][part] for layer in range(layer_count)]).astype(F32)
        for part in range(4)
    )
    return (
        jnp.stack(block_out),
        jnp.stack(tokens_grad),
        qkv_grad,
        shards_low[:, : 2 * local_width].reshape(layer_count, 2, local_width),
        out_grad_weight,
        rows[:, 4],
        up_grad,
        shards_low[:, 2 * local_width :],
        down_grad,
        rows[:, 5],
        rows[:, 0:2],
        rows[:, 2:4],
    )


def solution(mesh):
    return jax.shard_map(
        shards,
        mesh=mesh,
        in_specs=(
            P("cell", "seq", None),
            P("cell", "seq", None),
            P("cell", None),
            P("cell"),
            P(None, None, None, "tensor"),
            P(None, None, "tensor"),
            P(None, "tensor", None),
            P(),
            P(None, None, "tensor"),
            P(None, "tensor"),
            P(None, "tensor", None),
            P(),
            P(),
            P(),
        ),
        out_specs=(
            P("cell", "seq", None),
            P("cell", "seq", None),
            P(None, None, None, "tensor"),
            P(None, None, "tensor"),
            P(None, "tensor", None),
            P(),
            P(None, None, "tensor"),
            P(None, "tensor"),
            P(None, "tensor", None),
            P(),
            P(),
            P(),
        ),
        check_vma=False,
    )
```

```python
import functools
import types

import jax
import jax.numpy as jnp
from jax import lax
from jax.experimental import pallas as pl
from jax.experimental.pallas import tpu as pltpu
from jax.sharding import PartitionSpec as P

HEAD = 56
EPSILON = 1e-05
MASKED = -1e30
ROOT_TWO_PI = 0.7978845608028654
CUBIC = 0.044715
LOG2E = 1.4426950408889634
F32 = jnp.float32
BF16 = jnp.bfloat16
MESH = pl.DeviceIdType.MESH
CELL, SEQ, TENSOR = "cell", "seq", "tensor"
COPIES = 28


def swap(values, axis, bit):
    size = lax.axis_size(axis)
    return lax.ppermute(values, axis, [(i, i ^ bit) for i in range(size)])


def normalize(values):
    centred = values - jnp.mean(values, axis=-1, keepdims=True)
    spread = jnp.mean(centred * centred, axis=-1, keepdims=True)
    inverse = lax.rsqrt(spread + EPSILON)
    return (centred * inverse, inverse)


def norm_back(incoming, normed, inverse, gain_row):
    scaled = incoming * gain_row
    first_mean = jnp.mean(scaled, axis=-1, keepdims=True)
    second_mean = jnp.mean(scaled * normed, axis=-1, keepdims=True)
    return inverse * (scaled - first_mean - normed * second_mean)


def gelu_both(values):
    inner = jnp.tanh(ROOT_TWO_PI * (values + CUBIC * values * values * values))
    hidden = 0.5 * values * (1.0 + inner)
    slope = 0.5 * (1.0 + inner) + 0.5 * values * (1.0 - inner * inner) * ROOT_TWO_PI * (
        1.0 + 3.0 * CUBIC * values * values
    )
    return hidden.astype(BF16), slope.astype(BF16)


def contract(left, right, left_dim, right_dim):
    return lax.dot_general(
        left, right, (((left_dim,), (right_dim,)), ((), ())), preferred_element_type=F32
    )


def mm(left, right):
    return contract(left, right, 1, 0)


def mm_left(left, right):
    return contract(left, right, 0, 0)


def score_block(info, keys, queries, key_block, query_block, masked):
    scores = contract(keys, queries, 0, 0)
    if masked:
        rows = scores.shape[0]
        key_place = key_block * rows + lax.broadcasted_iota(jnp.int32, scores.shape, 0)
        query_place = query_block * rows + lax.broadcasted_iota(jnp.int32, scores.shape, 1)
        allowed = (key_place <= query_place) & (key_place < info[0])
        scores = jnp.where(allowed, scores, MASKED)
    return scores


def for_blocks(info, stream, chunk, block_rows, work):
    def one(step, carry):
        key_half, query_half = step // 2, step % 2
        key_block, query_block = info[5 + 2 * chunk + key_half], info[1 + 2 * stream + query_half]
        key_at = pl.ds(pl.multiple_of(key_half * block_rows, block_rows), block_rows)
        query_at = pl.ds(pl.multiple_of(query_half * block_rows, block_rows), block_rows)
        first = key_block * block_rows
        counts = (key_block <= query_block) & (first < info[0])
        partial = (key_block == query_block) | (first + block_rows > info[0])

        @pl.when(counts & partial)
        def _():
            work(key_at, query_at, key_block, query_block, True)

        @pl.when(counts & jnp.logical_not(partial))
        def _():
            work(key_at, query_at, key_block, query_block, False)

        return carry

    lax.fori_loop(0, 4, one, 0)


def attend_kernel(first_chunk, chunks, streams, resumed, last, info, *refs):
    per_stream = 4 if resumed else 1
    given = [refs[per_stream * i : per_stream * (i + 1)] for i in range(streams)]
    refs = refs[per_stream * streams :]
    pairs, refs = refs[:chunks], refs[chunks:]
    per_output = 2 if last else 3
    results = [refs[per_output * i : per_output * (i + 1)] for i in range(streams)]
    scratch = refs[per_output * streams :]
    heads, head_size, tokens = given[0][0].shape
    rows = tokens // 2
    factor = head_size**-0.5 * LOG2E
    for stream in range(streams):
        queries = given[stream][0]
        top, total, sums = (
            scratch[3 * stream : 3 * stream + 3] if last else results[stream]
        )
        if resumed:
            for kept, start in zip((top, total, sums), given[stream][1:]):
                kept[...] = start[...]
        else:
            top[...] = jnp.full_like(top, MASKED)
            total[...] = jnp.zeros_like(total)
            sums[...] = jnp.zeros_like(sums)
        for chunk in range(chunks):
            pair = pairs[chunk]

            def work(
                key_at,
                query_at,
                key_block,
                query_block,
                masked,
                pair=pair,
                queries=queries,
                top=top,
                total=total,
                sums=sums,
            ):
                for head in range(heads):
                    scores = score_block(
                        info,
                        pair[0, head, :, key_at],
                        queries[head, :, query_at],
                        key_block,
                        query_block,
                        masked,
                    )
                    old = top[head, :, query_at]
                    new = jnp.maximum(old, jnp.max(scores, axis=0, keepdims=True) * factor)
                    decay = jnp.exp2(old - new)
                    weights = jnp.exp2(scores * factor - new)
                    top[head, :, query_at] = new
                    total[head, :, query_at] = total[head, :, query_at] * decay + jnp.sum(
                        weights, axis=0, keepdims=True
                    )
                    sums[head, :, query_at] = sums[head, :, query_at] * decay + contract(
                        pair[1, head, :, key_at], weights.astype(BF16), 1, 0
                    )

            for_blocks(info, stream, first_chunk + chunk, rows, work)
        if last:
            mixed, log_total = results[stream]
            for head in range(heads):
                mixed[head] = (sums[head] / total[head]).astype(BF16)
                log_total[head] = top[head] + jnp.log2(total[head])


def attend_back_kernel(first_chunk, chunks, resumed, info, *refs):
    per_stream = 5 if resumed else 4
    streams = (len(refs) - 2 * chunks - 2) // (per_stream + 1)
    given = [refs[per_stream * i : per_stream * (i + 1)] for i in range(streams)]
    refs = refs[per_stream * streams :]
    pairs, refs = refs[:chunks], refs[chunks:]
    query_sums, refs = refs[:streams], refs[streams:]
    grad_pairs, refs = refs[:chunks], refs[chunks:]
    inner, pair_sums = refs
    heads, head_size, tokens = given[0][0].shape
    rows = tokens // 2
    scale = head_size**-0.5
    factor = scale * LOG2E
    for stream in range(streams):
        _, grad_mixed, mixed = given[stream][:3]
        for head in range(heads):
            inner[stream, head] = jnp.sum(
                grad_mixed[head].astype(F32) * mixed[head].astype(F32), axis=0, keepdims=True
            )
        query_sums[stream][...] = (
            given[stream][4][...] if resumed else jnp.zeros_like(query_sums[stream])
        )
    for chunk in range(chunks):
        pair = pairs[chunk]
        pair_sums[...] = jnp.zeros_like(pair_sums)
        for stream in range(streams):
            queries, grad_mixed, _, log_total = given[stream][:4]

            def work(
                key_at,
                query_at,
                key_block,
                query_block,
                masked,
                pair=pair,
                stream=stream,
                queries=queries,
                grad_mixed=grad_mixed,
                log_total=log_total,
            ):
                for head in range(heads):
                    keys, values = pair[0, head, :, key_at], pair[1, head, :, key_at]
                    query_part = queries[head, :, query_at]
                    grad_part = grad_mixed[head, :, query_at]
                    scores = score_block(info, keys, query_part, key_block, query_block, masked)
                    probs = jnp.exp2(scores * factor - log_total[head, :, query_at])
                    grad_probs = contract(values, grad_part, 0, 0)
                    grad_scores = (
                        probs * (grad_probs - inner[stream, head, :, query_at])
                    ).astype(BF16)
                    pair_sums[1, head, :, key_at] += contract(grad_part, probs.astype(BF16), 1, 1)
                    pair_sums[0, head, :, key_at] += contract(query_part, grad_scores, 1, 1)
                    query_sums[stream][head, :, query_at] += contract(keys, grad_scores, 1, 0)

            for_blocks(info, stream, first_chunk + chunk, rows, work)
        grad_pairs[chunk][0] = (pair_sums[0] * scale).astype(grad_pairs[chunk].dtype)
        grad_pairs[chunk][1] = pair_sums[1].astype(grad_pairs[chunk].dtype)


SMALL_COST = pl.CostEstimate(flops=1 << 20, bytes_accessed=1 << 20, transcendentals=0)


def attend(info, queries, pairs, first_chunk, states, last):
    heads, head_size, tokens = queries[0].shape
    vmem = pl.BlockSpec(memory_space=pltpu.VMEM)
    state = [(heads, 1, tokens), (heads, 1, tokens), (heads, head_size, tokens)]
    operands = []
    for stream, member in enumerate(queries):
        operands.append(member)
        if states is not None:
            operands.extend(states[stream])
    operands.extend(pairs)
    if last:
        shapes = [
            jax.ShapeDtypeStruct((heads, head_size, tokens), BF16),
            jax.ShapeDtypeStruct((heads, 1, tokens), F32),
        ]
    else:
        shapes = [jax.ShapeDtypeStruct(shape, F32) for shape in state]
    results = pl.pallas_call(
        functools.partial(
            attend_kernel, first_chunk, len(pairs), len(queries), states is not None, last
        ),
        out_shape=tuple(shapes * len(queries)),
        in_specs=[pl.BlockSpec(memory_space=pltpu.SMEM)] + [vmem] * len(operands),
        out_specs=(vmem,) * (len(shapes) * len(queries)),
        scratch_shapes=[pltpu.VMEM(shape, F32) for shape in state] * len(queries) if last else [],
        compiler_params=pltpu.CompilerParams(vmem_limit_bytes=24 << 20),
        cost_estimate=SMALL_COST,
    )(info, *operands)
    return [results[len(shapes) * i : len(shapes) * (i + 1)] for i in range(len(queries))]


def attend_back(info, given, pairs, first_chunk, resumed, pair_type):
    heads, head_size, tokens = given[0][0].shape
    vmem = pl.BlockSpec(memory_space=pltpu.VMEM)
    operands = [member for stream in given for member in stream] + list(pairs)
    results = pl.pallas_call(
        functools.partial(attend_back_kernel, first_chunk, len(pairs), resumed),
        out_shape=tuple(
            jax.ShapeDtypeStruct((heads, head_size, tokens), F32) for _ in given
        )
        + tuple(jax.ShapeDtypeStruct(pair.shape, pair_type) for pair in pairs),
        in_specs=[pl.BlockSpec(memory_space=pltpu.SMEM)] + [vmem] * len(operands),
        out_specs=(vmem,) * (len(given) + len(pairs)),
        scratch_shapes=[
            pltpu.VMEM((len(given), heads, 1, tokens), F32),
            pltpu.VMEM((2, heads, head_size, tokens), F32),
        ],
        compiler_params=pltpu.CompilerParams(vmem_limit_bytes=32 << 20),
        cost_estimate=SMALL_COST,
    )(info, *operands)
    return results[: len(given)], results[len(given) :]


def near():
    tensor = lax.axis_index(TENSOR)
    return {TENSOR: tensor + 1 - 2 * lax.rem(tensor, 2)}


def far():
    tensor = lax.axis_index(TENSOR)
    return {TENSOR: tensor + 2 - 4 * lax.rem(tensor // 2, 2)}


def pair():
    seq = lax.axis_index(SEQ)
    return {SEQ: seq + 1 - 2 * lax.rem(seq, 2)}


def pair_far():
    seq = lax.axis_index(SEQ)
    return {SEQ: seq + 2 - 4 * lax.rem(seq // 2, 2)}


def across():
    return {CELL: 1 - lax.axis_index(CELL)}


class Wires:
    def __init__(self, r, partners):
        self.send, self.recv, self.local = r.send, r.recv, r.local
        self.started, self.open = 0, []
        barrier = pltpu.get_barrier_semaphore()
        for partner in partners:
            pl.semaphore_signal(barrier, inc=1, device_id=partner(), device_id_type=MESH)
        pl.semaphore_wait(barrier, len(partners))

    def start(self, source, target, partner):
        at = self.started
        copy = pltpu.make_async_remote_copy(
            src_ref=source,
            dst_ref=target,
            send_sem=self.send.at[at],
            recv_sem=self.recv.at[at],
            device_id=partner(),
            device_id_type=MESH,
        )
        copy.start()
        self.started += 1
        self.open.append(copy)
        return copy

    def sent(self, copy):
        copy.wait_send()
        self.open = [member for member in self.open if member is not copy]

    def finish(self):
        for copy in self.open:
            copy.wait_send()


class Local:
    def __init__(self, r, at, source, target):
        self.copy = pltpu.make_async_copy(source, target, r.local.at[at])
        self.copy.start()
        self.target, self.waited = target, False

    def get(self):
        if not self.waited:
            self.copy.wait()
            self.waited = True
        return self.target


def call_kernel(body, given, in_hbm, results, out_hbm, scratch, collective_id):
    scratch = dict(
        scratch,
        send=pltpu.SemaphoreType.DMA((COPIES,)),
        recv=pltpu.SemaphoreType.DMA((COPIES,)),
        local=pltpu.SemaphoreType.DMA((12,)),
    )
    vmem, hbm = pl.BlockSpec(memory_space=pltpu.VMEM), pl.BlockSpec(memory_space=pl.ANY)
    trees = (given, in_hbm, results, out_hbm, scratch)
    flat = [jax.tree.flatten(tree) for tree in trees]

    def kernel(*refs):
        found, at = {}, 0
        for leaves, tree in flat:
            found.update(jax.tree.unflatten(tree, refs[at : at + len(leaves)]))
            at += len(leaves)
        body(types.SimpleNamespace(**found))

    outs = pl.pallas_call(
        kernel,
        out_shape=tuple(flat[2][0] + flat[3][0]),
        in_specs=[vmem] * len(flat[0][0]) + [hbm] * len(flat[1][0]),
        out_specs=tuple([vmem] * len(flat[2][0]) + [hbm] * len(flat[3][0])),
        scratch_shapes=flat[4][0],
        compiler_params=pltpu.CompilerParams(
            collective_id=collective_id, has_side_effects=True, vmem_limit_bytes=62 << 20
        ),
        cost_estimate=SMALL_COST,
    )(*flat[0][0], *flat[1][0])
    count = len(flat[2][0])
    found = jax.tree.unflatten(flat[2][1], outs[:count])
    found.update(jax.tree.unflatten(flat[3][1], outs[count:]))
    return found


def shape_of(shape, dtype):
    return jax.ShapeDtypeStruct(shape, dtype)


def twice(value):
    return [value, value]


def by_rows(count, work, step=32):
    def one(index, carry):
        work(pl.ds(pl.multiple_of(index * step, step), step))
        return carry

    lax.fori_loop(0, count // step, one, 0)


def by_columns(width, work, step=128):
    def one(index, carry):
        work(pl.ds(pl.multiple_of(index * step, step), step))
        return carry

    lax.fori_loop(0, width // step, one, 0)
    if width % step:
        work(pl.ds(width // step * step, width % step))


def head_rows(source, rows):
    parts = [source[head, :, rows].astype(F32) for head in range(source.shape[0])]
    return jnp.concatenate(parts, axis=0).T


def put_heads(target, rows, values):
    head_size = target.shape[1]
    for head in range(target.shape[0]):
        target[head, :, rows] = values[head * head_size : (head + 1) * head_size].astype(
            target.dtype
        )


class Exchange:
    def __init__(self, wires, part, sent, got):
        self.wires, self.part, self.sent, self.got = wires, part, sent, got
        self.rows = part.shape[0]

    def give(self, values):
        self.sent[0] = values.astype(BF16)
        self.to_near = self.wires.start(self.sent.at[0], self.got.at[0], near)

    def keep(self, values):
        self.part[...] = values

    def join(self):
        self.to_near.wait_recv()

        def work(rows):
            self.sent[1, rows] = (self.part[rows] + self.got[0, rows].astype(F32)).astype(BF16)

        by_rows(self.rows, work)

    def cross(self):
        self.to_far = self.wires.start(self.sent.at[1], self.got.at[1], far)

    def wait(self):
        self.to_far.wait_recv()

    def total(self, rows):
        return self.sent[1, rows].astype(F32) + self.got[1, rows].astype(F32)


class Sum:
    def __init__(self, wires, whole, out, near_sum, got, got_far):
        self.wires, self.whole, self.out = wires, whole, out
        self.near_sum, self.got, self.got_far = near_sum, got, got_far
        self.bit = lax.rem(lax.axis_index(SEQ), 2)
        self.copy = None

    def wait(self):
        if self.copy is not None:
            self.copy.wait_recv()
            self.copy = None

    def add(self, target, left, right):
        def work(columns):
            target[:, columns] = (
                left[:, columns].astype(F32) + right[:, columns].astype(F32)
            ).astype(BF16)

        by_columns(target.shape[1], work)

    def one(self):
        self.copy = self.wires.start(self.whole.at[1 - self.bit], self.got, pair)

    def two(self):
        self.wait()
        self.add(self.near_sum, self.whole.at[self.bit], self.got)
        self.copy = self.wires.start(self.near_sum, self.got_far, pair_far)

    def three(self):
        self.wait()
        mine = self.out.at[self.bit]
        self.add(mine, self.near_sum, self.got_far)
        self.copy = self.wires.start(mine, mine, pair)

    def five(self, everything, rows):
        self.wait()
        target = everything.at[lax.axis_index(CELL), :, rows]
        self.copy = self.wires.start(self.out, target, across)
        return self.out, target


def sum_scratch(rows, width):
    return [pltpu.VMEM((rows, width), BF16)] * 3


def exchange_scratch(half, width, exchanges):
    return dict(
        part=pltpu.VMEM((2, half, width), F32),
        sent=pltpu.VMEM((2 * exchanges, 2, half, width), BF16),
        got=pltpu.VMEM((2 * exchanges, 2, half, width), BF16),
    )


def exchanges_of(r, wires, count):
    return [
        [Exchange(wires, r.part.at[i], r.sent.at[2 * k + i], r.got.at[2 * k + i]) for i in (0, 1)]
        for k in range(count)
    ]


def project(r, i, to_near, weight):
    half = r.wide_one[i].shape[0] // 2
    for part in (0, 1):
        at = pl.ds(part * half, half)
        if part and to_near is not None:
            to_near.wait_recv()
        wide = r.wide_one[i][at]
        for j in range(3):
            values = contract(wide, weight[j], 1, 1) + r.qkv_b[j : j + 1]
            target = r.queries[i] if j == 0 else r.pair[i].at[j - 1]
            put_heads(target, at, values.T)


def side_and_core():
    return lax.axis_index(SEQ) // 2, lax.rem(lax.axis_index(TENSOR), 2)


def core_columns(half, core):
    return pl.ds(pl.multiple_of(core * half, half), half)


def start_kernel(r):
    side, core = side_and_core()
    half = r.stream[0].shape[0]
    own = Local(r, 0, r.tokens.at[side], r.own_tokens)
    weight = Local(r, 1, r.qkv_w.at[0], r.own_qkv)
    wires = Wires(r, (near, pair, pair_far))
    arriving = wires.start(
        r.tokens.at[1 - side, :, core_columns(half, core)], r.got_tokens, pair_far
    )

    def norm(i, part, values):
        r.rows[...] = values.astype(F32).T

        def work(rows):
            stream = r.rows[rows]
            normed, inverse = normalize(stream)
            if part == 0:
                r.stream[i][rows] = stream
                r.normed_one[i][rows] = normed.astype(BF16)
                r.inverse_one[i][rows] = inverse
            to = pl.ds(part * half + rows.start, rows.size)
            r.wide_one[i][to] = (normed * r.gain[...] + r.shift[...]).astype(BF16)

        by_rows(half, work)

    tokens = own.get()
    for part in (0, 1):
        norm(0, part, tokens[:, core_columns(half, lax.rem(core + part, 2))])
    project(r, 0, None, weight.get())
    paired = wires.start(r.pair[0], r.got_pair, pair)
    arriving.wait_recv()
    norm(1, 0, r.got_tokens[...])
    wide = r.wide_one[1]
    to_near = wires.start(wide.at[pl.ds(0, half)], wide.at[pl.ds(half, half)], near)
    project(r, 1, to_near, weight.get())
    paired.wait_recv()
    wires.finish()


def next_shapes(half, width, head_shape):
    return dict(
        stream=twice(shape_of((half, width), F32)),
        wide_one=twice(shape_of((2 * half, width), BF16)),
        normed_one=twice(shape_of((half, width), BF16)),
        inverse_one=twice(shape_of((half, 1), F32)),
        queries=twice(shape_of(head_shape, BF16)),
        pair=twice(shape_of((2,) + head_shape, BF16)),
        got_pair=shape_of((2,) + head_shape, BF16),
    )


def start_call(tokens, qkv_w, qkv_b, gain, shift, head_shape, collective_id):
    _, width, row_count = tokens.shape
    half = row_count // 2
    return call_kernel(
        start_kernel,
        dict(qkv_b=qkv_b, gain=gain, shift=shift),
        dict(tokens=tokens, qkv_w=qkv_w),
        next_shapes(half, width, head_shape),
        {},
        dict(
            own_tokens=pltpu.VMEM((width, row_count), BF16),
            got_tokens=pltpu.VMEM((width, half), BF16),
            own_qkv=pltpu.VMEM(qkv_w.shape[1:], BF16),
            rows=pltpu.VMEM((half, width), F32),
        ),
        collective_id,
    )


def forward_kernel(layer, last, r):
    side, core = side_and_core()
    half = r.base[0].shape[0]
    halves = (pl.ds(0, half), pl.ds(half, half))
    out_w = Local(r, 0, r.out_w.at[layer], r.own_out)
    up_w = Local(r, 1, r.up_w.at[layer], r.own_up)
    down_w = Local(r, 2, r.down_w.at[layer], r.own_down)
    if not last:
        qkv_w = Local(r, 3, r.qkv_w.at[layer + 1], r.own_qkv)
    wires = Wires(r, (near, far) + (() if last else (pair, pair_far)))
    first, second = exchanges_of(r, wires, 2)
    to_near = {}

    def row(index):
        return r.vectors[index : index + 1]

    def norm(i, exchange, base, at, kept, normed_to, inverse_to, wide):
        def work(rows):
            stream = base[rows] + exchange.total(rows) + row(at)
            normed, inverse = normalize(stream)
            kept[rows] = stream
            normed_to[rows] = normed.astype(BF16)
            inverse_to[rows] = inverse
            wide[rows] = (normed * row(at + 1) + row(at + 2)).astype(BF16)

        by_rows(half, work)
        to_near[i] = wires.start(wide.at[halves[0]], wide.at[halves[1]], near)

    def attended(i):
        for part in (1, 0):
            values = mm(head_rows(r.mixed[i], halves[part]).astype(BF16), out_w.get()[...])
            (first[i].give if part else first[i].keep)(values)

    def mid_norm(i):
        norm(
            i, first[i], r.base[i], 0, r.mid.at[i], r.normed_two[i], r.inverse_two[i], r.wide_two[i]
        )

    def feed(i):
        for part in (0, 1):
            if part:
                to_near[i].wait_recv()
            r.wide_part[...] = mm(r.wide_two[i][halves[part]], up_w.get()[...])

            def work(rows, part=part):
                hidden, slope = gelu_both(r.wide_part[rows] + r.up_b[...])
                to = pl.ds(part * half + rows.start, rows.size)
                r.hidden[i][to] = hidden
                r.slope[i][to] = slope

            by_rows(half, work)
        for part in (1, 0):
            values = mm(r.hidden[i][halves[part]], down_w.get()[...])
            (second[i].give if part else second[i].keep)(values)

    def leave(i):
        if last:

            def work(rows):
                r.part[i, rows] = r.mid[i, rows] + second[i].total(rows) + row(3)

            by_rows(half, work)
            r.low[i][...] = r.part[i].T.astype(BF16)
        else:
            norm(
                i, second[i], r.mid.at[i], 3, r.stream[i], r.normed_one[i], r.inverse_one[i],
                r.wide_one[i],
            )
            project(r, i, to_near[i], qkv_w.get())

    for i in (0, 1):
        attended(i)
    first[0].join()
    first[0].cross()
    first[1].join()
    first[0].wait()
    first[1].cross()
    if not last:
        given = wires.start(
            r.out_grad.at[1 - side, :, core_columns(half, core)], r.got_grad, pair_far
        )
    mid_norm(0)
    feed(0)
    second[0].join()
    first[1].wait()
    second[0].cross()
    mid_norm(1)
    feed(1)
    second[1].join()
    second[0].wait()
    second[1].cross()
    leave(0)
    if not last:
        paired = wires.start(r.pair[0], r.got_pair, pair)
    second[1].wait()
    leave(1)
    if not last:
        given.wait_recv()
        paired.wait_recv()
    wires.finish()


def forward_call(given, in_hbm, layer, last, collective_id):
    half, width = given["base"][0].shape
    hidden_width = in_hbm["up_w"].shape[2]
    head_shape = given["mixed"][0].shape
    wide_hidden = shape_of((2 * half, hidden_width), BF16)
    results = dict(
        wide_two=twice(shape_of((2 * half, width), BF16)),
        normed_two=twice(shape_of((half, width), BF16)),
        inverse_two=twice(shape_of((half, 1), F32)),
        hidden=twice(wide_hidden),
        slope=twice(wide_hidden),
    )
    out_hbm = {}
    scratch = dict(
        exchange_scratch(half, width, 2),
        mid=pltpu.VMEM((2, half, width), F32),
        wide_part=pltpu.VMEM((half, hidden_width), F32),
        own_out=pltpu.VMEM(in_hbm["out_w"].shape[1:], BF16),
        own_up=pltpu.VMEM(in_hbm["up_w"].shape[1:], BF16),
        own_down=pltpu.VMEM(in_hbm["down_w"].shape[1:], BF16),
    )
    if last:
        results.update(low=twice(shape_of((width, half), BF16)))
    else:
        results.update(next_shapes(half, width, head_shape))
        out_hbm.update(got_grad=shape_of((width, half), BF16))
        scratch.update(own_qkv=pltpu.VMEM(in_hbm["qkv_w"].shape[1:], BF16))
    return call_kernel(
        functools.partial(forward_kernel, layer, last),
        given,
        in_hbm,
        results,
        out_hbm,
        scratch,
        collective_id,
    )


def backward_kernel(attention, feed, riding, r):
    begin, end = attention is None, feed is None
    side, core = side_and_core()
    half = r.grad_out[0].shape[0]
    halves = (pl.ds(0, half), pl.ds(half, half))
    if begin:
        own = Local(r, 0, r.out_grad.at[side], r.own_grad)
    else:
        qkv_w = Local(r, 1, r.qkv_w.at[attention], r.own_qkv)
    if not end:
        down_w = Local(r, 2, r.down_w.at[feed], r.own_down)
        up_w = Local(r, 3, r.up_w.at[feed], r.own_up)
        out_w = Local(r, 4, r.out_w.at[feed], r.own_out)
    partners = [near, far]
    if begin or riding:
        partners.append(pair_far)
    if riding:
        partners.append(pair)
    wires = Wires(r, partners)
    exchanges = exchanges_of(r, wires, int(not begin) + int(not end))
    to_near = {}
    r.sums[...] = jnp.zeros_like(r.sums)
    if riding:
        rider = Sum(wires, r.whole, r.summed if riding == 2 else None, r.near_sum, r.got_sum, r.got_far)

    def note(index, values):
        r.sums[index : index + 1, : values.shape[1]] += jnp.sum(values, axis=0, keepdims=True)

    def gather(i, exchange):
        scale = HEAD**-0.5
        for part in (1, 0):
            at = halves[part]
            values = None
            for j in range(3):
                target = r.grads[i].at[j]
                for head in range(target.shape[0]):
                    if j == 0:
                        found = r.query_sum[i][head, :, at] * scale
                    else:
                        found = r.pair_sum[i][j - 1, head, :, at] + r.pair_got[i][
                            j - 1, head, :, at
                        ].astype(F32)
                    target[head, :, at] = found.astype(BF16)
                rows = head_rows(target, at)
                if j != 1:
                    index = 7 + j // 2
                    r.sums[index : index + 1, : rows.shape[1]] += jnp.sum(
                        rows, axis=0, keepdims=True
                    )
                product = mm(rows.astype(BF16), qkv_w.get()[j])
                values = product if values is None else values + product
            (exchange.give if part else exchange.keep)(values)

    def norm(i, exchange, base, normed_of, inverse_of, gain, at, wide):
        def work(rows):
            incoming = exchange.total(rows)
            normed = normed_of[rows].astype(F32)
            grad = base[rows] + norm_back(
                incoming, normed, inverse_of[rows], r.gains[gain : gain + 1]
            )
            r.grad_out[i][rows] = grad
            note(at, incoming * normed)
            note(at + 1, incoming)
            note(at + 2, grad)
            if wide is not None:
                wide[rows] = grad.astype(BF16)

        by_rows(half, work)
        if wide is not None:
            to_near[i] = wires.start(wide.at[halves[0]], wide.at[halves[1]], near)

    def first_norm(i):
        norm(
            i, exchanges[0][i], r.grad[i], r.normed_one[i], r.inverse_one[i], 0, 0,
            None if end else r.wide[i],
        )
        if end:
            r.low[i][...] = r.grad_out[i][...].T.astype(BF16)

    def second_norm(i):
        norm(
            i, exchanges[-1][i], r.grad_out[i], r.normed_two[i], r.inverse_two[i], 1, 3,
            r.wide_mid[i],
        )
        for part in (0, 1):
            if part:
                to_near[i].wait_recv()
            values = contract(out_w.get()[...], r.wide_mid[i][halves[part]], 1, 1)
            put_heads(r.mixed_grad[i], halves[part], values)

    def first_rows(i):
        if i == 0:
            given = own.get()
            for part in (0, 1):
                values = given[:, core_columns(half, lax.rem(core + part, 2))].astype(F32).T
                if part == 0:
                    r.grad_out[0][...] = values
                r.wide[0][halves[part]] = values.astype(BF16)
        else:
            r.grad_out[1][...] = r.got_grad[...].astype(F32).T
            wide = r.wide[1]
            wide[halves[0]] = r.grad_out[1][...].astype(BF16)
            to_near[1] = wires.start(wide.at[halves[0]], wide.at[halves[1]], near)
        by_rows(half, lambda rows: note(2, r.grad_out[i][rows]))

    def slide(i, exchange):
        wide = r.wide[i]
        for part in (0, 1):
            if part and i in to_near:
                to_near[i].wait_recv()
            r.wide_part[...] = contract(wide[halves[part]], down_w.get()[...], 1, 1)

            def work(rows, part=part):
                to = pl.ds(part * half + rows.start, rows.size)
                hidden = r.wide_part[rows].astype(BF16).astype(F32)
                pre = (hidden * r.slope[i][to].astype(F32)).astype(BF16)
                r.pre[i][to] = pre
                note(6, pre.astype(F32))

            by_rows(half, work)
        for part in (1, 0):
            values = contract(r.pre[i][halves[part]], up_w.get()[...], 1, 1)
            (exchange.give if part else exchange.keep)(values)

    def ride(step):
        if riding and step == 0:
            rider.one()
        elif riding and step == 1:
            rider.two()
        elif riding and step == 5:
            rider.wait()
        elif riding == 2 and step == 3:
            rider.three()

    ride(0)
    if begin:
        (after,) = exchanges
        placed = place_cells(r, wires, r.block, r.block_low)
        for i in (0, 1):
            first_rows(i)
            slide(i, after[i])
            after[i].join()
            if i == 1:
                after[0].wait()
            after[i].cross()
        second_norm(0)
        placed.forward()
        after[1].wait()
        second_norm(1)
        placed.finish()
    else:
        before, after = exchanges[0], exchanges[-1]
        a, b = (1, 0) if end else (0, 1)
        gather(a, before[a])
        gather(b, before[b])
        before[a].join()
        before[a].cross()
        before[b].join()
        before[a].wait()
        before[b].cross()
        ride(1)
        first_norm(a)
        if end:
            before[b].wait()
            first_norm(b)
        else:
            slide(a, after[a])
            after[a].join()
            before[b].wait()
            after[a].cross()
            first_norm(b)
            slide(b, after[b])
            after[b].join()
            after[a].wait()
            after[b].cross()
            ride(3)
            second_norm(a)
            after[b].wait()
            second_norm(b)
    ride(5)
    wires.finish()


class place_cells:
    def __init__(self, r, wires, target, low):
        side, core = side_and_core()
        half = low[0].shape[1]
        self.wires = wires
        columns = core_columns(half, core)
        self.own = target.at[side, :, columns]
        self.arrived = target.at[1 - side, :, columns]
        self.local = Local(r, 11, low[0], self.own)
        self.to_far = wires.start(low[1], self.own, pair_far)
        self.to_near = wires.start(low[0], self.own, near)

    def forward(self):
        self.to_far.wait_recv()
        self.second = self.wires.start(self.arrived, self.arrived, near)

    def finish(self):
        self.local.get()
        self.to_near.wait_recv()
        self.second.wait_recv()


def backward_call(given, in_hbm, attention, feed, riding, collective_id):
    begin, end = attention is None, feed is None
    some = given["block_low"][0] if begin else given["grad"][0]
    width = given["gains"].shape[1]
    half = some.shape[1] if begin else some.shape[0]
    results = dict(sums=shape_of((16, width), F32), grad_out=twice(shape_of((half, width), F32)))
    wide = twice(shape_of((2 * half, width), BF16))
    out_hbm = {}
    scratch = exchange_scratch(half, width, int(not begin) + int(not end))
    if begin:
        out_hbm.update(block=shape_of((2, width, 2 * half), BF16))
        scratch.update(own_grad=pltpu.VMEM((width, 2 * half), BF16))
    else:
        head_shape = given["query_sum"][0].shape
        results.update(grads=twice(shape_of((3,) + head_shape, BF16)))
        scratch.update(own_qkv=pltpu.VMEM(in_hbm["qkv_w"].shape[1:], BF16))
    if end:
        results.update(low=twice(shape_of((width, half), BF16)))
    else:
        hidden_width = in_hbm["up_w"].shape[2]
        head_count = in_hbm["out_w"].shape[1] // HEAD
        results.update(
            wide=wide,
            wide_mid=wide,
            pre=twice(shape_of((2 * half, hidden_width), BF16)),
            mixed_grad=twice(shape_of((head_count, HEAD, 2 * half), BF16)),
        )
        scratch.update(
            wide_part=pltpu.VMEM((half, hidden_width), F32),
            own_out=pltpu.VMEM(in_hbm["out_w"].shape[1:], BF16),
            own_up=pltpu.VMEM(in_hbm["up_w"].shape[1:], BF16),
            own_down=pltpu.VMEM(in_hbm["down_w"].shape[1:], BF16),
        )
    if riding:
        whole = given["whole"]
        one = pltpu.VMEM(whole.shape[1:], BF16)
        if riding == 2:
            results.update(summed=shape_of(whole.shape, BF16))
            scratch.update(near_sum=one, got_far=one)
        else:
            part = shape_of(whole.shape[1:], BF16)
            results.update(near_sum=part, got_far=part)
        scratch.update(got_sum=one)
    return call_kernel(
        functools.partial(backward_kernel, attention, feed, riding),
        given,
        in_hbm,
        results,
        out_hbm,
        scratch,
        collective_id,
    )


def closing_kernel(sums_too, r):
    wires = Wires(r, [near, pair, pair_far] + ([across] if sums_too else []))
    cell = lax.axis_index(CELL)
    kernels = r.vectors.shape[0]
    r.total[...] = r.vectors[...]

    def vectors(at, partner, own_rows=16):
        copy = wires.start(r.total, r.around.at[at], partner)

        def add():
            copy.wait_recv()
            wires.sent(copy)
            for kernel in range(kernels):
                r.total[kernel, :own_rows] += r.around[at, kernel, :own_rows]

        return add

    if sums_too:
        span = r.sum_feed[0].shape[1]
        spans = [pl.ds(0, span), pl.ds(span, r.all_feed.shape[2] - span)]
        whole = pl.ds(0, r.all_last.shape[2])
        arriving = wires.start(r.sent_last, r.got_last, across)
        feed = [
            Sum(wires, r.whole_feed[k], r.sum_feed[k], *r.riding_feed[k]) for k in (0, 1)
        ]
        last = Sum(wires, r.whole_last, r.sum_last, *r.riding_last)
        late = Sum(wires, r.whole_late, r.sum_late, *r.riding_late)
        prior = Sum(wires, None, r.sum_prior, r.near_prior, None, r.far_prior)
        local = []

        def fold(target, kept, got, rows):
            def work(columns):
                target[:, :, columns] = (
                    kept[:, rows, columns].astype(F32) + got[:, rows, columns].astype(F32)
                ).astype(BF16)

            by_columns(kept.shape[2], work)

        def five(member, everything, rows):
            own, target = member.five(everything, rows)
            local.append(Local(r, len(local), own, target))

        fold(r.whole_feed[0], r.kept_feed, r.got_feed, spans[0])
        feed[0].one()
        prior.three()
        late.one()
        placed = place_cells(r, wires, r.tokens_grad, r.low)
        add = vectors(0, near, 6)
        local.append(Local(r, 0, r.early, r.all_late.at[cell, :, spans[0]]))
        local.append(Local(r, 1, r.got_early, r.all_late.at[1 - cell, :, spans[0]]))
        fold(r.whole_feed[1], r.kept_feed, r.got_feed, spans[1])
        feed[0].two()
        feed[1].one()
        add()
        add = vectors(1, across)
        late.two()
        five(prior, r.all_prior, whole)
        arriving.wait_recv()
        fold(r.whole_last, r.kept_last, r.got_last, whole)
        last.one()
        add()
        add = vectors(2, pair)
        feed[1].two()
        feed[0].three()
        placed.forward()
        add()
        add = vectors(3, pair_far)
        last.two()
        late.three()
        feed[1].three()
        add()
        five(feed[0], r.all_feed, spans[0])
        five(late, r.all_late, spans[1])
        last.three()
        five(feed[1], r.all_feed, spans[1])
        five(last, r.all_last, whole)
        for member in feed + [late, prior, last]:
            member.wait()
        for copy in local:
            copy.get()
    else:
        placed = place_cells(r, wires, r.tokens_grad, r.low)
        vectors(0, near, 6)()
        placed.forward()
        vectors(1, pair)()
        vectors(2, pair_far)()
    r.totals[...] = r.total[...]
    placed.finish()
    wires.finish()


def closing_call(given, in_hbm, sums_too, collective_id):
    width, half = given["low"][0].shape
    vectors = given["vectors"].shape
    results = dict(totals=shape_of(vectors, F32))
    out_hbm = dict(tokens_grad=shape_of((2, width, 2 * half), BF16))
    scratch = dict(total=pltpu.VMEM(vectors, F32), around=pltpu.VMEM((4,) + vectors, F32))
    if sums_too:
        feed, last = given["kept_feed"].shape, given["kept_last"].shape
        late = given["whole_late"].shape
        early = (feed[0], feed[1] - late[1]) + feed[2:]
        spans = [pltpu.VMEM(early, BF16), pltpu.VMEM(late, BF16)]
        out_hbm.update(
            all_feed=shape_of((2,) + feed, BF16),
            all_late=shape_of((2,) + feed, BF16),
            all_last=shape_of((2,) + last, BF16),
            all_prior=shape_of((2,) + last, BF16),
        )
        scratch.update(
            whole_feed=spans,
            sum_feed=spans,
            riding_feed=[sum_scratch(*early[1:]), sum_scratch(*late[1:])],
            sum_late=spans[1],
            riding_late=sum_scratch(*late[1:]),
            whole_last=pltpu.VMEM(last, BF16),
            sum_last=pltpu.VMEM(last, BF16),
            got_last=pltpu.VMEM(last, BF16),
            riding_last=sum_scratch(*last[1:]),
            sum_prior=pltpu.VMEM(last, BF16),
        )
    return call_kernel(
        functools.partial(closing_kernel, sums_too),
        given,
        in_hbm,
        results,
        out_hbm,
        scratch,
        collective_id,
    )


class Line:
    def __init__(self):
        self.last = None

    def run(self, step, *operands):
        if self.last is not None:
            operands, _ = lax.optimization_barrier((operands, self.last))
        results = step(*operands)
        self.last = jax.tree.leaves(results)[0]
        return types.SimpleNamespace(**results) if isinstance(results, dict) else results


def add_low(kept, got):
    return (kept.astype(F32) + got.astype(F32)).astype(BF16)


def pick(cell, low, high):
    first, second = jnp.stack(low), jnp.stack(high)
    return jnp.where(cell == 0, first, second), jnp.where(cell == 0, second, first)


def two_sum(product, left, right):
    return (product(left[0], right[0]) + product(left[1], right[1])).astype(BF16)


def feed_sums(hidden, grad_down, wide_two, pre_grad):
    up, down = two_sum(mm_left, wide_two, pre_grad), two_sum(mm_left, hidden, grad_down)
    return [part for whole in (up, down) for part in jnp.split(whole, 2, axis=0)]


def attention_sums(wide_mid, mixed, wide_one, grads):
    def product(left, right):
        return mm(left.reshape(left.shape[0] * left.shape[1], left.shape[2]), right)

    return [two_sum(product, [grad[j] for grad in grads], wide_one) for j in range(3)] + [
        two_sum(product, mixed, wide_mid)
    ]


def shards(
    tokens,
    out_grad,
    group_order,
    lengths,
    qkv_weight,
    qv_bias,
    out_weight,
    out_bias,
    up_weight,
    up_bias,
    down_weight,
    down_bias,
    norm_gain,
    norm_shift,
):
    layer_count = qkv_weight.shape[0]
    local_width = qkv_weight.shape[3]
    seq_index = lax.axis_index(SEQ)
    cell = lax.axis_index(CELL)
    core = lax.axis_index(TENSOR) % 2
    side = seq_index // 2
    paired_cells = lax.axis_size(CELL) == 2
    gains, shifts = norm_gain.astype(F32), norm_shift.astype(F32)
    row_count = tokens.shape[1]
    head_shape = (local_width // HEAD, HEAD, row_count)
    tokens, out_grad = jnp.swapaxes(tokens, 1, 2), jnp.swapaxes(out_grad, 1, 2)
    qkv_weight = jnp.swapaxes(qkv_weight, 2, 3)
    biases = qv_bias.astype(F32)
    qkv_bias = jnp.stack([biases[:, 0], jnp.zeros_like(biases[:, 0]), biases[:, 1]], axis=1)
    line = Line()

    order = jnp.where(side == 0, group_order[0], group_order[1])
    length = jnp.where(side == 0, lengths[0], lengths[1])
    offsets = jnp.array([0, 2, 0, 2, 1, 3], jnp.int32)
    slots = 2 * (seq_index ^ offsets)[:, None] + (core + jnp.arange(2)[None]) % 2
    wanted = slots.reshape(-1, 1) == jnp.arange(order.shape[0])[None]
    blocks = jnp.sum(jnp.where(wanted, order[None], 0), axis=1)
    info = jnp.concatenate([length[None], blocks]).astype(jnp.int32)

    weights = dict(out_w=out_weight, up_w=up_weight, down_w=down_weight)
    now = line.run(
        lambda *given: start_call(*given, head_shape, 0),
        tokens,
        qkv_weight,
        qkv_bias[0],
        gains[0, :1],
        shifts[0, :1],
    )
    saved = []
    for layer in range(layer_count):
        last = layer == layer_count - 1
        got_pair = swap(now.pair[1], SEQ, 1)
        states = line.run(
            lambda queries, *pairs: attend(info, queries, pairs, 0, None, False),
            now.queries,
            *now.pair,
            now.got_pair,
        )
        mixed = line.run(
            lambda queries, states, pair: attend(info, queries, [pair], 3, states, True),
            now.queries,
            states,
            got_pair,
        )
        rows = [out_bias[layer], gains[layer, 1], shifts[layer, 1], down_bias[layer]]
        given = dict(
            base=now.stream,
            mixed=[mixed[0][0], mixed[1][0]],
            up_b=up_bias[layer].astype(F32)[None],
        )
        in_hbm = dict(weights)
        if not last:
            rows += [gains[layer + 1, 0], shifts[layer + 1, 0]]
            in_hbm.update(qkv_w=qkv_weight, out_grad=out_grad)
            given.update(qkv_b=qkv_bias[layer + 1])
        given.update(vectors=jnp.stack([row.astype(F32) for row in rows]))
        found = line.run(
            lambda given, in_hbm, layer=layer, last=last: forward_call(
                given, in_hbm, layer, last, 1 + layer
            ),
            given,
            in_hbm,
        )
        saved.append(
            types.SimpleNamespace(
                queries=now.queries,
                near_pairs=now.pair,
                far_pairs=[now.got_pair, got_pair],
                wide_one=now.wide_one,
                normed_one=now.normed_one,
                inverse_one=now.inverse_one,
                mixed=[mixed[0][0], mixed[1][0]],
                log_total=[mixed[0][1], mixed[1][1]],
                wide_two=found.wide_two,
                normed_two=found.normed_two,
                inverse_two=found.inverse_two,
                hidden=found.hidden,
                slope=found.slope,
            )
        )
        if not last:
            got_grad = found.got_grad
            now = found

    identity = layer_count + 1
    block_low = found.low
    vectors = []
    halves = {}
    for layer in reversed(range(layer_count + 1)):
        begin, end = layer == layer_count, layer == 0
        given, in_hbm = dict(), dict()
        gain_rows = [gains[0, 0], gains[0, 0]]
        riding = 0
        if begin:
            given.update(got_grad=got_grad, block_low=block_low)
            in_hbm.update(out_grad=out_grad)
        else:
            above = saved[layer]
            given.update(
                grad=found.grad_out,
                query_sum=query_sums,
                pair_sum=near_sums,
                pair_got=far_got,
                normed_one=above.normed_one,
                inverse_one=above.inverse_one,
            )
            in_hbm.update(qkv_w=qkv_weight)
            gain_rows[0] = gains[layer, 0]
            if paired_cells:
                given.update(whole=line.run(add_low, *pending))
                riding = 1 if end else 2
        if not end:
            below = saved[layer - 1]
            given.update(
                slope=below.slope, normed_two=below.normed_two, inverse_two=below.inverse_two
            )
            in_hbm.update(weights)
            gain_rows[1] = gains[layer - 1, 1]
        given.update(gains=jnp.stack(gain_rows))
        found = line.run(
            lambda given, in_hbm, layer=layer, riding=riding: backward_call(
                given,
                in_hbm,
                layer if layer < layer_count else None,
                layer - 1 if layer > 0 else None,
                riding,
                identity + layer,
            ),
            given,
            in_hbm,
        )
        vectors.append(found.sums)
        if begin:
            block_out = found.block
        else:
            if riding == 2:
                early = found.summed
                got_early = swap(early, CELL, 1)
                late = line.run(add_low, *late)
            sums = line.run(attention_sums, wide_mid, above.mixed, above.wide_one, found.grads)
            if paired_cells:
                kept, sent = line.run(functools.partial(pick, cell), sums[:2], sums[2:])
                if not end:
                    pending = [kept, swap(sent, CELL, 1)]
            else:
                halves[layer, 1] = sums
        if end:
            break
        wide_mid = found.wide_mid
        sums = line.run(feed_sums, below.hidden, found.wide, below.wide_two, found.pre)
        if paired_cells:
            kept_feed, sent_feed = line.run(functools.partial(pick, cell), sums[:2], sums[2:])
            if begin:
                cut = kept_feed.shape[1] // 32 * 16 + 16
                pending = [kept_feed[:, :cut], swap(sent_feed[:, :cut], CELL, 1)]
                late = [kept_feed[:, cut:], swap(sent_feed[:, cut:], CELL, 1)]
            else:
                got_feed = swap(sent_feed, CELL, 1)
        else:
            halves[layer - 1, 0] = sums
        streams = [
            list(members)
            for members in zip(below.queries, found.mixed_grad, below.mixed, below.log_total)
        ]
        query_sums, far_sums = line.run(
            lambda given, pairs: attend_back(info, given, pairs, 2, False, BF16),
            streams,
            below.far_pairs,
        )
        far_got = [swap(far_sum, SEQ, 1) for far_sum in far_sums]
        streams = [members + [start] for members, start in zip(streams, query_sums)]
        query_sums, near_sums = line.run(
            lambda given, pairs: attend_back(info, given, pairs, 0, True, F32),
            streams,
            below.near_pairs,
        )

    vectors = jnp.stack(vectors)
    if not paired_cells:
        vectors = lax.psum(vectors, CELL)
    given, in_hbm = dict(low=found.low, vectors=vectors), dict()
    if paired_cells:
        given.update(
            kept_feed=kept_feed,
            got_feed=got_feed,
            kept_last=kept,
            sent_last=sent,
            whole_late=late,
            near_prior=found.near_sum,
            far_prior=found.got_far,
        )
        in_hbm.update(early=early, got_early=got_early)
    closing = line.run(
        lambda given, in_hbm: closing_call(given, in_hbm, paired_cells, identity + layer_count + 1),
        given,
        in_hbm,
    )
    if paired_cells:
        feeds = [closing.all_feed, closing.all_late]
        attentions = [closing.all_last, closing.all_prior]
    else:

        def whole(part):
            found = []
            for layer in range(layer_count):
                total = lax.psum(jnp.stack(halves[layer, part]).astype(F32), (CELL, SEQ))
                found.append(total.reshape((2, 2) + total.shape[1:]))
            return found

        feeds, attentions = whole(0), whole(1)

    def final(pieces):
        return jnp.stack([piece.astype(F32) for piece in pieces])

    def square(member):
        return member.reshape(member.shape[0] * member.shape[1], member.shape[2])

    totals = closing.totals
    attention_rows = [totals[layer_count - layer] for layer in range(layer_count)]
    feed_rows = [totals[layer_count - 1 - layer] for layer in range(layer_count)]

    def rows_of(members, *indices):
        return jnp.stack([member[index] for member in members for index in indices])

    gain_grad = jnp.stack([rows_of(attention_rows, 0), rows_of(feed_rows, 3)], axis=1)
    shift_grad = jnp.stack([rows_of(attention_rows, 1), rows_of(feed_rows, 4)], axis=1)
    qv_grad = rows_of(attention_rows, 7, 8)[:, :local_width]
    return (
        jnp.swapaxes(block_out, 1, 2),
        jnp.swapaxes(closing.tokens_grad, 1, 2),
        jnp.swapaxes(
            final([jnp.stack([*member[0], member[1, 0]]) for member in attentions]), 2, 3
        ),
        qv_grad.reshape(layer_count, 2, local_width),
        final([member[1, 1] for member in attentions]),
        rows_of(feed_rows, 5),
        final([square(member[0]) for member in feeds]),
        rows_of(feed_rows, 6),
        final([square(member[1]) for member in feeds]),
        rows_of(feed_rows, 2),
        gain_grad,
        shift_grad,
    )


def solution(mesh):
    shared, by_tensor = P(), P(None, TENSOR)
    rows, last = P(CELL, SEQ, None), P(None, None, TENSOR)
    middle = P(None, TENSOR, None)
    weights = (P(None, None, None, TENSOR), last, middle, shared, last, by_tensor, middle)
    norms = (shared, shared, shared)
    return jax.shard_map(
        shards,
        mesh=mesh,
        in_specs=(rows, rows, P(CELL, None), P(CELL)) + weights + norms,
        out_specs=(rows, rows) + weights + norms,
        check_vma=False,
    )
```

```python
import functools
import types

import jax
import jax.numpy as jnp
from jax import lax
from jax.experimental import pallas as pl
from jax.experimental.pallas import tpu as pltpu
from jax.sharding import PartitionSpec as P

HEAD = 56
EPSILON = 1e-05
MASKED = -1e30
ROOT_TWO_PI = 0.7978845608028654
CUBIC = 0.044715
LOG2E = 1.4426950408889634
F32 = jnp.float32
BF16 = jnp.bfloat16
MESH = pl.DeviceIdType.MESH
CELL, SEQ, TENSOR = "cell", "seq", "tensor"
COPIES = 28


def swap(values, axis, bit):
    size = lax.axis_size(axis)
    return lax.ppermute(values, axis, [(i, i ^ bit) for i in range(size)])


def normalize(values):
    centred = values - jnp.mean(values, axis=-1, keepdims=True)
    spread = jnp.mean(centred * centred, axis=-1, keepdims=True)
    inverse = lax.rsqrt(spread + EPSILON)
    return (centred * inverse, inverse)


def norm_back(incoming, normed, inverse, gain_row):
    scaled = incoming * gain_row
    first_mean = jnp.mean(scaled, axis=-1, keepdims=True)
    second_mean = jnp.mean(scaled * normed, axis=-1, keepdims=True)
    return inverse * (scaled - first_mean - normed * second_mean)


def gelu_both(values):
    inner = jnp.tanh(ROOT_TWO_PI * (values + CUBIC * values * values * values))
    hidden = 0.5 * values * (1.0 + inner)
    slope = 0.5 * (1.0 + inner) + 0.5 * values * (1.0 - inner * inner) * ROOT_TWO_PI * (
        1.0 + 3.0 * CUBIC * values * values
    )
    return hidden.astype(BF16), slope.astype(BF16)


def contract(left, right, left_dim, right_dim):
    return lax.dot_general(
        left, right, (((left_dim,), (right_dim,)), ((), ())), preferred_element_type=F32
    )


def mm(left, right):
    return contract(left, right, 1, 0)


def mm_left(left, right):
    return contract(left, right, 0, 0)


def score_block(info, keys, queries, key_block, query_block, masked):
    scores = contract(keys, queries, 0, 0)
    if masked:
        rows = scores.shape[0]
        key_place = key_block * rows + lax.broadcasted_iota(jnp.int32, scores.shape, 0)
        query_place = query_block * rows + lax.broadcasted_iota(jnp.int32, scores.shape, 1)
        allowed = (key_place <= query_place) & (key_place < info[0])
        scores = jnp.where(allowed, scores, MASKED)
    return scores


def for_blocks(info, stream, chunk, block_rows, work):
    def one(step, carry):
        key_half, query_half = step // 2, step % 2
        key_block, query_block = info[5 + 2 * chunk + key_half], info[1 + 2 * stream + query_half]
        key_at = pl.ds(pl.multiple_of(key_half * block_rows, block_rows), block_rows)
        query_at = pl.ds(pl.multiple_of(query_half * block_rows, block_rows), block_rows)
        first = key_block * block_rows
        counts = (key_block <= query_block) & (first < info[0])
        partial = (key_block == query_block) | (first + block_rows > info[0])

        @pl.when(counts & partial)
        def _():
            work(key_at, query_at, key_block, query_block, True)

        @pl.when(counts & jnp.logical_not(partial))
        def _():
            work(key_at, query_at, key_block, query_block, False)

        return carry

    lax.fori_loop(0, 4, one, 0)


def attend_kernel(first_chunk, chunks, streams, resumed, last, info, *refs):
    per_stream = 4 if resumed else 1
    given = [refs[per_stream * i : per_stream * (i + 1)] for i in range(streams)]
    refs = refs[per_stream * streams :]
    pairs, refs = refs[:chunks], refs[chunks:]
    per_output = 2 if last else 3
    results = [refs[per_output * i : per_output * (i + 1)] for i in range(streams)]
    scratch = refs[per_output * streams :]
    heads, head_size, tokens = given[0][0].shape
    rows = tokens // 2
    factor = head_size**-0.5 * LOG2E
    for stream in range(streams):
        queries = given[stream][0]
        top, total, sums = (
            scratch[3 * stream : 3 * stream + 3] if last else results[stream]
        )
        if resumed:
            for kept, start in zip((top, total, sums), given[stream][1:]):
                kept[...] = start[...]
        else:
            top[...] = jnp.full_like(top, MASKED)
            total[...] = jnp.zeros_like(total)
            sums[...] = jnp.zeros_like(sums)
        for chunk in range(chunks):
            pair = pairs[chunk]

            def work(
                key_at,
                query_at,
                key_block,
                query_block,
                masked,
                pair=pair,
                queries=queries,
                top=top,
                total=total,
                sums=sums,
            ):
                scores = [
                    score_block(
                        info,
                        pair[0, head, :, key_at],
                        queries[head, :, query_at],
                        key_block,
                        query_block,
                        masked,
                    )
                    for head in range(heads)
                ]
                olds = [top[head, :, query_at] for head in range(heads)]
                news = [
                    jnp.maximum(old, jnp.max(score, axis=0, keepdims=True) * factor)
                    for old, score in zip(olds, scores)
                ]
                weights = [jnp.exp2(score * factor - new) for score, new in zip(scores, news)]
                products = [
                    contract(pair[1, head, :, key_at], weights[head].astype(BF16), 1, 0)
                    for head in range(heads)
                ]
                for head in range(heads):
                    decay = jnp.exp2(olds[head] - news[head])
                    top[head, :, query_at] = news[head]
                    total[head, :, query_at] = total[head, :, query_at] * decay + jnp.sum(
                        weights[head], axis=0, keepdims=True
                    )
                    sums[head, :, query_at] = sums[head, :, query_at] * decay + products[head]

            for_blocks(info, stream, first_chunk + chunk, rows, work)
        if last:
            mixed, log_total = results[stream]
            for head in range(heads):
                mixed[head] = (sums[head] / total[head]).astype(BF16)
                log_total[head] = top[head] + jnp.log2(total[head])


def attend_back_kernel(first_chunk, chunks, resumed, info, *refs):
    per_stream = 5 if resumed else 4
    streams = (len(refs) - 2 * chunks - 2) // (per_stream + 1)
    given = [refs[per_stream * i : per_stream * (i + 1)] for i in range(streams)]
    refs = refs[per_stream * streams :]
    pairs, refs = refs[:chunks], refs[chunks:]
    query_sums, refs = refs[:streams], refs[streams:]
    grad_pairs, refs = refs[:chunks], refs[chunks:]
    inner, pair_sums = refs
    heads, head_size, tokens = given[0][0].shape
    rows = tokens // 2
    scale = head_size**-0.5
    factor = scale * LOG2E
    for stream in range(streams):
        _, grad_mixed, mixed = given[stream][:3]
        for head in range(heads):
            inner[stream, head] = jnp.sum(
                grad_mixed[head].astype(F32) * mixed[head].astype(F32), axis=0, keepdims=True
            )
        query_sums[stream][...] = (
            given[stream][4][...] if resumed else jnp.zeros_like(query_sums[stream])
        )
    for chunk in range(chunks):
        pair = pairs[chunk]
        pair_sums[...] = jnp.zeros_like(pair_sums)
        for stream in range(streams):
            queries, grad_mixed, _, log_total = given[stream][:4]

            def work(
                key_at,
                query_at,
                key_block,
                query_block,
                masked,
                pair=pair,
                stream=stream,
                queries=queries,
                grad_mixed=grad_mixed,
                log_total=log_total,
            ):
                every = range(heads)
                keys = [pair[0, head, :, key_at] for head in every]
                values = [pair[1, head, :, key_at] for head in every]
                query_parts = [queries[head, :, query_at] for head in every]
                grad_parts = [grad_mixed[head, :, query_at] for head in every]
                scores = [
                    score_block(info, keys[h], query_parts[h], key_block, query_block, masked)
                    for h in every
                ]
                grad_probs = [contract(values[h], grad_parts[h], 0, 0) for h in every]
                probs = [
                    jnp.exp2(scores[h] * factor - log_total[h, :, query_at]) for h in every
                ]
                grad_scores = [
                    (probs[h] * (grad_probs[h] - inner[stream, h, :, query_at])).astype(BF16)
                    for h in every
                ]
                low_probs = [member.astype(BF16) for member in probs]
                for_values = [contract(grad_parts[h], low_probs[h], 1, 1) for h in every]
                for_keys = [contract(query_parts[h], grad_scores[h], 1, 1) for h in every]
                for_queries = [contract(keys[h], grad_scores[h], 1, 0) for h in every]
                for h in every:
                    pair_sums[0, h, :, key_at] += for_keys[h]
                    pair_sums[1, h, :, key_at] += for_values[h]
                    query_sums[stream][h, :, query_at] += for_queries[h]

            for_blocks(info, stream, first_chunk + chunk, rows, work)
        grad_pairs[chunk][0] = (pair_sums[0] * scale).astype(grad_pairs[chunk].dtype)
        grad_pairs[chunk][1] = pair_sums[1].astype(grad_pairs[chunk].dtype)


SMALL_COST = pl.CostEstimate(flops=1 << 20, bytes_accessed=1 << 20, transcendentals=0)


def attend(info, queries, pairs, first_chunk, states, last):
    heads, head_size, tokens = queries[0].shape
    vmem = pl.BlockSpec(memory_space=pltpu.VMEM)
    state = [(heads, 1, tokens), (heads, 1, tokens), (heads, head_size, tokens)]
    operands = []
    for stream, member in enumerate(queries):
        operands.append(member)
        if states is not None:
            operands.extend(states[stream])
    operands.extend(pairs)
    if last:
        shapes = [
            jax.ShapeDtypeStruct((heads, head_size, tokens), BF16),
            jax.ShapeDtypeStruct((heads, 1, tokens), F32),
        ]
    else:
        shapes = [jax.ShapeDtypeStruct(shape, F32) for shape in state]
    results = pl.pallas_call(
        functools.partial(
            attend_kernel, first_chunk, len(pairs), len(queries), states is not None, last
        ),
        out_shape=tuple(shapes * len(queries)),
        in_specs=[pl.BlockSpec(memory_space=pltpu.SMEM)] + [vmem] * len(operands),
        out_specs=(vmem,) * (len(shapes) * len(queries)),
        scratch_shapes=[pltpu.VMEM(shape, F32) for shape in state] * len(queries) if last else [],
        compiler_params=pltpu.CompilerParams(vmem_limit_bytes=24 << 20),
        cost_estimate=SMALL_COST,
    )(info, *operands)
    return [results[len(shapes) * i : len(shapes) * (i + 1)] for i in range(len(queries))]


def attend_back(info, given, pairs, first_chunk, resumed, pair_type):
    heads, head_size, tokens = given[0][0].shape
    vmem = pl.BlockSpec(memory_space=pltpu.VMEM)
    operands = [member for stream in given for member in stream] + list(pairs)
    results = pl.pallas_call(
        functools.partial(attend_back_kernel, first_chunk, len(pairs), resumed),
        out_shape=tuple(
            jax.ShapeDtypeStruct((heads, head_size, tokens), F32) for _ in given
        )
        + tuple(jax.ShapeDtypeStruct(pair.shape, pair_type) for pair in pairs),
        in_specs=[pl.BlockSpec(memory_space=pltpu.SMEM)] + [vmem] * len(operands),
        out_specs=(vmem,) * (len(given) + len(pairs)),
        scratch_shapes=[
            pltpu.VMEM((len(given), heads, 1, tokens), F32),
            pltpu.VMEM((2, heads, head_size, tokens), F32),
        ],
        compiler_params=pltpu.CompilerParams(vmem_limit_bytes=32 << 20),
        cost_estimate=SMALL_COST,
    )(info, *operands)
    return results[: len(given)], results[len(given) :]


def near():
    tensor = lax.axis_index(TENSOR)
    return {TENSOR: tensor + 1 - 2 * lax.rem(tensor, 2)}


def far():
    tensor = lax.axis_index(TENSOR)
    return {TENSOR: tensor + 2 - 4 * lax.rem(tensor // 2, 2)}


def pair():
    seq = lax.axis_index(SEQ)
    return {SEQ: seq + 1 - 2 * lax.rem(seq, 2)}


def pair_far():
    seq = lax.axis_index(SEQ)
    return {SEQ: seq + 2 - 4 * lax.rem(seq // 2, 2)}


def across():
    return {CELL: 1 - lax.axis_index(CELL)}


class Wires:
    def __init__(self, r, partners):
        self.send, self.recv, self.local = r.send, r.recv, r.local
        self.started, self.open = 0, []
        barrier = pltpu.get_barrier_semaphore()
        for partner in partners:
            pl.semaphore_signal(barrier, inc=1, device_id=partner(), device_id_type=MESH)
        pl.semaphore_wait(barrier, len(partners))

    def start(self, source, target, partner):
        at = self.started
        copy = pltpu.make_async_remote_copy(
            src_ref=source,
            dst_ref=target,
            send_sem=self.send.at[at],
            recv_sem=self.recv.at[at],
            device_id=partner(),
            device_id_type=MESH,
        )
        copy.start()
        self.started += 1
        self.open.append(copy)
        return copy

    def sent(self, copy):
        copy.wait_send()
        self.open = [member for member in self.open if member is not copy]

    def finish(self):
        for copy in self.open:
            copy.wait_send()


class Local:
    def __init__(self, r, at, source, target):
        self.copy = pltpu.make_async_copy(source, target, r.local.at[at])
        self.copy.start()
        self.target, self.waited = target, False

    def get(self):
        if not self.waited:
            self.copy.wait()
            self.waited = True
        return self.target


def call_kernel(body, given, in_hbm, results, out_hbm, scratch, collective_id):
    scratch = dict(
        scratch,
        send=pltpu.SemaphoreType.DMA((COPIES,)),
        recv=pltpu.SemaphoreType.DMA((COPIES,)),
        local=pltpu.SemaphoreType.DMA((12,)),
    )
    vmem, hbm = pl.BlockSpec(memory_space=pltpu.VMEM), pl.BlockSpec(memory_space=pl.ANY)
    trees = (given, in_hbm, results, out_hbm, scratch)
    flat = [jax.tree.flatten(tree) for tree in trees]

    def kernel(*refs):
        found, at = {}, 0
        for leaves, tree in flat:
            found.update(jax.tree.unflatten(tree, refs[at : at + len(leaves)]))
            at += len(leaves)
        body(types.SimpleNamespace(**found))

    outs = pl.pallas_call(
        kernel,
        out_shape=tuple(flat[2][0] + flat[3][0]),
        in_specs=[vmem] * len(flat[0][0]) + [hbm] * len(flat[1][0]),
        out_specs=tuple([vmem] * len(flat[2][0]) + [hbm] * len(flat[3][0])),
        scratch_shapes=flat[4][0],
        compiler_params=pltpu.CompilerParams(
            collective_id=collective_id, has_side_effects=True, vmem_limit_bytes=62 << 20
        ),
        cost_estimate=SMALL_COST,
    )(*flat[0][0], *flat[1][0])
    count = len(flat[2][0])
    found = jax.tree.unflatten(flat[2][1], outs[:count])
    found.update(jax.tree.unflatten(flat[3][1], outs[count:]))
    return found


def shape_of(shape, dtype):
    return jax.ShapeDtypeStruct(shape, dtype)


def twice(value):
    return [value, value]


def by_rows(count, work, step=32):
    def one(index, carry):
        work(pl.ds(pl.multiple_of(index * step, step), step))
        return carry

    lax.fori_loop(0, count // step, one, 0)


def by_columns(width, work, step=128):
    def one(index, carry):
        work(pl.ds(pl.multiple_of(index * step, step), step))
        return carry

    lax.fori_loop(0, width // step, one, 0)
    if width % step:
        work(pl.ds(width // step * step, width % step))


def head_rows(source, rows):
    parts = [source[head, :, rows].astype(F32) for head in range(source.shape[0])]
    return jnp.concatenate(parts, axis=0).T


def put_heads(target, rows, values):
    head_size = target.shape[1]
    for head in range(target.shape[0]):
        target[head, :, rows] = values[head * head_size : (head + 1) * head_size].astype(
            target.dtype
        )


class Exchange:
    def __init__(self, wires, part, sent, got):
        self.wires, self.part, self.sent, self.got = wires, part, sent, got
        self.rows = part.shape[0]

    def give(self, values):
        self.sent[0] = values.astype(BF16)
        self.to_near = self.wires.start(self.sent.at[0], self.got.at[0], near)

    def keep(self, values):
        self.part[...] = values

    def part_rows(self, part):
        return pl.ds(part * (self.rows // 2), self.rows // 2)

    def join(self, cross):
        self.to_near.wait_recv()
        self.to_far = [None, None]
        for part in (0, 1):
            start = part * (self.rows // 2)

            def work(rows, start=start):
                at = pl.ds(start + rows.start, rows.size)
                self.sent[1, at] = (self.part[at] + self.got[0, at].astype(F32)).astype(BF16)

            by_rows(self.rows // 2, work)
            if cross:
                self.cross(part)

    def cross(self, part):
        rows = self.part_rows(part)
        self.to_far[part] = self.wires.start(
            self.sent.at[1, rows], self.got.at[1, rows], far
        )

    def wait(self, then=None):
        for part in (0, 1):
            self.to_far[part].wait_recv()
            if then is not None:
                then.cross(part)

    def total(self, rows):
        return self.sent[1, rows].astype(F32) + self.got[1, rows].astype(F32)


class Sum:
    def __init__(self, wires, whole, out, near_sum, got, got_far):
        self.wires, self.whole, self.out = wires, whole, out
        self.near_sum, self.got, self.got_far = near_sum, got, got_far
        self.bit = lax.rem(lax.axis_index(SEQ), 2)
        self.copy = None

    def wait(self):
        if self.copy is not None:
            self.copy.wait_recv()
            self.copy = None

    def add(self, target, left, right):
        def work(columns):
            target[:, columns] = (
                left[:, columns].astype(F32) + right[:, columns].astype(F32)
            ).astype(BF16)

        by_columns(target.shape[1], work)

    def one(self):
        self.copy = self.wires.start(self.whole.at[1 - self.bit], self.got, pair)

    def two(self):
        self.wait()
        self.add(self.near_sum, self.whole.at[self.bit], self.got)
        self.copy = self.wires.start(self.near_sum, self.got_far, pair_far)

    def three(self):
        self.wait()
        mine = self.out.at[self.bit]
        self.add(mine, self.near_sum, self.got_far)
        self.copy = self.wires.start(mine, mine, pair)

    def five(self, everything, rows):
        self.wait()
        target = everything.at[lax.axis_index(CELL), :, rows]
        self.copy = self.wires.start(self.out, target, across)
        return self.out, target


def sum_scratch(rows, width):
    return [pltpu.VMEM((rows, width), BF16)] * 3


def exchange_scratch(half, width, exchanges):
    return dict(
        part=pltpu.VMEM((2, half, width), F32),
        sent=pltpu.VMEM((2 * exchanges, 2, half, width), BF16),
        got=pltpu.VMEM((2 * exchanges, 2, half, width), BF16),
    )


def exchanges_of(r, wires, count):
    return [
        [Exchange(wires, r.part.at[i], r.sent.at[2 * k + i], r.got.at[2 * k + i]) for i in (0, 1)]
        for k in range(count)
    ]


def project(r, i, to_near, weight):
    half = r.wide_one[i].shape[0] // 2
    for part in (0, 1):
        at = pl.ds(part * half, half)
        if part and to_near is not None:
            to_near.wait_recv()
        wide = r.wide_one[i][at]
        for j in range(3):
            values = contract(wide, weight[j], 1, 1) + r.qkv_b[j : j + 1]
            target = r.queries[i] if j == 0 else r.pair[i].at[j - 1]
            put_heads(target, at, values.T)


def side_and_core():
    return lax.axis_index(SEQ) // 2, lax.rem(lax.axis_index(TENSOR), 2)


def core_columns(half, core):
    return pl.ds(pl.multiple_of(core * half, half), half)


def start_kernel(r):
    side, core = side_and_core()
    half = r.stream[0].shape[0]
    own = Local(r, 0, r.tokens.at[side], r.own_tokens)
    weight = Local(r, 1, r.qkv_w.at[0], r.own_qkv)
    wires = Wires(r, (near, pair, pair_far))
    arriving = wires.start(
        r.tokens.at[1 - side, :, core_columns(half, core)], r.got_tokens, pair_far
    )

    def norm(i, part, values):
        r.rows[...] = values.astype(F32).T

        def work(rows):
            stream = r.rows[rows]
            normed, inverse = normalize(stream)
            if part == 0:
                r.stream[i][rows] = stream
                r.normed_one[i][rows] = normed.astype(BF16)
                r.inverse_one[i][rows] = inverse
            to = pl.ds(part * half + rows.start, rows.size)
            r.wide_one[i][to] = (normed * r.gain[...] + r.shift[...]).astype(BF16)

        by_rows(half, work)

    tokens = own.get()
    for part in (0, 1):
        norm(0, part, tokens[:, core_columns(half, lax.rem(core + part, 2))])
    project(r, 0, None, weight.get())
    paired = wires.start(r.pair[0], r.got_pair, pair)
    arriving.wait_recv()
    norm(1, 0, r.got_tokens[...])
    wide = r.wide_one[1]
    to_near = wires.start(wide.at[pl.ds(0, half)], wide.at[pl.ds(half, half)], near)
    project(r, 1, to_near, weight.get())
    paired.wait_recv()
    wires.finish()


def next_shapes(half, width, head_shape):
    return dict(
        stream=twice(shape_of((half, width), F32)),
        wide_one=twice(shape_of((2 * half, width), BF16)),
        normed_one=twice(shape_of((half, width), BF16)),
        inverse_one=twice(shape_of((half, 1), F32)),
        queries=twice(shape_of(head_shape, BF16)),
        pair=twice(shape_of((2,) + head_shape, BF16)),
        got_pair=shape_of((2,) + head_shape, BF16),
    )


def start_call(tokens, qkv_w, qkv_b, gain, shift, head_shape, collective_id):
    _, width, row_count = tokens.shape
    half = row_count // 2
    return call_kernel(
        start_kernel,
        dict(qkv_b=qkv_b, gain=gain, shift=shift),
        dict(tokens=tokens, qkv_w=qkv_w),
        next_shapes(half, width, head_shape),
        {},
        dict(
            own_tokens=pltpu.VMEM((width, row_count), BF16),
            got_tokens=pltpu.VMEM((width, half), BF16),
            own_qkv=pltpu.VMEM(qkv_w.shape[1:], BF16),
            rows=pltpu.VMEM((half, width), F32),
        ),
        collective_id,
    )


def forward_kernel(layer, last, r):
    side, core = side_and_core()
    half = r.base[0].shape[0]
    halves = (pl.ds(0, half), pl.ds(half, half))
    out_w = Local(r, 0, r.out_w.at[layer], r.own_out)
    up_w = Local(r, 1, r.up_w.at[layer], r.own_up)
    down_w = Local(r, 2, r.down_w.at[layer], r.own_down)
    if not last:
        qkv_w = Local(r, 3, r.qkv_w.at[layer + 1], r.own_qkv)
    wires = Wires(r, (near, far) + (() if last else (pair, pair_far)))
    first, second = exchanges_of(r, wires, 2)
    to_near = {}

    def row(index):
        return r.vectors[index : index + 1]

    def norm(i, exchange, base, at, kept, normed_to, inverse_to, wide):
        def work(rows):
            stream = base[rows] + exchange.total(rows) + row(at)
            normed, inverse = normalize(stream)
            kept[rows] = stream
            normed_to[rows] = normed.astype(BF16)
            inverse_to[rows] = inverse
            wide[rows] = (normed * row(at + 1) + row(at + 2)).astype(BF16)

        by_rows(half, work)
        to_near[i] = wires.start(wide.at[halves[0]], wide.at[halves[1]], near)

    def attended(i):
        for part in (1, 0):
            values = mm(head_rows(r.mixed[i], halves[part]).astype(BF16), out_w.get()[...])
            (first[i].give if part else first[i].keep)(values)

    def mid_norm(i):
        norm(
            i, first[i], r.base[i], 0, r.mid.at[i], r.normed_two[i], r.inverse_two[i], r.wide_two[i]
        )

    def feed(i):
        for part in (0, 1):
            if part:
                to_near[i].wait_recv()
            r.wide_part[...] = mm(r.wide_two[i][halves[part]], up_w.get()[...])

            def work(rows, part=part):
                hidden, slope = gelu_both(r.wide_part[rows] + r.up_b[...])
                to = pl.ds(part * half + rows.start, rows.size)
                r.hidden[i][to] = hidden
                r.slope[i][to] = slope

            by_rows(half, work)
        for part in (1, 0):
            values = mm(r.hidden[i][halves[part]], down_w.get()[...])
            (second[i].give if part else second[i].keep)(values)

    def leave(i):
        if last:

            def work(rows):
                r.part[i, rows] = r.mid[i, rows] + second[i].total(rows) + row(3)

            by_rows(half, work)
            r.low[i][...] = r.part[i].T.astype(BF16)
        else:
            norm(
                i, second[i], r.mid.at[i], 3, r.stream[i], r.normed_one[i], r.inverse_one[i],
                r.wide_one[i],
            )
            project(r, i, to_near[i], qkv_w.get())

    for i in (0, 1):
        attended(i)
    first[0].join(True)
    first[1].join(False)
    first[0].wait(first[1])
    if not last:
        given = wires.start(
            r.out_grad.at[1 - side, :, core_columns(half, core)], r.got_grad, pair_far
        )
    mid_norm(0)
    feed(0)
    second[0].join(False)
    first[1].wait(second[0])
    mid_norm(1)
    feed(1)
    second[1].join(False)
    second[0].wait(second[1])
    leave(0)
    if not last:
        paired = wires.start(r.pair[0], r.got_pair, pair)
    second[1].wait()
    leave(1)
    if not last:
        given.wait_recv()
        paired.wait_recv()
    wires.finish()


def forward_call(given, in_hbm, layer, last, collective_id):
    half, width = given["base"][0].shape
    hidden_width = in_hbm["up_w"].shape[2]
    head_shape = given["mixed"][0].shape
    wide_hidden = shape_of((2 * half, hidden_width), BF16)
    results = dict(
        wide_two=twice(shape_of((2 * half, width), BF16)),
        normed_two=twice(shape_of((half, width), BF16)),
        inverse_two=twice(shape_of((half, 1), F32)),
        hidden=twice(wide_hidden),
        slope=twice(wide_hidden),
    )
    out_hbm = {}
    scratch = dict(
        exchange_scratch(half, width, 2),
        mid=pltpu.VMEM((2, half, width), F32),
        wide_part=pltpu.VMEM((half, hidden_width), F32),
        own_out=pltpu.VMEM(in_hbm["out_w"].shape[1:], BF16),
        own_up=pltpu.VMEM(in_hbm["up_w"].shape[1:], BF16),
        own_down=pltpu.VMEM(in_hbm["down_w"].shape[1:], BF16),
    )
    if last:
        results.update(low=twice(shape_of((width, half), BF16)))
    else:
        results.update(next_shapes(half, width, head_shape))
        out_hbm.update(got_grad=shape_of((width, half), BF16))
        scratch.update(own_qkv=pltpu.VMEM(in_hbm["qkv_w"].shape[1:], BF16))
    return call_kernel(
        functools.partial(forward_kernel, layer, last),
        given,
        in_hbm,
        results,
        out_hbm,
        scratch,
        collective_id,
    )


def backward_kernel(attention, feed, riding, r):
    begin, end = attention is None, feed is None
    side, core = side_and_core()
    half = r.grad_out[0].shape[0]
    halves = (pl.ds(0, half), pl.ds(half, half))
    if begin:
        own = Local(r, 0, r.out_grad.at[side], r.own_grad)
    else:
        qkv_w = Local(r, 1, r.qkv_w.at[attention], r.own_qkv)
    if not end:
        down_w = Local(r, 2, r.down_w.at[feed], r.own_down)
        up_w = Local(r, 3, r.up_w.at[feed], r.own_up)
        out_w = Local(r, 4, r.out_w.at[feed], r.own_out)
    partners = [near, far]
    if begin or riding:
        partners.append(pair_far)
    if riding:
        partners.append(pair)
    wires = Wires(r, partners)
    exchanges = exchanges_of(r, wires, int(not begin) + int(not end))
    to_near = {}
    r.sums[...] = jnp.zeros_like(r.sums)
    if riding:
        rider = Sum(wires, r.whole, r.summed if riding == 2 else None, r.near_sum, r.got_sum, r.got_far)

    def note(index, values):
        r.sums[index : index + 1, : values.shape[1]] += jnp.sum(values, axis=0, keepdims=True)

    def gather(i, exchange):
        scale = HEAD**-0.5
        for part in (1, 0):
            at = halves[part]
            values = None
            for j in range(3):
                target = r.grads[i].at[j]
                for head in range(target.shape[0]):
                    if j == 0:
                        found = r.query_sum[i][head, :, at] * scale
                    else:
                        found = r.pair_sum[i][j - 1, head, :, at] + r.pair_got[i][
                            j - 1, head, :, at
                        ].astype(F32)
                    target[head, :, at] = found.astype(BF16)
                rows = head_rows(target, at)
                if j != 1:
                    start = j // 2 * (r.sums.shape[1] // 256 * 128)
                    r.sums[7:8, start : start + rows.shape[1]] += jnp.sum(
                        rows, axis=0, keepdims=True
                    )
                product = mm(rows.astype(BF16), qkv_w.get()[j])
                values = product if values is None else values + product
            (exchange.give if part else exchange.keep)(values)

    def norm(i, exchange, base, normed_of, inverse_of, gain, at, wide):
        def work(rows):
            incoming = exchange.total(rows)
            normed = normed_of[rows].astype(F32)
            grad = base[rows] + norm_back(
                incoming, normed, inverse_of[rows], r.gains[gain : gain + 1]
            )
            r.grad_out[i][rows] = grad
            note(at, incoming * normed)
            note(at + 1, incoming)
            note(at + 2, grad)
            if wide is not None:
                wide[rows] = grad.astype(BF16)

        by_rows(half, work)
        if wide is not None:
            to_near[i] = wires.start(wide.at[halves[0]], wide.at[halves[1]], near)

    def first_norm(i):
        norm(
            i, exchanges[0][i], r.grad[i], r.normed_one[i], r.inverse_one[i], 0, 0,
            None if end else r.wide[i],
        )
        if end:
            r.low[i][...] = r.grad_out[i][...].T.astype(BF16)

    def second_norm(i):
        norm(
            i, exchanges[-1][i], r.grad_out[i], r.normed_two[i], r.inverse_two[i], 1, 3,
            r.wide_mid[i],
        )
        for part in (0, 1):
            if part:
                to_near[i].wait_recv()
            values = contract(out_w.get()[...], r.wide_mid[i][halves[part]], 1, 1)
            put_heads(r.mixed_grad[i], halves[part], values)

    def first_rows(i):
        if i == 0:
            given = own.get()
            for part in (0, 1):
                values = given[:, core_columns(half, lax.rem(core + part, 2))].astype(F32).T
                if part == 0:
                    r.grad_out[0][...] = values
                r.wide[0][halves[part]] = values.astype(BF16)
        else:
            r.grad_out[1][...] = r.got_grad[...].astype(F32).T
            wide = r.wide[1]
            wide[halves[0]] = r.grad_out[1][...].astype(BF16)
            to_near[1] = wires.start(wide.at[halves[0]], wide.at[halves[1]], near)
        by_rows(half, lambda rows: note(2, r.grad_out[i][rows]))

    def slide(i, exchange):
        wide = r.wide[i]
        for part in (0, 1):
            if part and i in to_near:
                to_near[i].wait_recv()
            r.wide_part[...] = contract(wide[halves[part]], down_w.get()[...], 1, 1)

            def work(rows, part=part):
                to = pl.ds(part * half + rows.start, rows.size)
                hidden = r.wide_part[rows].astype(BF16).astype(F32)
                pre = (hidden * r.slope[i][to].astype(F32)).astype(BF16)
                r.pre[i][to] = pre
                note(6, pre.astype(F32))

            by_rows(half, work)
        for part in (1, 0):
            values = contract(r.pre[i][halves[part]], up_w.get()[...], 1, 1)
            (exchange.give if part else exchange.keep)(values)

    def ride(step):
        if riding and step == 0:
            rider.one()
            if riding == 1:
                r.late = wires.start(r.near_late, r.far_late, pair_far)
        elif riding and step == 1:
            rider.two()
        elif riding and step == 5:
            rider.wait()
            if riding == 1:
                r.late.wait_recv()
        elif riding == 2 and step == 3:
            rider.three()

    ride(0)
    if begin:
        (after,) = exchanges
        placed = place_cells(r, wires, r.block, r.block_low)
        for i in (0, 1):
            first_rows(i)
            slide(i, after[i])
            after[i].join(i == 0)
        after[0].wait(after[1])
        second_norm(0)
        placed.forward()
        after[1].wait()
        second_norm(1)
        placed.finish()
    else:
        before, after = exchanges[0], exchanges[-1]
        a, b = (1, 0) if end else (0, 1)
        gather(a, before[a])
        gather(b, before[b])
        before[a].join(True)
        before[b].join(False)
        ride(1)
        before[a].wait(before[b])
        first_norm(a)
        if end:
            before[b].wait()
            first_norm(b)
        else:
            slide(a, after[a])
            after[a].join(False)
            before[b].wait(after[a])
            first_norm(b)
            slide(b, after[b])
            after[b].join(False)
            after[a].wait(after[b])
            ride(3)
            second_norm(a)
            after[b].wait()
            second_norm(b)
    ride(5)
    wires.finish()


class place_cells:
    def __init__(self, r, wires, target, low):
        side, core = side_and_core()
        half = low[0].shape[1]
        self.wires = wires
        columns = core_columns(half, core)
        self.own = target.at[side, :, columns]
        self.arrived = target.at[1 - side, :, columns]
        self.local = Local(r, 11, low[0], self.own)
        self.to_far = wires.start(low[1], self.own, pair_far)
        self.to_near = wires.start(low[0], self.own, near)

    def forward(self):
        self.to_far.wait_recv()
        self.second = self.wires.start(self.arrived, self.arrived, near)

    def finish(self):
        self.local.get()
        self.to_near.wait_recv()
        self.second.wait_recv()


def backward_call(given, in_hbm, attention, feed, riding, collective_id):
    begin, end = attention is None, feed is None
    some = given["block_low"][0] if begin else given["grad"][0]
    width = given["gains"].shape[1]
    half = some.shape[1] if begin else some.shape[0]
    results = dict(sums=shape_of((8, width), F32), grad_out=twice(shape_of((half, width), F32)))
    wide = twice(shape_of((2 * half, width), BF16))
    out_hbm = {}
    scratch = exchange_scratch(half, width, int(not begin) + int(not end))
    if begin:
        out_hbm.update(block=shape_of((2, width, 2 * half), BF16))
        scratch.update(own_grad=pltpu.VMEM((width, 2 * half), BF16))
    else:
        head_shape = given["query_sum"][0].shape
        results.update(grads=twice(shape_of((3,) + head_shape, BF16)))
        scratch.update(own_qkv=pltpu.VMEM(in_hbm["qkv_w"].shape[1:], BF16))
    if end:
        results.update(low=twice(shape_of((width, half), BF16)))
    else:
        hidden_width = in_hbm["up_w"].shape[2]
        head_count = in_hbm["out_w"].shape[1] // HEAD
        results.update(
            wide=wide,
            wide_mid=wide,
            pre=twice(shape_of((2 * half, hidden_width), BF16)),
            mixed_grad=twice(shape_of((head_count, HEAD, 2 * half), BF16)),
        )
        scratch.update(
            wide_part=pltpu.VMEM((half, hidden_width), F32),
            own_out=pltpu.VMEM(in_hbm["out_w"].shape[1:], BF16),
            own_up=pltpu.VMEM(in_hbm["up_w"].shape[1:], BF16),
            own_down=pltpu.VMEM(in_hbm["down_w"].shape[1:], BF16),
        )
    if riding:
        whole = given["whole"]
        one = pltpu.VMEM(whole.shape[1:], BF16)
        if riding == 2:
            results.update(summed=shape_of(whole.shape, BF16))
            scratch.update(near_sum=one, got_far=one)
        else:
            part = shape_of(whole.shape[1:], BF16)
            results.update(near_sum=part, got_far=part)
            results.update(far_late=shape_of(given["near_late"].shape, BF16))
        scratch.update(got_sum=one)
    return call_kernel(
        functools.partial(backward_kernel, attention, feed, riding),
        given,
        in_hbm,
        results,
        out_hbm,
        scratch,
        collective_id,
    )


def closing_kernel(sums_too, r):
    wires = Wires(r, [near, pair, pair_far] + ([across] if sums_too else []))
    cell = lax.axis_index(CELL)
    kernels = r.vectors.shape[0]
    r.total[...] = r.vectors[...]

    def vectors(at, partner, own_rows=8):
        copy = wires.start(r.total, r.around.at[at], partner)

        def add():
            copy.wait_recv()
            wires.sent(copy)
            for kernel in range(kernels):
                r.total[kernel, :own_rows] += r.around[at, kernel, :own_rows]

        return add

    if sums_too:
        span = r.sum_feed[0].shape[1]
        spans = [pl.ds(0, span), pl.ds(span, r.all_feed.shape[2] - span)]
        whole = pl.ds(0, r.all_last.shape[2])
        arriving = wires.start(r.sent_last, r.got_last, across)
        feed = [
            Sum(wires, r.whole_feed[k], r.sum_feed[k], *r.riding_feed[k]) for k in (0, 1)
        ]
        last = Sum(wires, r.whole_last, r.sum_last, *r.riding_last)
        late = Sum(wires, None, r.sum_late, r.near_late, None, r.far_late)
        prior = Sum(wires, None, r.sum_prior, r.near_prior, None, r.far_prior)
        local = []

        def fold(target, kept, got, rows):
            def work(columns):
                target[:, :, columns] = (
                    kept[:, rows, columns].astype(F32) + got[:, rows, columns].astype(F32)
                ).astype(BF16)

            by_columns(kept.shape[2], work)

        def five(member, everything, rows):
            own, target = member.five(everything, rows)
            local.append(Local(r, len(local), own, target))

        late.three()
        fold(r.whole_feed[0], r.kept_feed, r.got_feed, spans[0])
        feed[0].one()
        local.append(Local(r, 0, r.early, r.all_late.at[cell, :, spans[0]]))
        local.append(Local(r, 1, r.got_early, r.all_late.at[1 - cell, :, spans[0]]))
        add = vectors(0, near, 6)
        feed[0].two()
        arriving.wait_recv()
        fold(r.whole_last, r.kept_last, r.got_last, whole)
        last.one()
        prior.three()
        five(late, r.all_late, spans[1])
        fold(r.whole_feed[1], r.kept_feed, r.got_feed, spans[1])
        feed[0].three()
        five(prior, r.all_prior, whole)
        last.two()
        feed[1].one()
        last.three()
        feed[1].two()
        five(feed[0], r.all_feed, spans[0])
        add()
        add = vectors(1, across)
        five(last, r.all_last, whole)
        feed[1].three()
        add()
        add = vectors(2, pair)
        five(feed[1], r.all_feed, spans[1])
        add()
        placed = place_cells(r, wires, r.tokens_grad, r.low)
        add = vectors(3, pair_far)
        placed.forward()
        add()
        for member in feed + [late, prior, last]:
            member.wait()
        for copy in local:
            copy.get()
    else:
        placed = place_cells(r, wires, r.tokens_grad, r.low)
        vectors(0, near, 6)()
        placed.forward()
        vectors(1, pair)()
        vectors(2, pair_far)()
    r.totals[...] = r.total[...]
    placed.finish()
    wires.finish()


def closing_call(given, in_hbm, sums_too, collective_id):
    width, half = given["low"][0].shape
    vectors = given["vectors"].shape
    results = dict(totals=shape_of(vectors, F32))
    out_hbm = dict(tokens_grad=shape_of((2, width, 2 * half), BF16))
    scratch = dict(total=pltpu.VMEM(vectors, F32), around=pltpu.VMEM((4,) + vectors, F32))
    if sums_too:
        feed, last = given["kept_feed"].shape, given["kept_last"].shape
        late = (2,) + given["near_late"].shape
        early = (feed[0], feed[1] - late[1]) + feed[2:]
        spans = [pltpu.VMEM(early, BF16), pltpu.VMEM(late, BF16)]
        out_hbm.update(
            all_feed=shape_of((2,) + feed, BF16),
            all_late=shape_of((2,) + feed, BF16),
            all_last=shape_of((2,) + last, BF16),
            all_prior=shape_of((2,) + last, BF16),
        )
        scratch.update(
            whole_feed=spans,
            sum_feed=spans,
            riding_feed=[sum_scratch(*early[1:]), sum_scratch(*late[1:])],
            sum_late=spans[1],
            whole_last=pltpu.VMEM(last, BF16),
            sum_last=pltpu.VMEM(last, BF16),
            got_last=pltpu.VMEM(last, BF16),
            riding_last=sum_scratch(*last[1:]),
            sum_prior=pltpu.VMEM(last, BF16),
        )
    return call_kernel(
        functools.partial(closing_kernel, sums_too),
        given,
        in_hbm,
        results,
        out_hbm,
        scratch,
        collective_id,
    )


class Line:
    def __init__(self):
        self.last = None

    def run(self, step, *operands):
        if self.last is not None:
            operands, _ = lax.optimization_barrier((operands, self.last))
        results = step(*operands)
        self.last = jax.tree.leaves(results)[0]
        return types.SimpleNamespace(**results) if isinstance(results, dict) else results


def add_low(kept, got):
    return (kept.astype(F32) + got.astype(F32)).astype(BF16)


def pick(cell, low, high):
    first, second = jnp.stack(low), jnp.stack(high)
    return jnp.where(cell == 0, first, second), jnp.where(cell == 0, second, first)


def two_sum(product, left, right):
    return (product(left[0], right[0]) + product(left[1], right[1])).astype(BF16)


def feed_sums(hidden, grad_down, wide_two, pre_grad):
    up, down = two_sum(mm_left, wide_two, pre_grad), two_sum(mm_left, hidden, grad_down)
    return [part for whole in (up, down) for part in jnp.split(whole, 2, axis=0)]


def attention_sums(wide_mid, mixed, wide_one, grads):
    def product(left, right):
        return mm(left.reshape(left.shape[0] * left.shape[1], left.shape[2]), right)

    return [two_sum(product, [grad[j] for grad in grads], wide_one) for j in range(3)] + [
        two_sum(product, mixed, wide_mid)
    ]


def shards(
    tokens,
    out_grad,
    group_order,
    lengths,
    qkv_weight,
    qv_bias,
    out_weight,
    out_bias,
    up_weight,
    up_bias,
    down_weight,
    down_bias,
    norm_gain,
    norm_shift,
):
    layer_count = qkv_weight.shape[0]
    local_width = qkv_weight.shape[3]
    seq_index = lax.axis_index(SEQ)
    cell = lax.axis_index(CELL)
    core = lax.axis_index(TENSOR) % 2
    side = seq_index // 2
    paired_cells = lax.axis_size(CELL) == 2
    gains, shifts = norm_gain.astype(F32), norm_shift.astype(F32)
    row_count = tokens.shape[1]
    head_shape = (local_width // HEAD, HEAD, row_count)
    tokens, out_grad = jnp.swapaxes(tokens, 1, 2), jnp.swapaxes(out_grad, 1, 2)
    qkv_weight = jnp.swapaxes(qkv_weight, 2, 3)
    biases = qv_bias.astype(F32)
    qkv_bias = jnp.stack([biases[:, 0], jnp.zeros_like(biases[:, 0]), biases[:, 1]], axis=1)
    line = Line()

    order = jnp.where(side == 0, group_order[0], group_order[1])
    length = jnp.where(side == 0, lengths[0], lengths[1])
    offsets = jnp.array([0, 2, 0, 2, 1, 3], jnp.int32)
    slots = 2 * (seq_index ^ offsets)[:, None] + (core + jnp.arange(2)[None]) % 2
    wanted = slots.reshape(-1, 1) == jnp.arange(order.shape[0])[None]
    blocks = jnp.sum(jnp.where(wanted, order[None], 0), axis=1)
    info = jnp.concatenate([length[None], blocks]).astype(jnp.int32)

    weights = dict(out_w=out_weight, up_w=up_weight, down_w=down_weight)
    now = line.run(
        lambda *given: start_call(*given, head_shape, 0),
        tokens,
        qkv_weight,
        qkv_bias[0],
        gains[0, :1],
        shifts[0, :1],
    )
    saved = []
    for layer in range(layer_count):
        last = layer == layer_count - 1
        got_pair = swap(now.pair[1], SEQ, 1)
        states = line.run(
            lambda queries, *pairs: attend(info, queries, pairs, 0, None, False),
            now.queries,
            *now.pair,
            now.got_pair,
        )
        mixed = line.run(
            lambda queries, states, pair: attend(info, queries, [pair], 3, states, True),
            now.queries,
            states,
            got_pair,
        )
        rows = [out_bias[layer], gains[layer, 1], shifts[layer, 1], down_bias[layer]]
        given = dict(
            base=now.stream,
            mixed=[mixed[0][0], mixed[1][0]],
            up_b=up_bias[layer].astype(F32)[None],
        )
        in_hbm = dict(weights)
        if not last:
            rows += [gains[layer + 1, 0], shifts[layer + 1, 0]]
            in_hbm.update(qkv_w=qkv_weight, out_grad=out_grad)
            given.update(qkv_b=qkv_bias[layer + 1])
        given.update(vectors=jnp.stack([row.astype(F32) for row in rows]))
        found = line.run(
            lambda given, in_hbm, layer=layer, last=last: forward_call(
                given, in_hbm, layer, last, 1 + layer
            ),
            given,
            in_hbm,
        )
        saved.append(
            types.SimpleNamespace(
                queries=now.queries,
                near_pairs=now.pair,
                far_pairs=[now.got_pair, got_pair],
                wide_one=now.wide_one,
                normed_one=now.normed_one,
                inverse_one=now.inverse_one,
                mixed=[mixed[0][0], mixed[1][0]],
                log_total=[mixed[0][1], mixed[1][1]],
                wide_two=found.wide_two,
                normed_two=found.normed_two,
                inverse_two=found.inverse_two,
                hidden=found.hidden,
                slope=found.slope,
            )
        )
        if not last:
            got_grad = found.got_grad
            now = found

    identity = layer_count + 1
    block_low = found.low
    vectors = []
    halves = {}
    for layer in reversed(range(layer_count + 1)):
        begin, end = layer == layer_count, layer == 0
        given, in_hbm = dict(), dict()
        gain_rows = [gains[0, 0], gains[0, 0]]
        riding = 0
        if begin:
            given.update(got_grad=got_grad, block_low=block_low)
            in_hbm.update(out_grad=out_grad)
        else:
            above = saved[layer]
            given.update(
                grad=found.grad_out,
                query_sum=query_sums,
                pair_sum=near_sums,
                pair_got=far_got,
                normed_one=above.normed_one,
                inverse_one=above.inverse_one,
            )
            in_hbm.update(qkv_w=qkv_weight)
            gain_rows[0] = gains[layer, 0]
            if paired_cells:
                given.update(whole=line.run(add_low, *pending))
                riding = 1 if end else 2
                if end:
                    near_late = line.run(add_low, kept_late, got_late)
                    given.update(near_late=near_late)
        if not end:
            below = saved[layer - 1]
            given.update(
                slope=below.slope, normed_two=below.normed_two, inverse_two=below.inverse_two
            )
            in_hbm.update(weights)
            gain_rows[1] = gains[layer - 1, 1]
        given.update(gains=jnp.stack(gain_rows))
        found = line.run(
            lambda given, in_hbm, layer=layer, riding=riding: backward_call(
                given,
                in_hbm,
                layer if layer < layer_count else None,
                layer - 1 if layer > 0 else None,
                riding,
                identity + layer,
            ),
            given,
            in_hbm,
        )
        vectors.append(found.sums)
        if begin:
            block_out = found.block
        else:
            if riding == 2:
                early = found.summed
                got_early = swap(early, CELL, 1)
                late = line.run(add_low, *late)
                bit = seq_index % 2
                kept_late = jnp.where(bit == 0, late[0], late[1])
                got_late = swap(jnp.where(bit == 0, late[1], late[0]), SEQ, 1)
            sums = line.run(attention_sums, wide_mid, above.mixed, above.wide_one, found.grads)
            if paired_cells:
                kept, sent = line.run(functools.partial(pick, cell), sums[:2], sums[2:])
                if not end:
                    pending = [kept, swap(sent, CELL, 1)]
            else:
                halves[layer, 1] = sums
        if end:
            break
        wide_mid = found.wide_mid
        sums = line.run(feed_sums, below.hidden, found.wide, below.wide_two, found.pre)
        if paired_cells:
            kept_feed, sent_feed = line.run(functools.partial(pick, cell), sums[:2], sums[2:])
            if begin:
                cut = kept_feed.shape[1] // 32 * 16 + 16
                pending = [kept_feed[:, :cut], swap(sent_feed[:, :cut], CELL, 1)]
                late = [kept_feed[:, cut:], swap(sent_feed[:, cut:], CELL, 1)]
            else:
                got_feed = swap(sent_feed, CELL, 1)
        else:
            halves[layer - 1, 0] = sums
        streams = [
            list(members)
            for members in zip(below.queries, found.mixed_grad, below.mixed, below.log_total)
        ]
        query_sums, far_sums = line.run(
            lambda given, pairs: attend_back(info, given, pairs, 2, False, BF16),
            streams,
            below.far_pairs,
        )
        far_got = [swap(far_sum, SEQ, 1) for far_sum in far_sums]
        streams = [members + [start] for members, start in zip(streams, query_sums)]
        query_sums, near_sums = line.run(
            lambda given, pairs: attend_back(info, given, pairs, 0, True, F32),
            streams,
            below.near_pairs,
        )

    vectors = jnp.stack(vectors)
    if not paired_cells:
        vectors = lax.psum(vectors, CELL)
    given, in_hbm = dict(low=found.low, vectors=vectors), dict()
    if paired_cells:
        given.update(
            kept_feed=kept_feed,
            got_feed=got_feed,
            kept_last=kept,
            sent_last=sent,
            near_late=near_late,
            far_late=found.far_late,
            near_prior=found.near_sum,
            far_prior=found.got_far,
        )
        in_hbm.update(early=early, got_early=got_early)
    closing = line.run(
        lambda given, in_hbm: closing_call(given, in_hbm, paired_cells, identity + layer_count + 1),
        given,
        in_hbm,
    )
    if paired_cells:
        feeds = [closing.all_feed, closing.all_late]
        attentions = [closing.all_last, closing.all_prior]
    else:

        def whole(part):
            found = []
            for layer in range(layer_count):
                total = lax.psum(jnp.stack(halves[layer, part]).astype(F32), (CELL, SEQ))
                found.append(total.reshape((2, 2) + total.shape[1:]))
            return found

        feeds, attentions = whole(0), whole(1)

    def final(pieces):
        return jnp.stack([piece.astype(F32) for piece in pieces])

    def square(member):
        return member.reshape(member.shape[0] * member.shape[1], member.shape[2])

    totals = closing.totals
    attention_rows = [totals[layer_count - layer] for layer in range(layer_count)]
    feed_rows = [totals[layer_count - 1 - layer] for layer in range(layer_count)]

    def rows_of(members, *indices):
        return jnp.stack([member[index] for member in members for index in indices])

    gain_grad = jnp.stack([rows_of(attention_rows, 0), rows_of(feed_rows, 3)], axis=1)
    shift_grad = jnp.stack([rows_of(attention_rows, 1), rows_of(feed_rows, 4)], axis=1)
    second = totals.shape[2] // 256 * 128
    qv_rows = rows_of(attention_rows, 7)
    qv_grad = jnp.stack(
        [qv_rows[:, :local_width], qv_rows[:, second : second + local_width]], axis=1
    )
    return (
        jnp.swapaxes(block_out, 1, 2),
        jnp.swapaxes(closing.tokens_grad, 1, 2),
        jnp.swapaxes(
            final([jnp.stack([*member[0], member[1, 0]]) for member in attentions]), 2, 3
        ),
        qv_grad,
        final([member[1, 1] for member in attentions]),
        rows_of(feed_rows, 5),
        final([square(member[0]) for member in feeds]),
        rows_of(feed_rows, 6),
        final([square(member[1]) for member in feeds]),
        rows_of(feed_rows, 2),
        gain_grad,
        shift_grad,
    )


def solution(mesh):
    shared, by_tensor = P(), P(None, TENSOR)
    rows, last = P(CELL, SEQ, None), P(None, None, TENSOR)
    middle = P(None, TENSOR, None)
    weights = (P(None, None, None, TENSOR), last, middle, shared, last, by_tensor, middle)
    norms = (shared, shared, shared)
    return jax.shard_map(
        shards,
        mesh=mesh,
        in_specs=(rows, rows, P(CELL, None), P(CELL)) + weights + norms,
        out_specs=(rows, rows) + weights + norms,
        check_vma=False,
    )
```

```python
import functools
import types

import jax
import jax.numpy as jnp
from jax import lax
from jax.experimental import pallas as pl
from jax.experimental.pallas import tpu as pltpu
from jax.sharding import PartitionSpec as P

HEAD = 56
EPSILON = 1e-05
MASKED = -1e30
ROOT_TWO_PI = 0.7978845608028654
CUBIC = 0.044715
LOG2E = 1.4426950408889634
F32 = jnp.float32
BF16 = jnp.bfloat16
MESH = pl.DeviceIdType.MESH
CELL, SEQ, TENSOR = "cell", "seq", "tensor"
COPIES = 28


def swap(values, axis, bit):
    size = lax.axis_size(axis)
    return lax.ppermute(values, axis, [(i, i ^ bit) for i in range(size)])


def normalize(values):
    centred = values - jnp.mean(values, axis=-1, keepdims=True)
    spread = jnp.mean(centred * centred, axis=-1, keepdims=True)
    inverse = lax.rsqrt(spread + EPSILON)
    return (centred * inverse, inverse)


def norm_back(incoming, normed, inverse, gain_row):
    scaled = incoming * gain_row
    first_mean = jnp.mean(scaled, axis=-1, keepdims=True)
    second_mean = jnp.mean(scaled * normed, axis=-1, keepdims=True)
    return inverse * (scaled - first_mean - normed * second_mean)


def gelu_both(values):
    inner = jnp.tanh(ROOT_TWO_PI * (values + CUBIC * values * values * values))
    hidden = 0.5 * values * (1.0 + inner)
    slope = 0.5 * (1.0 + inner) + 0.5 * values * (1.0 - inner * inner) * ROOT_TWO_PI * (
        1.0 + 3.0 * CUBIC * values * values
    )
    return hidden.astype(BF16), slope.astype(BF16)


def contract(left, right, left_dim, right_dim):
    return lax.dot_general(
        left, right, (((left_dim,), (right_dim,)), ((), ())), preferred_element_type=F32
    )


def mm(left, right):
    return contract(left, right, 1, 0)


def mm_left(left, right):
    return contract(left, right, 0, 0)


def score_block(info, keys, queries, key_block, query_block, masked):
    scores = contract(keys, queries, 0, 0)
    if masked:
        rows = scores.shape[0]
        key_place = key_block * rows + lax.broadcasted_iota(jnp.int32, scores.shape, 0)
        query_place = query_block * rows + lax.broadcasted_iota(jnp.int32, scores.shape, 1)
        allowed = (key_place <= query_place) & (key_place < info[0])
        scores = jnp.where(allowed, scores, MASKED)
    return scores


def for_blocks(info, stream, chunk, block_rows, work):
    def one(step, carry):
        key_half, query_half = step // 2, step % 2
        key_block, query_block = info[5 + 2 * chunk + key_half], info[1 + 2 * stream + query_half]
        key_at = pl.ds(pl.multiple_of(key_half * block_rows, block_rows), block_rows)
        query_at = pl.ds(pl.multiple_of(query_half * block_rows, block_rows), block_rows)
        first = key_block * block_rows
        counts = (key_block <= query_block) & (first < info[0])
        partial = (key_block == query_block) | (first + block_rows > info[0])

        @pl.when(counts & partial)
        def _():
            work(key_at, query_at, key_block, query_block, True)

        @pl.when(counts & jnp.logical_not(partial))
        def _():
            work(key_at, query_at, key_block, query_block, False)

        return carry

    lax.fori_loop(0, 4, one, 0)


def attend_kernel(first_chunk, chunks, streams, resumed, last, info, *refs):
    per_stream = 4 if resumed else 1
    given = [refs[per_stream * i : per_stream * (i + 1)] for i in range(streams)]
    refs = refs[per_stream * streams :]
    pairs, refs = refs[:chunks], refs[chunks:]
    per_output = 2 if last else 3
    results = [refs[per_output * i : per_output * (i + 1)] for i in range(streams)]
    scratch = refs[per_output * streams :]
    heads, head_size, tokens = given[0][0].shape
    rows = tokens // 2
    factor = head_size**-0.5 * LOG2E
    for stream in range(streams):
        queries = given[stream][0]
        top, total, sums = (
            scratch[3 * stream : 3 * stream + 3] if last else results[stream]
        )
        if resumed:
            for kept, start in zip((top, total, sums), given[stream][1:]):
                kept[...] = start[...]
        else:
            top[...] = jnp.full_like(top, MASKED)
            total[...] = jnp.zeros_like(total)
            sums[...] = jnp.zeros_like(sums)
        for chunk in range(chunks):
            pair = pairs[chunk]

            def work(
                key_at,
                query_at,
                key_block,
                query_block,
                masked,
                pair=pair,
                queries=queries,
                top=top,
                total=total,
                sums=sums,
            ):
                scores = [
                    score_block(
                        info,
                        pair[0, head, :, key_at],
                        queries[head, :, query_at],
                        key_block,
                        query_block,
                        masked,
                    )
                    for head in range(heads)
                ]
                olds = [top[head, :, query_at] for head in range(heads)]
                news = [
                    jnp.maximum(old, jnp.max(score, axis=0, keepdims=True) * factor)
                    for old, score in zip(olds, scores)
                ]
                weights = [jnp.exp2(score * factor - new) for score, new in zip(scores, news)]
                products = [
                    contract(pair[1, head, :, key_at], weights[head].astype(BF16), 1, 0)
                    for head in range(heads)
                ]
                for head in range(heads):
                    decay = jnp.exp2(olds[head] - news[head])
                    top[head, :, query_at] = news[head]
                    total[head, :, query_at] = total[head, :, query_at] * decay + jnp.sum(
                        weights[head], axis=0, keepdims=True
                    )
                    sums[head, :, query_at] = sums[head, :, query_at] * decay + products[head]

            for_blocks(info, stream, first_chunk + chunk, rows, work)
        if last:
            mixed, log_total = results[stream]
            for head in range(heads):
                mixed[head] = (sums[head] / total[head]).astype(BF16)
                log_total[head] = top[head] + jnp.log2(total[head])


def attend_back_kernel(first_chunk, chunks, resumed, info, *refs):
    per_stream = 5 if resumed else 4
    streams = (len(refs) - 2 * chunks - 2) // (per_stream + 1)
    given = [refs[per_stream * i : per_stream * (i + 1)] for i in range(streams)]
    refs = refs[per_stream * streams :]
    pairs, refs = refs[:chunks], refs[chunks:]
    query_sums, refs = refs[:streams], refs[streams:]
    grad_pairs, refs = refs[:chunks], refs[chunks:]
    inner, pair_sums = refs
    heads, head_size, tokens = given[0][0].shape
    rows = tokens // 2
    scale = head_size**-0.5
    factor = scale * LOG2E
    for stream in range(streams):
        _, grad_mixed, mixed = given[stream][:3]
        for head in range(heads):
            inner[stream, head] = jnp.sum(
                grad_mixed[head].astype(F32) * mixed[head].astype(F32), axis=0, keepdims=True
            )
        query_sums[stream][...] = (
            given[stream][4][...] if resumed else jnp.zeros_like(query_sums[stream])
        )
    for chunk in range(chunks):
        pair = pairs[chunk]
        pair_sums[...] = jnp.zeros_like(pair_sums)
        for stream in range(streams):
            queries, grad_mixed, _, log_total = given[stream][:4]

            def work(
                key_at,
                query_at,
                key_block,
                query_block,
                masked,
                pair=pair,
                stream=stream,
                queries=queries,
                grad_mixed=grad_mixed,
                log_total=log_total,
            ):
                every = range(heads)
                keys = [pair[0, head, :, key_at] for head in every]
                values = [pair[1, head, :, key_at] for head in every]
                query_parts = [queries[head, :, query_at] for head in every]
                grad_parts = [grad_mixed[head, :, query_at] for head in every]
                scores = [
                    score_block(info, keys[h], query_parts[h], key_block, query_block, masked)
                    for h in every
                ]
                grad_probs = [contract(values[h], grad_parts[h], 0, 0) for h in every]
                probs = [
                    jnp.exp2(scores[h] * factor - log_total[h, :, query_at]) for h in every
                ]
                grad_scores = [
                    (probs[h] * (grad_probs[h] - inner[stream, h, :, query_at])).astype(BF16)
                    for h in every
                ]
                low_probs = [member.astype(BF16) for member in probs]
                for_values = [contract(grad_parts[h], low_probs[h], 1, 1) for h in every]
                for_keys = [contract(query_parts[h], grad_scores[h], 1, 1) for h in every]
                for_queries = [contract(keys[h], grad_scores[h], 1, 0) for h in every]
                for h in every:
                    pair_sums[0, h, :, key_at] += for_keys[h]
                    pair_sums[1, h, :, key_at] += for_values[h]
                    query_sums[stream][h, :, query_at] += for_queries[h]

            for_blocks(info, stream, first_chunk + chunk, rows, work)
        grad_pairs[chunk][0] = (pair_sums[0] * scale).astype(grad_pairs[chunk].dtype)
        grad_pairs[chunk][1] = pair_sums[1].astype(grad_pairs[chunk].dtype)


SMALL_COST = pl.CostEstimate(flops=1 << 20, bytes_accessed=1 << 20, transcendentals=0)


def attend(info, queries, pairs, first_chunk, states, last):
    heads, head_size, tokens = queries[0].shape
    vmem = pl.BlockSpec(memory_space=pltpu.VMEM)
    state = [(heads, 1, tokens), (heads, 1, tokens), (heads, head_size, tokens)]
    operands = []
    for stream, member in enumerate(queries):
        operands.append(member)
        if states is not None:
            operands.extend(states[stream])
    operands.extend(pairs)
    if last:
        shapes = [
            jax.ShapeDtypeStruct((heads, head_size, tokens), BF16),
            jax.ShapeDtypeStruct((heads, 1, tokens), F32),
        ]
    else:
        shapes = [jax.ShapeDtypeStruct(shape, F32) for shape in state]
    results = pl.pallas_call(
        functools.partial(
            attend_kernel, first_chunk, len(pairs), len(queries), states is not None, last
        ),
        out_shape=tuple(shapes * len(queries)),
        in_specs=[pl.BlockSpec(memory_space=pltpu.SMEM)] + [vmem] * len(operands),
        out_specs=(vmem,) * (len(shapes) * len(queries)),
        scratch_shapes=[pltpu.VMEM(shape, F32) for shape in state] * len(queries) if last else [],
        compiler_params=pltpu.CompilerParams(vmem_limit_bytes=62 << 20),
        cost_estimate=SMALL_COST,
    )(info, *operands)
    return [results[len(shapes) * i : len(shapes) * (i + 1)] for i in range(len(queries))]


def attend_back(info, given, pairs, first_chunk, resumed, pair_type):
    heads, head_size, tokens = given[0][0].shape
    vmem = pl.BlockSpec(memory_space=pltpu.VMEM)
    operands = [member for stream in given for member in stream] + list(pairs)
    results = pl.pallas_call(
        functools.partial(attend_back_kernel, first_chunk, len(pairs), resumed),
        out_shape=tuple(
            jax.ShapeDtypeStruct((heads, head_size, tokens), F32) for _ in given
        )
        + tuple(jax.ShapeDtypeStruct(pair.shape, pair_type) for pair in pairs),
        in_specs=[pl.BlockSpec(memory_space=pltpu.SMEM)] + [vmem] * len(operands),
        out_specs=(vmem,) * (len(given) + len(pairs)),
        scratch_shapes=[
            pltpu.VMEM((len(given), heads, 1, tokens), F32),
            pltpu.VMEM((2, heads, head_size, tokens), F32),
        ],
        compiler_params=pltpu.CompilerParams(vmem_limit_bytes=62 << 20),
        cost_estimate=SMALL_COST,
    )(info, *operands)
    return results[: len(given)], results[len(given) :]


def near():
    tensor = lax.axis_index(TENSOR)
    return {TENSOR: tensor + 1 - 2 * lax.rem(tensor, 2)}


def far():
    tensor = lax.axis_index(TENSOR)
    return {TENSOR: tensor + 2 - 4 * lax.rem(tensor // 2, 2)}


def pair():
    seq = lax.axis_index(SEQ)
    return {SEQ: seq + 1 - 2 * lax.rem(seq, 2)}


def pair_far():
    seq = lax.axis_index(SEQ)
    return {SEQ: seq + 2 - 4 * lax.rem(seq // 2, 2)}


def across():
    return {CELL: 1 - lax.axis_index(CELL)}


class Wires:
    def __init__(self, r, partners):
        self.send, self.recv, self.local = r.send, r.recv, r.local
        self.started, self.open = 0, []
        barrier = pltpu.get_barrier_semaphore()
        for partner in partners:
            pl.semaphore_signal(barrier, inc=1, device_id=partner(), device_id_type=MESH)
        pl.semaphore_wait(barrier, len(partners))

    def start(self, source, target, partner):
        at = self.started
        copy = pltpu.make_async_remote_copy(
            src_ref=source,
            dst_ref=target,
            send_sem=self.send.at[at],
            recv_sem=self.recv.at[at],
            device_id=partner(),
            device_id_type=MESH,
        )
        copy.start()
        self.started += 1
        self.open.append(copy)
        return copy

    def sent(self, copy):
        copy.wait_send()
        self.open = [member for member in self.open if member is not copy]

    def finish(self):
        for copy in self.open:
            copy.wait_send()


class Local:
    def __init__(self, r, at, source, target):
        self.copy = pltpu.make_async_copy(source, target, r.local.at[at])
        self.copy.start()
        self.target, self.waited = target, False

    def get(self):
        if not self.waited:
            self.copy.wait()
            self.waited = True
        return self.target


def call_kernel(body, given, in_hbm, results, streamed, out_hbm, scratch, collective_id):
    out_hbm = dict(out_hbm, out=streamed)
    scratch = dict(
        scratch,
        **jax.tree.map(lambda member: pltpu.VMEM(member.shape, member.dtype), streamed),
        send=pltpu.SemaphoreType.DMA((COPIES,)),
        recv=pltpu.SemaphoreType.DMA((COPIES,)),
        local=pltpu.SemaphoreType.DMA((40,)),
    )
    vmem, hbm = pl.BlockSpec(memory_space=pltpu.VMEM), pl.BlockSpec(memory_space=pl.ANY)
    trees = (given, in_hbm, results, out_hbm, scratch)
    flat = [jax.tree.flatten(tree) for tree in trees]

    def kernel(*refs):
        found, at = {}, 0
        for leaves, tree in flat:
            found.update(jax.tree.unflatten(tree, refs[at : at + len(leaves)]))
            at += len(leaves)
        found.update(out=types.SimpleNamespace(**found[next(iter(dict(out=0)))]))
        body(types.SimpleNamespace(**found))

    outs = pl.pallas_call(
        kernel,
        out_shape=tuple(flat[2][0] + flat[3][0]),
        in_specs=[vmem] * len(flat[0][0]) + [hbm] * len(flat[1][0]),
        out_specs=tuple([vmem] * len(flat[2][0]) + [hbm] * len(flat[3][0])),
        scratch_shapes=flat[4][0],
        compiler_params=pltpu.CompilerParams(
            collective_id=collective_id, has_side_effects=True, vmem_limit_bytes=62 << 20
        ),
        cost_estimate=SMALL_COST,
    )(*flat[0][0], *flat[1][0])
    count = len(flat[2][0])
    found = jax.tree.unflatten(flat[2][1], outs[:count])
    others = jax.tree.unflatten(flat[3][1], outs[count:])
    found.update(others.pop(next(iter(dict(out=0)))))
    found.update(others)
    return found


class Flush:
    def __init__(self, r):
        self.r, self.copies = r, []

    def __call__(self, source, target):
        self.copies.append(Local(self.r, 12 + len(self.copies), source, target))

    def finish(self):
        for copy in self.copies:
            copy.get()


def shape_of(shape, dtype):
    return jax.ShapeDtypeStruct(shape, dtype)


def twice(value):
    return [value, value]


def by_rows(count, work, step=32):
    def one(index, carry):
        work(pl.ds(pl.multiple_of(index * step, step), step))
        return carry

    lax.fori_loop(0, count // step, one, 0)


def by_columns(width, work, step=128):
    def one(index, carry):
        work(pl.ds(pl.multiple_of(index * step, step), step))
        return carry

    lax.fori_loop(0, width // step, one, 0)
    if width % step:
        work(pl.ds(width // step * step, width % step))


def head_rows(source, rows):
    parts = [source[head, :, rows].astype(F32) for head in range(source.shape[0])]
    return jnp.concatenate(parts, axis=0).T


def put_heads(target, rows, values):
    head_size = target.shape[1]
    for head in range(target.shape[0]):
        target[head, :, rows] = values[head * head_size : (head + 1) * head_size].astype(
            target.dtype
        )


class Exchange:
    def __init__(self, wires, part, sent, got):
        self.wires, self.part, self.sent, self.got = wires, part, sent, got
        self.rows = part.shape[0]

    def give(self, values):
        self.sent[0] = values.astype(BF16)
        self.to_near = self.wires.start(self.sent.at[0], self.got.at[0], near)

    def keep(self, values):
        self.part[...] = values

    def part_rows(self, part):
        return pl.ds(part * (self.rows // 2), self.rows // 2)

    def join(self, cross):
        self.to_near.wait_recv()
        self.to_far = [None, None]
        for part in (0, 1):
            start = part * (self.rows // 2)

            def work(rows, start=start):
                at = pl.ds(start + rows.start, rows.size)
                self.sent[1, at] = (self.part[at] + self.got[0, at].astype(F32)).astype(BF16)

            by_rows(self.rows // 2, work)
            if cross:
                self.cross(part)

    def cross(self, part):
        rows = self.part_rows(part)
        self.to_far[part] = self.wires.start(
            self.sent.at[1, rows], self.got.at[1, rows], far
        )

    def wait(self, then=None):
        for part in (0, 1):
            self.to_far[part].wait_recv()
            if then is not None:
                then.cross(part)

    def total(self, rows):
        return self.sent[1, rows].astype(F32) + self.got[1, rows].astype(F32)


def add_into(target, left, right):
    def work(columns):
        target[:, columns] = (
            left[:, columns].astype(F32) + right[:, columns].astype(F32)
        ).astype(BF16)

    by_columns(target.shape[1], work)


def weight_grads(r):
    for j in range(3):
        total = None
        for grads, wide in zip(r.grads, r.wide_one):
            heads = [grads[j, head].astype(F32) for head in range(grads.shape[1])]
            product = mm(jnp.concatenate(heads, axis=0).astype(BF16), wide[...])
            total = product if total is None else total + product
        r.pieces[j // 2, j % 2] = total.astype(BF16)
    r.pieces[1, 1] = r.out_piece[...]


class Sum:
    def __init__(self, wires, whole, out, near_sum, got, got_far):
        self.wires, self.whole, self.out = wires, whole, out
        self.near_sum, self.got, self.got_far = near_sum, got, got_far
        self.bit = lax.rem(lax.axis_index(SEQ), 2)
        self.copy = None

    def wait(self):
        if self.copy is not None:
            self.copy.wait_recv()
            self.copy = None

    def one(self):
        self.copy = self.wires.start(self.whole.at[1 - self.bit], self.got, pair)

    def two(self):
        self.wait()
        add_into(self.near_sum, self.whole.at[self.bit], self.got)
        self.copy = self.wires.start(self.near_sum, self.got_far, pair_far)

    def three(self):
        self.wait()
        mine = self.out.at[self.bit]
        add_into(mine, self.near_sum, self.got_far)
        self.copy = self.wires.start(mine, mine, pair)

    def five(self, everything, rows):
        self.wait()
        target = everything.at[lax.axis_index(CELL), :, rows]
        self.copy = self.wires.start(self.out, target, across)
        return self.out, target


def sum_scratch(rows, width):
    return [pltpu.VMEM((rows, width), BF16)] * 3


def exchange_scratch(half, width, exchanges):
    return dict(
        part=pltpu.VMEM((2, half, width), F32),
        sent=pltpu.VMEM((2 * exchanges, 2, half, width), BF16),
        got=pltpu.VMEM((2 * exchanges, 2, half, width), BF16),
    )


def exchanges_of(r, wires, count):
    return [
        [Exchange(wires, r.part.at[i], r.sent.at[2 * k + i], r.got.at[2 * k + i]) for i in (0, 1)]
        for k in range(count)
    ]


def project(r, i, to_near, weight):
    half = r.wide_one[i].shape[0] // 2
    for part in (0, 1):
        at = pl.ds(part * half, half)
        if part and to_near is not None:
            to_near.wait_recv()
        wide = r.wide_one[i][at]
        for j in range(3):
            values = contract(wide, weight[j], 1, 1) + r.qkv_b[j : j + 1]
            target = r.queries[i] if j == 0 else r.pair[i].at[j - 1]
            put_heads(target, at, values.T)


def side_and_core():
    return lax.axis_index(SEQ) // 2, lax.rem(lax.axis_index(TENSOR), 2)


def core_columns(half, core):
    return pl.ds(pl.multiple_of(core * half, half), half)


def start_kernel(r):
    side, core = side_and_core()
    half = r.stream[0].shape[0]
    own = Local(r, 0, r.tokens.at[side], r.own_tokens)
    weight = Local(r, 1, r.qkv_w.at[0], r.own_qkv)
    wires = Wires(r, (near, pair, pair_far))
    flush = Flush(r)
    arriving = wires.start(
        r.tokens.at[1 - side, :, core_columns(half, core)], r.got_tokens, pair_far
    )

    def norm(i, part, values):
        r.rows[...] = values.astype(F32).T

        def work(rows):
            stream = r.rows[rows]
            normed, inverse = normalize(stream)
            if part == 0:
                r.stream[i][rows] = stream
                r.normed_one[i][rows] = normed.astype(BF16)
                r.inverse_one[i][rows] = inverse
            to = pl.ds(part * half + rows.start, rows.size)
            r.wide_one[i][to] = (normed * r.gain[...] + r.shift[...]).astype(BF16)

        by_rows(half, work)

    tokens = own.get()
    for part in (0, 1):
        norm(0, part, tokens[:, core_columns(half, lax.rem(core + part, 2))])
    project(r, 0, None, weight.get())
    paired = wires.start(r.pair[0], r.got_pair, pair)
    flush_next(r, flush, 0)
    arriving.wait_recv()
    norm(1, 0, r.got_tokens[...])
    wide = r.wide_one[1]
    to_near = wires.start(wide.at[pl.ds(0, half)], wide.at[pl.ds(half, half)], near)
    project(r, 1, to_near, weight.get())
    flush_next(r, flush, 1)
    paired.wait_recv()
    flush(r.got_pair, r.out.got_pair)
    flush.finish()
    wires.finish()


def flush_next(r, flush, i):
    for own, out in (
        (r.stream, r.out.stream),
        (r.wide_one, r.out.wide_one),
        (r.normed_one, r.out.normed_one),
        (r.inverse_one, r.out.inverse_one),
        (r.queries, r.out.queries),
        (r.pair, r.out.pair),
    ):
        flush(own[i], out[i])


def next_shapes(half, width, head_shape):
    return dict(
        stream=twice(shape_of((half, width), F32)),
        wide_one=twice(shape_of((2 * half, width), BF16)),
        normed_one=twice(shape_of((half, width), BF16)),
        inverse_one=twice(shape_of((half, 1), F32)),
        queries=twice(shape_of(head_shape, BF16)),
        pair=twice(shape_of((2,) + head_shape, BF16)),
        got_pair=shape_of((2,) + head_shape, BF16),
    )


def start_call(tokens, qkv_w, qkv_b, gain, shift, head_shape, collective_id):
    _, width, row_count = tokens.shape
    half = row_count // 2
    return call_kernel(
        start_kernel,
        dict(qkv_b=qkv_b, gain=gain, shift=shift),
        dict(tokens=tokens, qkv_w=qkv_w),
        {},
        next_shapes(half, width, head_shape),
        {},
        dict(
            own_tokens=pltpu.VMEM((width, row_count), BF16),
            got_tokens=pltpu.VMEM((width, half), BF16),
            own_qkv=pltpu.VMEM(qkv_w.shape[1:], BF16),
            rows=pltpu.VMEM((half, width), F32),
        ),
        collective_id,
    )


def forward_kernel(layer, last, r):
    side, core = side_and_core()
    half = r.base[0].shape[0]
    halves = (pl.ds(0, half), pl.ds(half, half))
    out_w = Local(r, 0, r.out_w.at[layer], r.own_out)
    up_w = Local(r, 1, r.up_w.at[layer], r.own_up)
    down_w = Local(r, 2, r.down_w.at[layer], r.own_down)
    if not last:
        qkv_w = Local(r, 3, r.qkv_w.at[layer + 1], r.own_qkv)
    wires = Wires(r, (near, far) + (() if last else (pair, pair_far)))
    flush = Flush(r)
    first, second = exchanges_of(r, wires, 2)
    to_near = {}

    def row(index):
        return r.vectors[index : index + 1]

    def norm(i, exchange, base, at, kept, normed_to, inverse_to, wide):
        def work(rows):
            stream = base[rows] + exchange.total(rows) + row(at)
            normed, inverse = normalize(stream)
            kept[rows] = stream
            normed_to[rows] = normed.astype(BF16)
            inverse_to[rows] = inverse
            wide[rows] = (normed * row(at + 1) + row(at + 2)).astype(BF16)

        by_rows(half, work)
        to_near[i] = wires.start(wide.at[halves[0]], wide.at[halves[1]], near)

    def attended(i):
        for part in (1, 0):
            values = mm(head_rows(r.mixed[i], halves[part]).astype(BF16), out_w.get()[...])
            (first[i].give if part else first[i].keep)(values)

    def mid_norm(i):
        norm(
            i, first[i], r.base[i], 0, r.mid.at[i], r.normed_two[i], r.inverse_two[i], r.wide_two[i]
        )

    def feed(i):
        for part in (0, 1):
            if part:
                to_near[i].wait_recv()
            r.wide_part[...] = mm(r.wide_two[i][halves[part]], up_w.get()[...])

            def work(rows, part=part):
                hidden, slope = gelu_both(r.wide_part[rows] + r.up_b[...])
                to = pl.ds(part * half + rows.start, rows.size)
                r.hidden[i][to] = hidden
                r.slope[i][to] = slope

            by_rows(half, work)
        for part in (1, 0):
            values = mm(r.hidden[i][halves[part]], down_w.get()[...])
            (second[i].give if part else second[i].keep)(values)
        for own, out in (
            (r.wide_two, r.out.wide_two),
            (r.normed_two, r.out.normed_two),
            (r.inverse_two, r.out.inverse_two),
            (r.hidden, r.out.hidden),
            (r.slope, r.out.slope),
        ):
            flush(own[i], out[i])

    def leave(i):
        if last:

            def work(rows):
                r.part[i, rows] = r.mid[i, rows] + second[i].total(rows) + row(3)

            by_rows(half, work)
            r.low[i][...] = r.part[i].T.astype(BF16)
        else:
            norm(
                i, second[i], r.mid.at[i], 3, r.stream[i], r.normed_one[i], r.inverse_one[i],
                r.wide_one[i],
            )
            project(r, i, to_near[i], qkv_w.get())
            flush_next(r, flush, i)

    for i in (0, 1):
        attended(i)
    first[0].join(True)
    first[1].join(False)
    first[0].wait(first[1])
    if not last:
        given = wires.start(
            r.out_grad.at[1 - side, :, core_columns(half, core)], r.got_grad, pair_far
        )
    mid_norm(0)
    feed(0)
    second[0].join(False)
    first[1].wait(second[0])
    mid_norm(1)
    feed(1)
    second[1].join(False)
    second[0].wait(second[1])
    leave(0)
    if not last:
        paired = wires.start(r.pair[0], r.got_pair, pair)
    second[1].wait()
    leave(1)
    if not last:
        given.wait_recv()
        paired.wait_recv()
        flush(r.got_pair, r.out.got_pair)
    flush.finish()
    wires.finish()


def forward_call(given, in_hbm, layer, last, collective_id):
    half, width = given["base"][0].shape
    hidden_width = in_hbm["up_w"].shape[2]
    head_shape = given["mixed"][0].shape
    wide_hidden = shape_of((2 * half, hidden_width), BF16)
    results = {}
    streamed = dict(
        wide_two=twice(shape_of((2 * half, width), BF16)),
        normed_two=twice(shape_of((half, width), BF16)),
        inverse_two=twice(shape_of((half, 1), F32)),
        hidden=twice(wide_hidden),
        slope=twice(wide_hidden),
    )
    out_hbm = {}
    scratch = dict(
        exchange_scratch(half, width, 2),
        mid=pltpu.VMEM((2, half, width), F32),
        wide_part=pltpu.VMEM((half, hidden_width), F32),
        own_out=pltpu.VMEM(in_hbm["out_w"].shape[1:], BF16),
        own_up=pltpu.VMEM(in_hbm["up_w"].shape[1:], BF16),
        own_down=pltpu.VMEM(in_hbm["down_w"].shape[1:], BF16),
    )
    if last:
        results.update(low=twice(shape_of((width, half), BF16)))
    else:
        streamed.update(next_shapes(half, width, head_shape))
        out_hbm.update(got_grad=shape_of((width, half), BF16))
        scratch.update(own_qkv=pltpu.VMEM(in_hbm["qkv_w"].shape[1:], BF16))
    return call_kernel(
        functools.partial(forward_kernel, layer, last),
        given,
        in_hbm,
        results,
        streamed,
        out_hbm,
        scratch,
        collective_id,
    )


def backward_kernel(attention, feed, riding, r):
    begin, end = attention is None, feed is None
    side, core = side_and_core()
    half = r.grad_out[0].shape[0]
    halves = (pl.ds(0, half), pl.ds(half, half))
    if begin:
        own = Local(r, 0, r.out_grad.at[side], r.own_grad)
    else:
        qkv_w = Local(r, 1, r.qkv_w.at[attention], r.own_qkv)
    if not end:
        down_w = Local(r, 2, r.down_w.at[feed], r.own_down)
        up_w = Local(r, 3, r.up_w.at[feed], r.own_up)
        out_w = Local(r, 4, r.out_w.at[feed], r.own_out)
    partners = [near, far]
    if begin or riding:
        partners.append(pair_far)
    if riding:
        partners.append(pair)
    if riding == 2:
        partners.append(across)
    wires = Wires(r, partners)
    exchanges = exchanges_of(r, wires, int(not begin) + int(not end))
    to_near = {}
    flush = Flush(r)
    r.sums[...] = jnp.zeros_like(r.sums)
    cell = lax.axis_index(CELL)
    if riding:
        rider = Sum(wires, r.whole, r.summed if riding == 2 else None, r.near_sum, r.got_sum, r.got_far)

    def note(index, values):
        r.sums[index : index + 1, : values.shape[1]] += jnp.sum(values, axis=0, keepdims=True)

    def gather(i, exchange):
        scale = HEAD**-0.5
        for part in (1, 0):
            at = halves[part]
            values = None
            for j in range(3):
                target = r.grads[i].at[j]
                for head in range(target.shape[0]):
                    if j == 0:
                        found = r.query_sum[i][head, :, at] * scale
                    else:
                        found = r.pair_sum[i][j - 1, head, :, at] + r.pair_got[i][
                            j - 1, head, :, at
                        ].astype(F32)
                    target[head, :, at] = found.astype(BF16)
                rows = head_rows(target, at)
                if j != 1:
                    start = j // 2 * (r.sums.shape[1] // 256 * 128)
                    r.sums[7:8, start : start + rows.shape[1]] += jnp.sum(
                        rows, axis=0, keepdims=True
                    )
                product = mm(rows.astype(BF16), qkv_w.get()[j])
                values = product if values is None else values + product
            (exchange.give if part else exchange.keep)(values)
        flush(r.grads[i], r.out.grads[i])

    def norm(i, exchange, base, normed_of, inverse_of, gain, at, wide):
        def work(rows):
            incoming = exchange.total(rows)
            normed = normed_of[rows].astype(F32)
            grad = base[rows] + norm_back(
                incoming, normed, inverse_of[rows], r.gains[gain : gain + 1]
            )
            r.grad_out[i][rows] = grad
            note(at, incoming * normed)
            note(at + 1, incoming)
            note(at + 2, grad)
            if wide is not None:
                wide[rows] = grad.astype(BF16)

        by_rows(half, work)
        if wide is not None:
            to_near[i] = wires.start(wide.at[halves[0]], wide.at[halves[1]], near)

    def first_norm(i):
        norm(
            i, exchanges[0][i], r.grad[i], r.normed_one[i], r.inverse_one[i], 0, 0,
            None if end else r.wide[i],
        )
        if end:
            r.low[i][...] = r.grad_out[i][...].T.astype(BF16)

    def second_norm(i):
        norm(
            i, exchanges[-1][i], r.grad_out[i], r.normed_two[i], r.inverse_two[i], 1, 3,
            r.wide_mid[i],
        )
        for part in (0, 1):
            if part:
                to_near[i].wait_recv()
            values = contract(out_w.get()[...], r.wide_mid[i][halves[part]], 1, 1)
            put_heads(r.mixed_grad[i], halves[part], values)
        for own, out in (
            (r.wide_mid, r.out.wide_mid),
            (r.mixed_grad, r.out.mixed_grad),
            (r.grad_out, r.out.grad_out),
        ):
            flush(own[i], out[i])

    def first_rows(i):
        if i == 0:
            given = own.get()
            for part in (0, 1):
                values = given[:, core_columns(half, lax.rem(core + part, 2))].astype(F32).T
                if part == 0:
                    r.grad_out[0][...] = values
                r.wide[0][halves[part]] = values.astype(BF16)
        else:
            r.grad_out[1][...] = r.got_grad[...].astype(F32).T
            wide = r.wide[1]
            wide[halves[0]] = r.grad_out[1][...].astype(BF16)
            to_near[1] = wires.start(wide.at[halves[0]], wide.at[halves[1]], near)
        by_rows(half, lambda rows: note(2, r.grad_out[i][rows]))

    def slide(i, exchange):
        wide = r.wide[i]
        for part in (0, 1):
            if part and i in to_near:
                to_near[i].wait_recv()
            r.wide_part[...] = contract(wide[halves[part]], down_w.get()[...], 1, 1)

            def work(rows, part=part):
                to = pl.ds(part * half + rows.start, rows.size)
                hidden = r.wide_part[rows].astype(BF16).astype(F32)
                pre = (hidden * r.slope[i][to].astype(F32)).astype(BF16)
                r.pre[i][to] = pre
                note(6, pre.astype(F32))

            by_rows(half, work)
        for part in (1, 0):
            values = contract(r.pre[i][halves[part]], up_w.get()[...], 1, 1)
            (exchange.give if part else exchange.keep)(values)
        flush(r.pre[i], r.out.pre[i])
        flush(r.wide[i], r.out.wide[i])

    def ride(step):
        if riding == 1 and step == 0:
            rider.one()
            r.late = wires.start(r.near_late, r.far_late, pair_far)
        elif riding == 1 and step == 1:
            rider.two()
        elif riding == 1 and step == 5:
            rider.wait()
            r.late.wait_recv()
        elif riding == 2 and step == 0:
            rider.one()
        elif riding == 2 and step == 1:
            rider.two()
            weight_grads(r)
            r.crossing = wires.start(r.pieces.at[1 - cell], r.got_pieces, across)
        elif riding == 2 and step == 3:
            rider.three()
            r.crossing.wait_recv()
            for k in (0, 1):
                add_into(r.whole_next.at[k], r.pieces.at[cell, k], r.got_pieces.at[k])
        elif riding == 2 and step == 5:
            rider.wait()

    ride(0)
    if begin:
        (after,) = exchanges
        placed = place_cells(r, wires, r.block, r.block_low)
        for i in (0, 1):
            first_rows(i)
            slide(i, after[i])
            after[i].join(i == 0)
        after[0].wait(after[1])
        second_norm(0)
        placed.forward()
        after[1].wait()
        second_norm(1)
        placed.finish()
    else:
        before, after = exchanges[0], exchanges[-1]
        a, b = (1, 0) if end else (0, 1)
        gather(a, before[a])
        gather(b, before[b])
        before[a].join(True)
        before[b].join(False)
        ride(1)
        before[a].wait(before[b])
        first_norm(a)
        if end:
            before[b].wait()
            first_norm(b)
        else:
            slide(a, after[a])
            after[a].join(False)
            before[b].wait(after[a])
            first_norm(b)
            slide(b, after[b])
            after[b].join(False)
            after[a].wait(after[b])
            ride(3)
            second_norm(a)
            after[b].wait()
            second_norm(b)
    ride(5)
    flush.finish()
    wires.finish()


class place_cells:
    def __init__(self, r, wires, target, low):
        side, core = side_and_core()
        half = low[0].shape[1]
        self.wires = wires
        columns = core_columns(half, core)
        self.own = target.at[side, :, columns]
        self.arrived = target.at[1 - side, :, columns]
        self.local = Local(r, 11, low[0], self.own)
        self.to_far = wires.start(low[1], self.own, pair_far)
        self.to_near = wires.start(low[0], self.own, near)

    def forward(self):
        self.to_far.wait_recv()
        self.second = self.wires.start(self.arrived, self.arrived, near)

    def finish(self):
        self.local.get()
        self.to_near.wait_recv()
        self.second.wait_recv()


def backward_call(given, in_hbm, attention, feed, riding, collective_id):
    begin, end = attention is None, feed is None
    some = given["block_low"][0] if begin else given["grad"][0]
    width = given["gains"].shape[1]
    half = some.shape[1] if begin else some.shape[0]
    results = dict(sums=shape_of((8, width), F32))
    streamed = dict()
    grad_out = twice(shape_of((half, width), F32))
    wide = twice(shape_of((2 * half, width), BF16))
    out_hbm = {}
    scratch = exchange_scratch(half, width, int(not begin) + int(not end))
    if begin:
        out_hbm.update(block=shape_of((2, width, 2 * half), BF16))
        scratch.update(own_grad=pltpu.VMEM((width, 2 * half), BF16))
    else:
        head_shape = given["query_sum"][0].shape
        streamed.update(grads=twice(shape_of((3,) + head_shape, BF16)))
        scratch.update(own_qkv=pltpu.VMEM(in_hbm["qkv_w"].shape[1:], BF16))
    if end:
        results.update(low=twice(shape_of((width, half), BF16)), grad_out=grad_out)
    else:
        hidden_width = in_hbm["up_w"].shape[2]
        head_count = in_hbm["out_w"].shape[1] // HEAD
        streamed.update(
            grad_out=grad_out,
            wide=wide,
            wide_mid=wide,
            pre=twice(shape_of((2 * half, hidden_width), BF16)),
            mixed_grad=twice(shape_of((head_count, HEAD, 2 * half), BF16)),
        )
        scratch.update(
            wide_part=pltpu.VMEM((half, hidden_width), F32),
            own_out=pltpu.VMEM(in_hbm["out_w"].shape[1:], BF16),
            own_up=pltpu.VMEM(in_hbm["up_w"].shape[1:], BF16),
            own_down=pltpu.VMEM(in_hbm["down_w"].shape[1:], BF16),
        )
    if riding:
        whole = given["whole"]
        one = pltpu.VMEM(whole.shape[1:], BF16)
        if riding == 2:
            piece = given["out_piece"].shape
            results.update(
                summed=shape_of(whole.shape, BF16),
                whole_next=shape_of((2,) + piece, BF16),
            )
            scratch.update(
                near_sum=one,
                got_far=one,
                pieces=pltpu.VMEM((2, 2) + piece, BF16),
                got_pieces=pltpu.VMEM((2,) + piece, BF16),
            )
        else:
            part = shape_of(whole.shape[1:], BF16)
            results.update(near_sum=part, got_far=part)
            results.update(far_late=shape_of(given["near_late"].shape, BF16))
        scratch.update(got_sum=one)
    return call_kernel(
        functools.partial(backward_kernel, attention, feed, riding),
        given,
        in_hbm,
        results,
        streamed,
        out_hbm,
        scratch,
        collective_id,
    )


def closing_kernel(sums_too, r):
    wires = Wires(r, [near, pair, pair_far] + ([across] if sums_too else []))
    cell = lax.axis_index(CELL)
    kernels = r.vectors.shape[0]
    r.total[...] = r.vectors[...]

    def vectors(at, partner, own_rows=8):
        copy = wires.start(r.total, r.around.at[at], partner)

        def add():
            copy.wait_recv()
            wires.sent(copy)
            for kernel in range(kernels):
                r.total[kernel, :own_rows] += r.around[at, kernel, :own_rows]

        return add

    if sums_too:
        span = r.sum_feed[0].shape[1]
        spans = [pl.ds(0, span), pl.ds(span, r.all_feed.shape[2] - span)]
        whole = pl.ds(0, r.all_last.shape[2])
        feed = [
            Sum(wires, r.whole_feed[k], r.sum_feed[k], *r.riding_feed[k]) for k in (0, 1)
        ]
        last = Sum(wires, r.whole_last, r.sum_last, *r.riding_last)
        late = Sum(wires, None, r.sum_late, r.near_late, None, r.far_late)
        prior = Sum(wires, None, r.sum_prior, r.near_prior, None, r.far_prior)
        local = []

        def fold(target, kept, got, rows):
            def work(columns):
                target[:, :, columns] = (
                    kept[:, rows, columns].astype(F32) + got[:, rows, columns].astype(F32)
                ).astype(BF16)

            by_columns(kept.shape[2], work)

        def five(member, everything, rows):
            own, target = member.five(everything, rows)
            local.append(Local(r, len(local), own, target))

        fold(r.whole_feed[0], r.kept_feed, r.got_feed, spans[0])
        feed[0].one()
        late.three()
        weight_grads(r)
        arriving = wires.start(r.pieces.at[1 - cell], r.got_last, across)
        local.append(Local(r, 0, r.early, r.all_late.at[cell, :, spans[0]]))
        local.append(Local(r, 1, r.got_early, r.all_late.at[1 - cell, :, spans[0]]))
        add = vectors(0, near, 6)
        feed[0].two()
        arriving.wait_recv()
        for k in (0, 1):
            add_into(r.whole_last.at[k], r.pieces.at[cell, k], r.got_last.at[k])
        last.one()
        prior.three()
        five(late, r.all_late, spans[1])
        fold(r.whole_feed[1], r.kept_feed, r.got_feed, spans[1])
        feed[0].three()
        five(prior, r.all_prior, whole)
        last.two()
        feed[1].one()
        last.three()
        feed[1].two()
        five(feed[0], r.all_feed, spans[0])
        add()
        add = vectors(1, across)
        five(last, r.all_last, whole)
        feed[1].three()
        add()
        add = vectors(2, pair)
        five(feed[1], r.all_feed, spans[1])
        add()
        placed = place_cells(r, wires, r.tokens_grad, r.low)
        add = vectors(3, pair_far)
        placed.forward()
        add()
        for member in feed + [late, prior, last]:
            member.wait()
        for copy in local:
            copy.get()
    else:
        placed = place_cells(r, wires, r.tokens_grad, r.low)
        vectors(0, near, 6)()
        placed.forward()
        vectors(1, pair)()
        vectors(2, pair_far)()
    r.totals[...] = r.total[...]
    placed.finish()
    wires.finish()


def closing_call(given, in_hbm, sums_too, collective_id):
    width, half = given["low"][0].shape
    vectors = given["vectors"].shape
    results = dict(totals=shape_of(vectors, F32))
    out_hbm = dict(tokens_grad=shape_of((2, width, 2 * half), BF16))
    scratch = dict(total=pltpu.VMEM(vectors, F32), around=pltpu.VMEM((4,) + vectors, F32))
    if sums_too:
        feed, last = given["kept_feed"].shape, (2,) + given["out_piece"].shape
        late = (2,) + given["near_late"].shape
        early = (feed[0], feed[1] - late[1]) + feed[2:]
        spans = [pltpu.VMEM(early, BF16), pltpu.VMEM(late, BF16)]
        out_hbm.update(
            all_feed=shape_of((2,) + feed, BF16),
            all_late=shape_of((2,) + feed, BF16),
            all_last=shape_of((2,) + last, BF16),
            all_prior=shape_of((2,) + last, BF16),
        )
        scratch.update(
            whole_feed=spans,
            sum_feed=spans,
            riding_feed=[sum_scratch(*early[1:]), sum_scratch(*late[1:])],
            sum_late=spans[1],
            whole_last=pltpu.VMEM(last, BF16),
            sum_last=pltpu.VMEM(last, BF16),
            got_last=pltpu.VMEM(last, BF16),
            pieces=pltpu.VMEM((2,) + last, BF16),
            riding_last=sum_scratch(*last[1:]),
            sum_prior=pltpu.VMEM(last, BF16),
        )
    return call_kernel(
        functools.partial(closing_kernel, sums_too),
        given,
        in_hbm,
        results,
        {},
        out_hbm,
        scratch,
        collective_id,
    )


class Line:
    def __init__(self):
        self.last = None

    def run(self, step, *operands):
        if self.last is not None:
            operands, _ = lax.optimization_barrier((operands, self.last))
        results = step(*operands)
        self.last = jax.tree.leaves(results)[0]
        return types.SimpleNamespace(**results) if isinstance(results, dict) else results


def add_low(kept, got):
    return (kept.astype(F32) + got.astype(F32)).astype(BF16)


def pick(cell, low, high):
    first, second = jnp.stack(low), jnp.stack(high)
    return jnp.where(cell == 0, first, second), jnp.where(cell == 0, second, first)


def two_sum(product, left, right):
    return (product(left[0], right[0]) + product(left[1], right[1])).astype(BF16)


def feed_sums(hidden, grad_down, wide_two, pre_grad):
    up, down = two_sum(mm_left, wide_two, pre_grad), two_sum(mm_left, hidden, grad_down)
    return [part for whole in (up, down) for part in jnp.split(whole, 2, axis=0)]


def attention_sums(wide_mid, mixed, wide_one, grads):
    def product(left, right):
        return mm(left.reshape(left.shape[0] * left.shape[1], left.shape[2]), right)

    return [two_sum(product, [grad[j] for grad in grads], wide_one) for j in range(3)] + [
        two_sum(product, mixed, wide_mid)
    ]


def shards(
    tokens,
    out_grad,
    group_order,
    lengths,
    qkv_weight,
    qv_bias,
    out_weight,
    out_bias,
    up_weight,
    up_bias,
    down_weight,
    down_bias,
    norm_gain,
    norm_shift,
):
    layer_count = qkv_weight.shape[0]
    local_width = qkv_weight.shape[3]
    seq_index = lax.axis_index(SEQ)
    cell = lax.axis_index(CELL)
    core = lax.axis_index(TENSOR) % 2
    side = seq_index // 2
    paired_cells = lax.axis_size(CELL) == 2
    gains, shifts = norm_gain.astype(F32), norm_shift.astype(F32)
    row_count = tokens.shape[1]
    head_shape = (local_width // HEAD, HEAD, row_count)
    tokens, out_grad = jnp.swapaxes(tokens, 1, 2), jnp.swapaxes(out_grad, 1, 2)
    qkv_weight = jnp.swapaxes(qkv_weight, 2, 3)
    biases = qv_bias.astype(F32)
    qkv_bias = jnp.stack([biases[:, 0], jnp.zeros_like(biases[:, 0]), biases[:, 1]], axis=1)
    line = Line()

    order = jnp.where(side == 0, group_order[0], group_order[1])
    length = jnp.where(side == 0, lengths[0], lengths[1])
    offsets = jnp.array([0, 2, 0, 2, 1, 3], jnp.int32)
    slots = 2 * (seq_index ^ offsets)[:, None] + (core + jnp.arange(2)[None]) % 2
    wanted = slots.reshape(-1, 1) == jnp.arange(order.shape[0])[None]
    blocks = jnp.sum(jnp.where(wanted, order[None], 0), axis=1)
    info = jnp.concatenate([length[None], blocks]).astype(jnp.int32)

    weights = dict(out_w=out_weight, up_w=up_weight, down_w=down_weight)
    now = line.run(
        lambda *given: start_call(*given, head_shape, 0),
        tokens,
        qkv_weight,
        qkv_bias[0],
        gains[0, :1],
        shifts[0, :1],
    )
    saved = []
    for layer in range(layer_count):
        last = layer == layer_count - 1
        got_pair = swap(now.pair[1], SEQ, 1)
        states = line.run(
            lambda queries, *pairs: attend(info, queries, pairs, 0, None, False),
            now.queries,
            *now.pair,
            now.got_pair,
        )
        mixed = line.run(
            lambda queries, states, pair: attend(info, queries, [pair], 3, states, True),
            now.queries,
            states,
            got_pair,
        )
        rows = [out_bias[layer], gains[layer, 1], shifts[layer, 1], down_bias[layer]]
        given = dict(
            base=now.stream,
            mixed=[mixed[0][0], mixed[1][0]],
            up_b=up_bias[layer].astype(F32)[None],
        )
        in_hbm = dict(weights)
        if not last:
            rows += [gains[layer + 1, 0], shifts[layer + 1, 0]]
            in_hbm.update(qkv_w=qkv_weight, out_grad=out_grad)
            given.update(qkv_b=qkv_bias[layer + 1])
        given.update(vectors=jnp.stack([row.astype(F32) for row in rows]))
        found = line.run(
            lambda given, in_hbm, layer=layer, last=last: forward_call(
                given, in_hbm, layer, last, 1 + layer
            ),
            given,
            in_hbm,
        )
        saved.append(
            types.SimpleNamespace(
                queries=now.queries,
                near_pairs=now.pair,
                far_pairs=[now.got_pair, got_pair],
                wide_one=now.wide_one,
                normed_one=now.normed_one,
                inverse_one=now.inverse_one,
                mixed=[mixed[0][0], mixed[1][0]],
                log_total=[mixed[0][1], mixed[1][1]],
                wide_two=found.wide_two,
                normed_two=found.normed_two,
                inverse_two=found.inverse_two,
                hidden=found.hidden,
                slope=found.slope,
            )
        )
        if not last:
            got_grad = found.got_grad
            now = found

    identity = layer_count + 1
    block_low = found.low
    vectors = []
    halves = {}
    for layer in reversed(range(layer_count + 1)):
        begin, end = layer == layer_count, layer == 0
        given, in_hbm = dict(), dict()
        gain_rows = [gains[0, 0], gains[0, 0]]
        riding = 0
        if begin:
            given.update(got_grad=got_grad, block_low=block_low)
            in_hbm.update(out_grad=out_grad)
        else:
            above = saved[layer]
            given.update(
                grad=found.grad_out,
                query_sum=query_sums,
                pair_sum=near_sums,
                pair_got=far_got,
                normed_one=above.normed_one,
                inverse_one=above.inverse_one,
            )
            in_hbm.update(qkv_w=qkv_weight)
            gain_rows[0] = gains[layer, 0]
            if paired_cells:
                riding = 1 if end else 2
                if end:
                    near_late = line.run(add_low, kept_late, got_late)
                    given.update(near_late=near_late, whole=next_whole)
                else:
                    given.update(
                        whole=line.run(add_low, *pending),
                        wide_one=above.wide_one,
                        out_piece=out_piece,
                    )
        if not end:
            below = saved[layer - 1]
            given.update(
                slope=below.slope, normed_two=below.normed_two, inverse_two=below.inverse_two
            )
            in_hbm.update(weights)
            gain_rows[1] = gains[layer - 1, 1]
        given.update(gains=jnp.stack(gain_rows))
        found = line.run(
            lambda given, in_hbm, layer=layer, riding=riding: backward_call(
                given,
                in_hbm,
                layer if layer < layer_count else None,
                layer - 1 if layer > 0 else None,
                riding,
                identity + layer,
            ),
            given,
            in_hbm,
        )
        vectors.append(found.sums)
        if begin:
            block_out = found.block
        else:
            if riding == 2:
                early = found.summed
                got_early = swap(early, CELL, 1)
                next_whole = found.whole_next
                late = line.run(add_low, *late)
                bit = seq_index % 2
                kept_late = jnp.where(bit == 0, late[0], late[1])
                got_late = swap(jnp.where(bit == 0, late[1], late[0]), SEQ, 1)
            elif not paired_cells:
                halves[layer, 1] = line.run(
                    attention_sums, wide_mid, above.mixed, above.wide_one, found.grads
                )
        if end:
            break
        wide_mid = found.wide_mid
        streams = [
            list(members)
            for members in zip(below.queries, found.mixed_grad, below.mixed, below.log_total)
        ]

        def feed_totals():
            return line.run(feed_sums, below.hidden, found.wide, below.wide_two, found.pre)

        if paired_cells:
            sums = feed_totals()
            if begin:
                cut = sums[0].shape[0] // 32 * 16 + 16
                spans = [slice(0, cut), slice(cut, None)]

                def pick_spans(low, high):
                    return [
                        pick(cell, [m[span] for m in low], [m[span] for m in high])
                        for span in spans
                    ]

                pending, late = (
                    [kept, swap(sent, CELL, 1)]
                    for kept, sent in line.run(pick_spans, sums[:2], sums[2:])
                )
            else:
                kept_feed, sent_feed = line.run(
                    functools.partial(pick, cell), sums[:2], sums[2:]
                )
                got_feed = swap(sent_feed, CELL, 1)
            out_piece = line.run(
                lambda mixed, wide: two_sum(
                    lambda left, right: mm(left.reshape(local_width, row_count), right), mixed, wide
                ),
                below.mixed,
                wide_mid,
            )
        else:
            halves[layer - 1, 0] = feed_totals()
        query_sums, far_sums = line.run(
            lambda given, pairs: attend_back(info, given, pairs, 2, False, BF16),
            streams,
            below.far_pairs,
        )
        far_got = [swap(far_sum, SEQ, 1) for far_sum in far_sums]
        streams = [members + [start] for members, start in zip(streams, query_sums)]
        query_sums, near_sums = line.run(
            lambda given, pairs: attend_back(info, given, pairs, 0, True, F32),
            streams,
            below.near_pairs,
        )

    vectors = jnp.stack(vectors)
    if not paired_cells:
        vectors = lax.psum(vectors, CELL)
    given, in_hbm = dict(low=found.low, vectors=vectors), dict()
    if paired_cells:
        given.update(
            kept_feed=kept_feed,
            got_feed=got_feed,
            grads=found.grads,
            wide_one=above.wide_one,
            out_piece=out_piece,
            near_late=near_late,
            far_late=found.far_late,
            near_prior=found.near_sum,
            far_prior=found.got_far,
        )
        in_hbm.update(early=early, got_early=got_early)
    closing = line.run(
        lambda given, in_hbm: closing_call(given, in_hbm, paired_cells, identity + layer_count + 1),
        given,
        in_hbm,
    )
    if paired_cells:
        feeds = [closing.all_feed, closing.all_late]
        attentions = [closing.all_last, closing.all_prior]
    else:

        def whole(part):
            found = []
            for layer in range(layer_count):
                total = lax.psum(jnp.stack(halves[layer, part]).astype(F32), (CELL, SEQ))
                found.append(total.reshape((2, 2) + total.shape[1:]))
            return found

        feeds, attentions = whole(0), whole(1)

    def final(pieces):
        return jnp.stack([piece.astype(F32) for piece in pieces])

    def quarters(member):
        return member.reshape((4,) + member.shape[2:])

    def square(member):
        return member.reshape(member.shape[0] * member.shape[1], member.shape[2])

    totals = closing.totals
    attention_rows = [totals[layer_count - layer] for layer in range(layer_count)]
    feed_rows = [totals[layer_count - 1 - layer] for layer in range(layer_count)]

    def rows_of(members, *indices):
        return jnp.stack([member[index] for member in members for index in indices])

    gain_grad = jnp.stack([rows_of(attention_rows, 0), rows_of(feed_rows, 3)], axis=1)
    shift_grad = jnp.stack([rows_of(attention_rows, 1), rows_of(feed_rows, 4)], axis=1)
    second = totals.shape[2] // 256 * 128
    qv_rows = rows_of(attention_rows, 7)
    qv_grad = jnp.stack(
        [qv_rows[:, :local_width], qv_rows[:, second : second + local_width]], axis=1
    )
    return (
        jnp.swapaxes(block_out, 1, 2),
        jnp.swapaxes(closing.tokens_grad, 1, 2),
        jnp.swapaxes(
            final([quarters(member)[:3] for member in attentions]), 2, 3
        ),
        qv_grad,
        final([quarters(member)[3] for member in attentions]),
        rows_of(feed_rows, 5),
        final([square(member[0]) for member in feeds]),
        rows_of(feed_rows, 6),
        final([square(member[1]) for member in feeds]),
        rows_of(feed_rows, 2),
        gain_grad,
        shift_grad,
    )


def solution(mesh):
    shared, by_tensor = P(), P(None, TENSOR)
    rows, last = P(CELL, SEQ, None), P(None, None, TENSOR)
    middle = P(None, TENSOR, None)
    weights = (P(None, None, None, TENSOR), last, middle, shared, last, by_tensor, middle)
    norms = (shared, shared, shared)
    return jax.shard_map(
        shards,
        mesh=mesh,
        in_specs=(rows, rows, P(CELL, None), P(CELL)) + weights + norms,
        out_specs=(rows, rows) + weights + norms,
        check_vma=False,
    )
```

```python
import functools
import types

import jax
import jax.numpy as jnp
from jax import lax
from jax.experimental import pallas as pl
from jax.experimental.pallas import tpu as pltpu
from jax.sharding import PartitionSpec as P

HEAD = 56
EPSILON = 1e-05
MASKED = -1e30
ROOT_TWO_PI = 0.7978845608028654
CUBIC = 0.044715
LOG2E = 1.4426950408889634
F32 = jnp.float32
BF16 = jnp.bfloat16
MESH = pl.DeviceIdType.MESH
CELL, SEQ, TENSOR = "cell", "seq", "tensor"
COPIES = 28


def swap(values, axis, bit):
    size = lax.axis_size(axis)
    return lax.ppermute(values, axis, [(i, i ^ bit) for i in range(size)])


def normalize(values):
    centred = values - jnp.mean(values, axis=-1, keepdims=True)
    spread = jnp.mean(centred * centred, axis=-1, keepdims=True)
    inverse = lax.rsqrt(spread + EPSILON)
    return (centred * inverse, inverse)


def norm_back(incoming, normed, inverse, gain_row):
    scaled = incoming * gain_row
    first_mean = jnp.mean(scaled, axis=-1, keepdims=True)
    second_mean = jnp.mean(scaled * normed, axis=-1, keepdims=True)
    return inverse * (scaled - first_mean - normed * second_mean)


def gelu_both(values):
    inner = jnp.tanh(ROOT_TWO_PI * (values + CUBIC * values * values * values))
    hidden = 0.5 * values * (1.0 + inner)
    slope = 0.5 * (1.0 + inner) + 0.5 * values * (1.0 - inner * inner) * ROOT_TWO_PI * (
        1.0 + 3.0 * CUBIC * values * values
    )
    return hidden.astype(BF16), slope.astype(BF16)


def contract(left, right, left_dim, right_dim):
    return lax.dot_general(
        left, right, (((left_dim,), (right_dim,)), ((), ())), preferred_element_type=F32
    )


def mm(left, right):
    return contract(left, right, 1, 0)


def mm_left(left, right):
    return contract(left, right, 0, 0)


def score_block(info, keys, queries, key_block, query_block, masked):
    scores = contract(keys, queries, 0, 0)
    if masked:
        rows = scores.shape[0]
        key_place = key_block * rows + lax.broadcasted_iota(jnp.int32, scores.shape, 0)
        query_place = query_block * rows + lax.broadcasted_iota(jnp.int32, scores.shape, 1)
        allowed = (key_place <= query_place) & (key_place < info[0])
        scores = jnp.where(allowed, scores, MASKED)
    return scores


def for_blocks(info, stream, chunk, block_rows, work):
    def one(step, carry):
        key_half, query_half = step // 2, step % 2
        key_block, query_block = info[5 + 2 * chunk + key_half], info[1 + 2 * stream + query_half]
        key_at = pl.ds(pl.multiple_of(key_half * block_rows, block_rows), block_rows)
        query_at = pl.ds(pl.multiple_of(query_half * block_rows, block_rows), block_rows)
        first = key_block * block_rows
        counts = (key_block <= query_block) & (first < info[0])
        partial = (key_block == query_block) | (first + block_rows > info[0])

        @pl.when(counts & partial)
        def _():
            work(key_at, query_at, key_block, query_block, True)

        @pl.when(counts & jnp.logical_not(partial))
        def _():
            work(key_at, query_at, key_block, query_block, False)

        return carry

    lax.fori_loop(0, 4, one, 0)


def attend_kernel(first_chunk, chunks, streams, resumed, last, info, *refs):
    per_stream = 4 if resumed else 1
    given = [refs[per_stream * i : per_stream * (i + 1)] for i in range(streams)]
    refs = refs[per_stream * streams :]
    pairs, refs = refs[:chunks], refs[chunks:]
    per_output = 2 if last else 3
    results = [refs[per_output * i : per_output * (i + 1)] for i in range(streams)]
    scratch = refs[per_output * streams :]
    heads, head_size, tokens = given[0][0].shape
    rows = tokens // 2
    factor = head_size**-0.5 * LOG2E
    for stream in range(streams):
        queries = given[stream][0]
        top, total, sums = (
            scratch[3 * stream : 3 * stream + 3] if last else results[stream]
        )
        if resumed:
            for kept, start in zip((top, total, sums), given[stream][1:]):
                kept[...] = start[...]
        else:
            top[...] = jnp.full_like(top, MASKED)
            total[...] = jnp.zeros_like(total)
            sums[...] = jnp.zeros_like(sums)
        for chunk in range(chunks):
            pair = pairs[chunk]

            def work(
                key_at,
                query_at,
                key_block,
                query_block,
                masked,
                pair=pair,
                queries=queries,
                top=top,
                total=total,
                sums=sums,
            ):
                scores = [
                    score_block(
                        info,
                        pair[0, head, :, key_at],
                        queries[head, :, query_at],
                        key_block,
                        query_block,
                        masked,
                    )
                    for head in range(heads)
                ]
                olds = [top[head, :, query_at] for head in range(heads)]
                news = [
                    jnp.maximum(old, jnp.max(score, axis=0, keepdims=True) * factor)
                    for old, score in zip(olds, scores)
                ]
                weights = [jnp.exp2(score * factor - new) for score, new in zip(scores, news)]
                products = [
                    contract(pair[1, head, :, key_at], weights[head].astype(BF16), 1, 0)
                    for head in range(heads)
                ]
                for head in range(heads):
                    decay = jnp.exp2(olds[head] - news[head])
                    top[head, :, query_at] = news[head]
                    total[head, :, query_at] = total[head, :, query_at] * decay + jnp.sum(
                        weights[head], axis=0, keepdims=True
                    )
                    sums[head, :, query_at] = sums[head, :, query_at] * decay + products[head]

            for_blocks(info, stream, first_chunk + chunk, rows, work)
        if last:
            mixed, log_total = results[stream]
            for head in range(heads):
                mixed[head] = (sums[head] / total[head]).astype(BF16)
                log_total[head] = top[head] + jnp.log2(total[head])


def attend_back_kernel(first_chunk, chunks, resumed, info, *refs):
    per_stream = 5 if resumed else 4
    streams = (len(refs) - 2 * chunks - 2) // (per_stream + 1)
    given = [refs[per_stream * i : per_stream * (i + 1)] for i in range(streams)]
    refs = refs[per_stream * streams :]
    pairs, refs = refs[:chunks], refs[chunks:]
    query_sums, refs = refs[:streams], refs[streams:]
    grad_pairs, refs = refs[:chunks], refs[chunks:]
    inner, pair_sums = refs
    heads, head_size, tokens = given[0][0].shape
    rows = tokens // 2
    scale = head_size**-0.5
    factor = scale * LOG2E
    for stream in range(streams):
        _, grad_mixed, mixed = given[stream][:3]
        for head in range(heads):
            inner[stream, head] = jnp.sum(
                grad_mixed[head].astype(F32) * mixed[head].astype(F32), axis=0, keepdims=True
            )
        query_sums[stream][...] = (
            given[stream][4][...] if resumed else jnp.zeros_like(query_sums[stream])
        )
    for chunk in range(chunks):
        pair = pairs[chunk]
        pair_sums[...] = jnp.zeros_like(pair_sums)
        for stream in range(streams):
            queries, grad_mixed, _, log_total = given[stream][:4]

            def work(
                key_at,
                query_at,
                key_block,
                query_block,
                masked,
                pair=pair,
                stream=stream,
                queries=queries,
                grad_mixed=grad_mixed,
                log_total=log_total,
            ):
                every = range(heads)
                keys = [pair[0, head, :, key_at] for head in every]
                values = [pair[1, head, :, key_at] for head in every]
                query_parts = [queries[head, :, query_at] for head in every]
                grad_parts = [grad_mixed[head, :, query_at] for head in every]
                scores = [
                    score_block(info, keys[h], query_parts[h], key_block, query_block, masked)
                    for h in every
                ]
                grad_probs = [contract(values[h], grad_parts[h], 0, 0) for h in every]
                probs = [
                    jnp.exp2(scores[h] * factor - log_total[h, :, query_at]) for h in every
                ]
                grad_scores = [
                    (probs[h] * (grad_probs[h] - inner[stream, h, :, query_at])).astype(BF16)
                    for h in every
                ]
                low_probs = [member.astype(BF16) for member in probs]
                for_values = [contract(grad_parts[h], low_probs[h], 1, 1) for h in every]
                for_keys = [contract(query_parts[h], grad_scores[h], 1, 1) for h in every]
                for_queries = [contract(keys[h], grad_scores[h], 1, 0) for h in every]
                for h in every:
                    pair_sums[0, h, :, key_at] += for_keys[h]
                    pair_sums[1, h, :, key_at] += for_values[h]
                    query_sums[stream][h, :, query_at] += for_queries[h]

            for_blocks(info, stream, first_chunk + chunk, rows, work)
        grad_pairs[chunk][0] = (pair_sums[0] * scale).astype(grad_pairs[chunk].dtype)
        grad_pairs[chunk][1] = pair_sums[1].astype(grad_pairs[chunk].dtype)


SMALL_COST = pl.CostEstimate(flops=1 << 20, bytes_accessed=1 << 20, transcendentals=0)


def attend(info, queries, pairs, first_chunk, states, last):
    heads, head_size, tokens = queries[0].shape
    vmem = pl.BlockSpec(memory_space=pltpu.VMEM)
    state = [(heads, 1, tokens), (heads, 1, tokens), (heads, head_size, tokens)]
    operands = []
    for stream, member in enumerate(queries):
        operands.append(member)
        if states is not None:
            operands.extend(states[stream])
    operands.extend(pairs)
    if last:
        shapes = [
            jax.ShapeDtypeStruct((heads, head_size, tokens), BF16),
            jax.ShapeDtypeStruct((heads, 1, tokens), F32),
        ]
    else:
        shapes = [jax.ShapeDtypeStruct(shape, F32) for shape in state]
    results = pl.pallas_call(
        functools.partial(
            attend_kernel, first_chunk, len(pairs), len(queries), states is not None, last
        ),
        out_shape=tuple(shapes * len(queries)),
        in_specs=[pl.BlockSpec(memory_space=pltpu.SMEM)] + [vmem] * len(operands),
        out_specs=(vmem,) * (len(shapes) * len(queries)),
        scratch_shapes=[pltpu.VMEM(shape, F32) for shape in state] * len(queries) if last else [],
        compiler_params=pltpu.CompilerParams(vmem_limit_bytes=62 << 20),
        cost_estimate=SMALL_COST,
    )(info, *operands)
    return [results[len(shapes) * i : len(shapes) * (i + 1)] for i in range(len(queries))]


def attend_back(info, given, pairs, first_chunk, resumed, pair_type):
    heads, head_size, tokens = given[0][0].shape
    vmem = pl.BlockSpec(memory_space=pltpu.VMEM)
    operands = [member for stream in given for member in stream] + list(pairs)
    results = pl.pallas_call(
        functools.partial(attend_back_kernel, first_chunk, len(pairs), resumed),
        out_shape=tuple(
            jax.ShapeDtypeStruct((heads, head_size, tokens), F32) for _ in given
        )
        + tuple(jax.ShapeDtypeStruct(pair.shape, pair_type) for pair in pairs),
        in_specs=[pl.BlockSpec(memory_space=pltpu.SMEM)] + [vmem] * len(operands),
        out_specs=(vmem,) * (len(given) + len(pairs)),
        scratch_shapes=[
            pltpu.VMEM((len(given), heads, 1, tokens), F32),
            pltpu.VMEM((2, heads, head_size, tokens), F32),
        ],
        compiler_params=pltpu.CompilerParams(vmem_limit_bytes=62 << 20),
        cost_estimate=SMALL_COST,
    )(info, *operands)
    return results[: len(given)], results[len(given) :]


def near():
    tensor = lax.axis_index(TENSOR)
    return {TENSOR: tensor + 1 - 2 * lax.rem(tensor, 2)}


def far():
    tensor = lax.axis_index(TENSOR)
    return {TENSOR: tensor + 2 - 4 * lax.rem(tensor // 2, 2)}


def pair():
    seq = lax.axis_index(SEQ)
    return {SEQ: seq + 1 - 2 * lax.rem(seq, 2)}


def pair_far():
    seq = lax.axis_index(SEQ)
    return {SEQ: seq + 2 - 4 * lax.rem(seq // 2, 2)}


def across():
    return {CELL: 1 - lax.axis_index(CELL)}


class Wires:
    def __init__(self, r, partners):
        self.send, self.recv, self.local = r.send, r.recv, r.local
        self.started, self.open = 0, []
        barrier = pltpu.get_barrier_semaphore()
        for partner in partners:
            pl.semaphore_signal(barrier, inc=1, device_id=partner(), device_id_type=MESH)
        pl.semaphore_wait(barrier, len(partners))

    def start(self, source, target, partner):
        at = self.started
        copy = pltpu.make_async_remote_copy(
            src_ref=source,
            dst_ref=target,
            send_sem=self.send.at[at],
            recv_sem=self.recv.at[at],
            device_id=partner(),
            device_id_type=MESH,
        )
        copy.start()
        self.started += 1
        self.open.append(copy)
        return copy

    def sent(self, copy):
        copy.wait_send()
        self.open = [member for member in self.open if member is not copy]

    def finish(self):
        for copy in self.open:
            copy.wait_send()


class Local:
    def __init__(self, r, at, source, target):
        self.copy = pltpu.make_async_copy(source, target, r.local.at[at])
        self.copy.start()
        self.target, self.waited = target, False

    def get(self):
        if not self.waited:
            self.copy.wait()
            self.waited = True
        return self.target


def call_kernel(body, given, in_hbm, results, streamed, out_hbm, scratch, collective_id):
    out_hbm = dict(out_hbm, out=streamed)
    scratch = dict(
        scratch,
        **jax.tree.map(lambda member: pltpu.VMEM(member.shape, member.dtype), streamed),
        send=pltpu.SemaphoreType.DMA((COPIES,)),
        recv=pltpu.SemaphoreType.DMA((COPIES,)),
        local=pltpu.SemaphoreType.DMA((40,)),
    )
    vmem, hbm = pl.BlockSpec(memory_space=pltpu.VMEM), pl.BlockSpec(memory_space=pl.ANY)
    trees = (given, in_hbm, results, out_hbm, scratch)
    flat = [jax.tree.flatten(tree) for tree in trees]

    def kernel(*refs):
        found, at = {}, 0
        for leaves, tree in flat:
            found.update(jax.tree.unflatten(tree, refs[at : at + len(leaves)]))
            at += len(leaves)
        found.update(out=types.SimpleNamespace(**found[next(iter(dict(out=0)))]))
        body(types.SimpleNamespace(**found))

    outs = pl.pallas_call(
        kernel,
        out_shape=tuple(flat[2][0] + flat[3][0]),
        in_specs=[vmem] * len(flat[0][0]) + [hbm] * len(flat[1][0]),
        out_specs=tuple([vmem] * len(flat[2][0]) + [hbm] * len(flat[3][0])),
        scratch_shapes=flat[4][0],
        compiler_params=pltpu.CompilerParams(
            collective_id=collective_id, has_side_effects=True, vmem_limit_bytes=62 << 20
        ),
        cost_estimate=SMALL_COST,
    )(*flat[0][0], *flat[1][0])
    count = len(flat[2][0])
    found = jax.tree.unflatten(flat[2][1], outs[:count])
    others = jax.tree.unflatten(flat[3][1], outs[count:])
    found.update(others.pop(next(iter(dict(out=0)))))
    found.update(others)
    return found


class Flush:
    def __init__(self, r):
        self.r, self.copies = r, []

    def __call__(self, source, target):
        self.copies.append(Local(self.r, 12 + len(self.copies), source, target))

    def finish(self):
        for copy in self.copies:
            copy.get()


def shape_of(shape, dtype):
    return jax.ShapeDtypeStruct(shape, dtype)


def twice(value):
    return [value, value]


def by_rows(count, work, step=32):
    def one(index, carry):
        work(pl.ds(pl.multiple_of(index * step, step), step))
        return carry

    lax.fori_loop(0, count // step, one, 0)


def by_columns(width, work, step=128):
    def one(index, carry):
        work(pl.ds(pl.multiple_of(index * step, step), step))
        return carry

    lax.fori_loop(0, width // step, one, 0)
    if width % step:
        work(pl.ds(width // step * step, width % step))


def head_rows(source, rows):
    parts = [source[head, :, rows].astype(F32) for head in range(source.shape[0])]
    return jnp.concatenate(parts, axis=0).T


def put_heads(target, rows, values):
    head_size = target.shape[1]
    for head in range(target.shape[0]):
        target[head, :, rows] = values[head * head_size : (head + 1) * head_size].astype(
            target.dtype
        )


class Exchange:
    def __init__(self, wires, part, sent, got):
        self.wires, self.part, self.sent, self.got = wires, part, sent, got
        self.rows = part.shape[0]

    def give(self, values):
        self.sent[0] = values.astype(BF16)
        self.to_near = self.wires.start(self.sent.at[0], self.got.at[0], near)

    def keep(self, values):
        self.part[...] = values

    def part_rows(self, part):
        return pl.ds(part * (self.rows // 2), self.rows // 2)

    def join(self, cross):
        self.to_near.wait_recv()
        self.to_far = [None, None]
        for part in (0, 1):
            start = part * (self.rows // 2)

            def work(rows, start=start):
                at = pl.ds(start + rows.start, rows.size)
                self.sent[1, at] = (self.part[at] + self.got[0, at].astype(F32)).astype(BF16)

            by_rows(self.rows // 2, work)
            if cross:
                self.cross(part)

    def cross(self, part):
        rows = self.part_rows(part)
        self.to_far[part] = self.wires.start(
            self.sent.at[1, rows], self.got.at[1, rows], far
        )

    def wait(self, then=None):
        for part in (0, 1):
            self.to_far[part].wait_recv()
            if then is not None:
                then.cross(part)

    def total(self, rows):
        return self.sent[1, rows].astype(F32) + self.got[1, rows].astype(F32)


def add_into(target, left, right):
    def work(columns):
        target[:, columns] = (
            left[:, columns].astype(F32) + right[:, columns].astype(F32)
        ).astype(BF16)

    by_columns(target.shape[1], work)


def weight_grads(r):
    for j in range(3):
        total = None
        for grads, wide in zip(r.grads, r.wide_one):
            heads = [grads[j, head].astype(F32) for head in range(grads.shape[1])]
            product = mm(jnp.concatenate(heads, axis=0).astype(BF16), wide[...])
            total = product if total is None else total + product
        r.pieces[j // 2, j % 2] = total.astype(BF16)
    r.pieces[1, 1] = r.out_piece[...]


class Sum:
    def __init__(self, wires, whole, out, near_sum, got, got_far):
        self.wires, self.whole, self.out = wires, whole, out
        self.near_sum, self.got, self.got_far = near_sum, got, got_far
        self.bit = lax.rem(lax.axis_index(SEQ), 2)
        self.copy = None

    def wait(self):
        if self.copy is not None:
            self.copy.wait_recv()
            self.copy = None

    def one(self):
        self.copy = self.wires.start(self.whole.at[1 - self.bit], self.got, pair)

    def two(self):
        self.wait()
        add_into(self.near_sum, self.whole.at[self.bit], self.got)
        self.copy = self.wires.start(self.near_sum, self.got_far, pair_far)

    def three(self):
        self.wait()
        mine = self.out.at[self.bit]
        add_into(mine, self.near_sum, self.got_far)
        self.copy = self.wires.start(mine, mine, pair)

    def five(self, everything, rows):
        self.wait()
        target = everything.at[lax.axis_index(CELL), :, rows]
        self.copy = self.wires.start(self.out, target, across)
        return self.out, target


def sum_scratch(rows, width):
    return [pltpu.VMEM((rows, width), BF16)] * 3


def exchange_scratch(half, width, exchanges):
    return dict(
        part=pltpu.VMEM((2, half, width), F32),
        sent=pltpu.VMEM((2 * exchanges, 2, half, width), BF16),
        got=pltpu.VMEM((2 * exchanges, 2, half, width), BF16),
    )


def exchanges_of(r, wires, count):
    return [
        [Exchange(wires, r.part.at[i], r.sent.at[2 * k + i], r.got.at[2 * k + i]) for i in (0, 1)]
        for k in range(count)
    ]


def project(r, i, to_near, weight):
    half = r.wide_one[i].shape[0] // 2
    for part in (0, 1):
        at = pl.ds(part * half, half)
        if part and to_near is not None:
            to_near.wait_recv()
        wide = r.wide_one[i][at]
        for j in range(3):
            values = contract(wide, weight[j], 1, 1) + r.qkv_b[j : j + 1]
            target = r.queries[i] if j == 0 else r.pair[i].at[j - 1]
            put_heads(target, at, values.T)


def side_and_core():
    return lax.axis_index(SEQ) // 2, lax.rem(lax.axis_index(TENSOR), 2)


def core_columns(half, core):
    return pl.ds(pl.multiple_of(core * half, half), half)


def start_kernel(r):
    side, core = side_and_core()
    half = r.stream[0].shape[0]
    own = Local(r, 0, r.tokens.at[side], r.own_tokens)
    weight = Local(r, 1, r.qkv_w.at[0], r.own_qkv)
    wires = Wires(r, (near, pair, pair_far))
    flush = Flush(r)
    arriving = wires.start(
        r.tokens.at[1 - side, :, core_columns(half, core)], r.got_tokens, pair_far
    )

    def norm(i, part, values):
        r.rows[...] = values.astype(F32).T

        def work(rows):
            stream = r.rows[rows]
            normed, inverse = normalize(stream)
            if part == 0:
                r.stream[i][rows] = stream
                r.normed_one[i][rows] = normed.astype(BF16)
                r.inverse_one[i][rows] = inverse
            to = pl.ds(part * half + rows.start, rows.size)
            r.wide_one[i][to] = (normed * r.gain[...] + r.shift[...]).astype(BF16)

        by_rows(half, work)

    tokens = own.get()
    for part in (0, 1):
        norm(0, part, tokens[:, core_columns(half, lax.rem(core + part, 2))])
    project(r, 0, None, weight.get())
    paired = wires.start(r.pair[0], r.got_pair, pair)
    flush_next(r, flush, 0)
    arriving.wait_recv()
    norm(1, 0, r.got_tokens[...])
    wide = r.wide_one[1]
    to_near = wires.start(wide.at[pl.ds(0, half)], wide.at[pl.ds(half, half)], near)
    project(r, 1, to_near, weight.get())
    flush_next(r, flush, 1)
    paired.wait_recv()
    flush(r.got_pair, r.out.got_pair)
    flush.finish()
    wires.finish()


def flush_next(r, flush, i):
    for own, out in (
        (r.stream, r.out.stream),
        (r.wide_one, r.out.wide_one),
        (r.normed_one, r.out.normed_one),
        (r.inverse_one, r.out.inverse_one),
        (r.queries, r.out.queries),
        (r.pair, r.out.pair),
    ):
        flush(own[i], out[i])


def next_shapes(half, width, head_shape):
    return dict(
        stream=twice(shape_of((half, width), F32)),
        wide_one=twice(shape_of((2 * half, width), BF16)),
        normed_one=twice(shape_of((half, width), BF16)),
        inverse_one=twice(shape_of((half, 1), F32)),
        queries=twice(shape_of(head_shape, BF16)),
        pair=twice(shape_of((2,) + head_shape, BF16)),
        got_pair=shape_of((2,) + head_shape, BF16),
    )


def start_call(tokens, qkv_w, qkv_b, gain, shift, head_shape, collective_id):
    _, width, row_count = tokens.shape
    half = row_count // 2
    return call_kernel(
        start_kernel,
        dict(qkv_b=qkv_b, gain=gain, shift=shift),
        dict(tokens=tokens, qkv_w=qkv_w),
        {},
        next_shapes(half, width, head_shape),
        {},
        dict(
            own_tokens=pltpu.VMEM((width, row_count), BF16),
            got_tokens=pltpu.VMEM((width, half), BF16),
            own_qkv=pltpu.VMEM(qkv_w.shape[1:], BF16),
            rows=pltpu.VMEM((half, width), F32),
        ),
        collective_id,
    )


def forward_kernel(layer, last, r):
    side, core = side_and_core()
    half = r.base[0].shape[0]
    halves = (pl.ds(0, half), pl.ds(half, half))
    out_w = Local(r, 0, r.out_w.at[layer], r.own_out)
    up_w = Local(r, 1, r.up_w.at[layer], r.own_up)
    down_w = Local(r, 2, r.down_w.at[layer], r.own_down)
    if not last:
        qkv_w = Local(r, 3, r.qkv_w.at[layer + 1], r.own_qkv)
    wires = Wires(r, (near, far) + (() if last else (pair, pair_far)))
    flush = Flush(r)
    first, second = exchanges_of(r, wires, 2)
    to_near = {}

    def row(index):
        return r.vectors[index : index + 1]

    def norm(i, exchange, base, at, kept, normed_to, inverse_to, wide):
        def work(rows):
            stream = base[rows] + exchange.total(rows) + row(at)
            normed, inverse = normalize(stream)
            kept[rows] = stream
            normed_to[rows] = normed.astype(BF16)
            inverse_to[rows] = inverse
            wide[rows] = (normed * row(at + 1) + row(at + 2)).astype(BF16)

        by_rows(half, work)
        to_near[i] = wires.start(wide.at[halves[0]], wide.at[halves[1]], near)

    def attended(i):
        for part in (1, 0):
            values = mm(head_rows(r.mixed[i], halves[part]).astype(BF16), out_w.get()[...])
            (first[i].give if part else first[i].keep)(values)

    def mid_norm(i):
        norm(
            i, first[i], r.base[i], 0, r.mid.at[i], r.normed_two[i], r.inverse_two[i], r.wide_two[i]
        )

    def feed(i):
        for part in (0, 1):
            if part:
                to_near[i].wait_recv()
            r.wide_part[...] = mm(r.wide_two[i][halves[part]], up_w.get()[...])

            def work(rows, part=part):
                hidden, slope = gelu_both(r.wide_part[rows] + r.up_b[...])
                to = pl.ds(part * half + rows.start, rows.size)
                r.hidden[i][to] = hidden
                r.slope[i][to] = slope

            by_rows(half, work)
        for part in (1, 0):
            values = mm(r.hidden[i][halves[part]], down_w.get()[...])
            (second[i].give if part else second[i].keep)(values)
        for own, out in (
            (r.wide_two, r.out.wide_two),
            (r.normed_two, r.out.normed_two),
            (r.inverse_two, r.out.inverse_two),
            (r.hidden, r.out.hidden),
            (r.slope, r.out.slope),
        ):
            flush(own[i], out[i])

    def leave(i):
        if last:

            def work(rows):
                r.part[i, rows] = r.mid[i, rows] + second[i].total(rows) + row(3)

            by_rows(half, work)
            r.low[i][...] = r.part[i].T.astype(BF16)
        else:
            norm(
                i, second[i], r.mid.at[i], 3, r.stream[i], r.normed_one[i], r.inverse_one[i],
                r.wide_one[i],
            )
            project(r, i, to_near[i], qkv_w.get())
            flush_next(r, flush, i)

    for i in (0, 1):
        attended(i)
    first[0].join(True)
    first[1].join(False)
    first[0].wait(first[1])
    if not last:
        given = wires.start(
            r.out_grad.at[1 - side, :, core_columns(half, core)], r.got_grad, pair_far
        )
    mid_norm(0)
    feed(0)
    second[0].join(False)
    first[1].wait(second[0])
    mid_norm(1)
    feed(1)
    second[1].join(False)
    second[0].wait(second[1])
    leave(0)
    if not last:
        paired = wires.start(r.pair[0], r.got_pair, pair)
    second[1].wait()
    leave(1)
    if not last:
        given.wait_recv()
        paired.wait_recv()
        flush(r.got_pair, r.out.got_pair)
    flush.finish()
    wires.finish()


def forward_call(given, in_hbm, layer, last, collective_id):
    half, width = given["base"][0].shape
    hidden_width = in_hbm["up_w"].shape[2]
    head_shape = given["mixed"][0].shape
    wide_hidden = shape_of((2 * half, hidden_width), BF16)
    results = {}
    streamed = dict(
        wide_two=twice(shape_of((2 * half, width), BF16)),
        normed_two=twice(shape_of((half, width), BF16)),
        inverse_two=twice(shape_of((half, 1), F32)),
        hidden=twice(wide_hidden),
        slope=twice(wide_hidden),
    )
    out_hbm = {}
    scratch = dict(
        exchange_scratch(half, width, 2),
        mid=pltpu.VMEM((2, half, width), F32),
        wide_part=pltpu.VMEM((half, hidden_width), F32),
        own_out=pltpu.VMEM(in_hbm["out_w"].shape[1:], BF16),
        own_up=pltpu.VMEM(in_hbm["up_w"].shape[1:], BF16),
        own_down=pltpu.VMEM(in_hbm["down_w"].shape[1:], BF16),
    )
    if last:
        results.update(low=twice(shape_of((width, half), BF16)))
    else:
        streamed.update(next_shapes(half, width, head_shape))
        out_hbm.update(got_grad=shape_of((width, half), BF16))
        scratch.update(own_qkv=pltpu.VMEM(in_hbm["qkv_w"].shape[1:], BF16))
    return call_kernel(
        functools.partial(forward_kernel, layer, last),
        given,
        in_hbm,
        results,
        streamed,
        out_hbm,
        scratch,
        collective_id,
    )


def backward_kernel(attention, feed, riding, r):
    begin, end = attention is None, feed is None
    side, core = side_and_core()
    half = r.grad_out[0].shape[0]
    halves = (pl.ds(0, half), pl.ds(half, half))
    if begin:
        own = Local(r, 0, r.out_grad.at[side], r.own_grad)
    else:
        qkv_w = Local(r, 1, r.qkv_w.at[attention], r.own_qkv)
    if not end:
        down_w = Local(r, 2, r.down_w.at[feed], r.own_down)
        up_w = Local(r, 3, r.up_w.at[feed], r.own_up)
        out_w = Local(r, 4, r.out_w.at[feed], r.own_out)
    partners = [near, far]
    if begin or riding:
        partners.append(pair_far)
    if riding:
        partners.append(pair)
    if riding == 2:
        partners.append(across)
    wires = Wires(r, partners)
    exchanges = exchanges_of(r, wires, int(not begin) + int(not end))
    to_near = {}
    flush = Flush(r)
    r.sums[...] = jnp.zeros_like(r.sums)
    cell = lax.axis_index(CELL)
    if riding:
        rider = Sum(wires, r.whole, r.summed if riding == 2 else None, r.near_sum, r.got_sum, r.got_far)

    def note(index, values):
        r.sums[index : index + 1, : values.shape[1]] += jnp.sum(values, axis=0, keepdims=True)

    def gather(i, exchange):
        scale = HEAD**-0.5
        for part in (1, 0):
            at = halves[part]
            values = None
            for j in range(3):
                target = r.grads[i].at[j]
                for head in range(target.shape[0]):
                    if j == 0:
                        found = r.query_sum[i][head, :, at] * scale
                    else:
                        found = r.pair_sum[i][j - 1, head, :, at] + r.pair_got[i][
                            j - 1, head, :, at
                        ].astype(F32)
                    target[head, :, at] = found.astype(BF16)
                rows = head_rows(target, at)
                if j != 1:
                    start = j // 2 * (r.sums.shape[1] // 256 * 128)
                    r.sums[7:8, start : start + rows.shape[1]] += jnp.sum(
                        rows, axis=0, keepdims=True
                    )
                product = mm(rows.astype(BF16), qkv_w.get()[j])
                values = product if values is None else values + product
            (exchange.give if part else exchange.keep)(values)
        flush(r.grads[i], r.out.grads[i])

    def norm(i, exchange, base, normed_of, inverse_of, gain, at, wide):
        def work(rows):
            incoming = exchange.total(rows)
            normed = normed_of[rows].astype(F32)
            grad = base[rows] + norm_back(
                incoming, normed, inverse_of[rows], r.gains[gain : gain + 1]
            )
            r.grad_out[i][rows] = grad
            note(at, incoming * normed)
            note(at + 1, incoming)
            note(at + 2, grad)
            if wide is not None:
                wide[rows] = grad.astype(BF16)

        by_rows(half, work)
        if wide is not None:
            to_near[i] = wires.start(wide.at[halves[0]], wide.at[halves[1]], near)

    def first_norm(i):
        norm(
            i, exchanges[0][i], r.grad[i], r.normed_one[i], r.inverse_one[i], 0, 0,
            None if end else r.wide[i],
        )
        if end:
            r.low[i][...] = r.grad_out[i][...].T.astype(BF16)

    def second_norm(i):
        norm(
            i, exchanges[-1][i], r.grad_out[i], r.normed_two[i], r.inverse_two[i], 1, 3,
            r.wide_mid[i],
        )
        for part in (0, 1):
            if part:
                to_near[i].wait_recv()
            values = contract(out_w.get()[...], r.wide_mid[i][halves[part]], 1, 1)
            put_heads(r.mixed_grad[i], halves[part], values)
        for own, out in (
            (r.wide_mid, r.out.wide_mid),
            (r.mixed_grad, r.out.mixed_grad),
            (r.grad_out, r.out.grad_out),
        ):
            flush(own[i], out[i])

    def first_rows(i):
        if i == 0:
            given = own.get()
            for part in (0, 1):
                values = given[:, core_columns(half, lax.rem(core + part, 2))].astype(F32).T
                if part == 0:
                    r.grad_out[0][...] = values
                r.wide[0][halves[part]] = values.astype(BF16)
        else:
            r.grad_out[1][...] = r.got_grad[...].astype(F32).T
            wide = r.wide[1]
            wide[halves[0]] = r.grad_out[1][...].astype(BF16)
            to_near[1] = wires.start(wide.at[halves[0]], wide.at[halves[1]], near)
        by_rows(half, lambda rows: note(2, r.grad_out[i][rows]))

    def slide(i, exchange):
        wide = r.wide[i]
        for part in (0, 1):
            if part and i in to_near:
                to_near[i].wait_recv()
            r.wide_part[...] = contract(wide[halves[part]], down_w.get()[...], 1, 1)

            def work(rows, part=part):
                to = pl.ds(part * half + rows.start, rows.size)
                hidden = r.wide_part[rows].astype(BF16).astype(F32)
                pre = (hidden * r.slope[i][to].astype(F32)).astype(BF16)
                r.pre[i][to] = pre
                note(6, pre.astype(F32))

            by_rows(half, work)
        for part in (1, 0):
            values = contract(r.pre[i][halves[part]], up_w.get()[...], 1, 1)
            (exchange.give if part else exchange.keep)(values)
        flush(r.pre[i], r.out.pre[i])
        flush(r.wide[i], r.out.wide[i])

    def ride(step):
        if riding == 1 and step == 0:
            rider.one()
        elif riding == 1 and step == 1:
            rider.two()
        elif riding == 1 and step == 5:
            rider.wait()
        elif riding == 2 and step == 0:
            rider.one()
        elif riding == 2 and step == 1:
            rider.two()
            weight_grads(r)
            r.crossing = wires.start(r.pieces.at[1 - cell], r.got_pieces, across)
        elif riding == 2 and step == 3:
            rider.three()
            r.crossing.wait_recv()
            for k in (0, 1):
                add_into(r.whole_next.at[k], r.pieces.at[cell, k], r.got_pieces.at[k])
        elif riding == 2 and step == 5:
            rider.wait()

    ride(0)
    if begin:
        (after,) = exchanges
        placed = place_cells(r, wires, r.block, r.block_low)
        for i in (0, 1):
            first_rows(i)
            slide(i, after[i])
            after[i].join(i == 0)
        after[0].wait(after[1])
        second_norm(0)
        placed.forward()
        after[1].wait()
        second_norm(1)
        placed.finish()
    else:
        before, after = exchanges[0], exchanges[-1]
        a, b = (1, 0) if end else (0, 1)
        gather(a, before[a])
        gather(b, before[b])
        before[a].join(True)
        before[b].join(False)
        ride(1)
        before[a].wait(before[b])
        first_norm(a)
        if end:
            before[b].wait()
            first_norm(b)
        else:
            slide(a, after[a])
            after[a].join(False)
            before[b].wait(after[a])
            first_norm(b)
            slide(b, after[b])
            after[b].join(False)
            after[a].wait(after[b])
            ride(3)
            second_norm(a)
            after[b].wait()
            second_norm(b)
    ride(5)
    flush.finish()
    wires.finish()


class place_cells:
    def __init__(self, r, wires, target, low):
        side, core = side_and_core()
        half = low[0].shape[1]
        self.wires = wires
        columns = core_columns(half, core)
        self.own = target.at[side, :, columns]
        self.arrived = target.at[1 - side, :, columns]
        self.local = Local(r, 11, low[0], self.own)
        self.to_far = wires.start(low[1], self.own, pair_far)
        self.to_near = wires.start(low[0], self.own, near)

    def forward(self):
        self.to_far.wait_recv()
        self.second = self.wires.start(self.arrived, self.arrived, near)

    def finish(self):
        self.local.get()
        self.to_near.wait_recv()
        self.second.wait_recv()


def backward_call(given, in_hbm, attention, feed, riding, collective_id):
    begin, end = attention is None, feed is None
    some = given["block_low"][0] if begin else given["grad"][0]
    width = given["gains"].shape[1]
    half = some.shape[1] if begin else some.shape[0]
    results = dict(sums=shape_of((8, width), F32))
    streamed = dict()
    grad_out = twice(shape_of((half, width), F32))
    wide = twice(shape_of((2 * half, width), BF16))
    out_hbm = {}
    scratch = exchange_scratch(half, width, int(not begin) + int(not end))
    if begin:
        out_hbm.update(block=shape_of((2, width, 2 * half), BF16))
        scratch.update(own_grad=pltpu.VMEM((width, 2 * half), BF16))
    else:
        head_shape = given["query_sum"][0].shape
        streamed.update(grads=twice(shape_of((3,) + head_shape, BF16)))
        scratch.update(own_qkv=pltpu.VMEM(in_hbm["qkv_w"].shape[1:], BF16))
    if end:
        results.update(low=twice(shape_of((width, half), BF16)), grad_out=grad_out)
    else:
        hidden_width = in_hbm["up_w"].shape[2]
        head_count = in_hbm["out_w"].shape[1] // HEAD
        streamed.update(
            grad_out=grad_out,
            wide=wide,
            wide_mid=wide,
            pre=twice(shape_of((2 * half, hidden_width), BF16)),
            mixed_grad=twice(shape_of((head_count, HEAD, 2 * half), BF16)),
        )
        scratch.update(
            wide_part=pltpu.VMEM((half, hidden_width), F32),
            own_out=pltpu.VMEM(in_hbm["out_w"].shape[1:], BF16),
            own_up=pltpu.VMEM(in_hbm["up_w"].shape[1:], BF16),
            own_down=pltpu.VMEM(in_hbm["down_w"].shape[1:], BF16),
        )
    if riding:
        whole = given["whole"]
        one = pltpu.VMEM(whole.shape[1:], BF16)
        if riding == 2:
            piece = given["out_piece"].shape
            results.update(
                summed=shape_of(whole.shape, BF16),
                whole_next=shape_of((2,) + piece, BF16),
            )
            scratch.update(
                near_sum=one,
                got_far=one,
                pieces=pltpu.VMEM((2, 2) + piece, BF16),
                got_pieces=pltpu.VMEM((2,) + piece, BF16),
            )
        else:
            part = shape_of(whole.shape[1:], BF16)
            results.update(near_sum=part, got_far=part)
        scratch.update(got_sum=one)
    return call_kernel(
        functools.partial(backward_kernel, attention, feed, riding),
        given,
        in_hbm,
        results,
        streamed,
        out_hbm,
        scratch,
        collective_id,
    )


def closing_kernel(sums_too, r):
    wires = Wires(r, [near, pair, pair_far] + ([across] if sums_too else []))
    cell = lax.axis_index(CELL)
    kernels = r.vectors.shape[0]
    r.total[...] = r.vectors[...]

    def vectors(at, partner, own_rows=8):
        copy = wires.start(r.total, r.around.at[at], partner)

        def add():
            copy.wait_recv()
            wires.sent(copy)
            for kernel in range(kernels):
                r.total[kernel, :own_rows] += r.around[at, kernel, :own_rows]

        return add

    if sums_too:
        span = r.sum_feed[0].shape[1]
        spans = [pl.ds(0, span), pl.ds(span, r.all_feed.shape[2] - span)]
        whole = pl.ds(0, r.all_last.shape[2])
        feed = [
            Sum(wires, r.whole_feed[k], r.sum_feed[k], *r.riding_feed[k]) for k in (0, 1)
        ]
        last = Sum(wires, r.whole_last, r.sum_last, *r.riding_last)
        late = Sum(wires, None, r.sum_late, r.near_late, None, r.far_late)
        prior = Sum(wires, None, r.sum_prior, r.near_prior, None, r.far_prior)
        local = []

        def fold(target, kept, got, rows):
            def work(columns):
                target[:, :, columns] = (
                    kept[:, rows, columns].astype(F32) + got[:, rows, columns].astype(F32)
                ).astype(BF16)

            by_columns(kept.shape[2], work)

        def five(member, everything, rows):
            own, target = member.five(everything, rows)
            local.append(Local(r, len(local), own, target))

        fold(r.whole_feed[0], r.kept_feed, r.got_feed, spans[0])
        feed[0].one()
        late.three()
        weight_grads(r)
        arriving = wires.start(r.pieces.at[1 - cell], r.got_last, across)
        local.append(Local(r, 0, r.early, r.all_late.at[cell, :, spans[0]]))
        local.append(Local(r, 1, r.got_early, r.all_late.at[1 - cell, :, spans[0]]))
        add = vectors(0, near, 6)
        feed[0].two()
        arriving.wait_recv()
        for k in (0, 1):
            add_into(r.whole_last.at[k], r.pieces.at[cell, k], r.got_last.at[k])
        last.one()
        prior.three()
        five(late, r.all_late, spans[1])
        fold(r.whole_feed[1], r.kept_feed, r.got_feed, spans[1])
        feed[0].three()
        five(prior, r.all_prior, whole)
        last.two()
        feed[1].one()
        last.three()
        feed[1].two()
        five(feed[0], r.all_feed, spans[0])
        add()
        add = vectors(1, across)
        five(last, r.all_last, whole)
        feed[1].three()
        add()
        add = vectors(2, pair)
        five(feed[1], r.all_feed, spans[1])
        add()
        placed = place_cells(r, wires, r.tokens_grad, r.low)
        add = vectors(3, pair_far)
        placed.forward()
        add()
        for member in feed + [late, prior, last]:
            member.wait()
        for copy in local:
            copy.get()
    else:
        placed = place_cells(r, wires, r.tokens_grad, r.low)
        vectors(0, near, 6)()
        placed.forward()
        vectors(1, pair)()
        vectors(2, pair_far)()
    r.totals[...] = r.total[...]
    placed.finish()
    wires.finish()


def closing_call(given, in_hbm, sums_too, collective_id):
    width, half = given["low"][0].shape
    vectors = given["vectors"].shape
    results = dict(totals=shape_of(vectors, F32))
    out_hbm = dict(tokens_grad=shape_of((2, width, 2 * half), BF16))
    scratch = dict(total=pltpu.VMEM(vectors, F32), around=pltpu.VMEM((4,) + vectors, F32))
    if sums_too:
        feed, last = given["kept_feed"].shape, (2,) + given["out_piece"].shape
        late = (2,) + given["near_late"].shape
        early = (feed[0], feed[1] - late[1]) + feed[2:]
        spans = [pltpu.VMEM(early, BF16), pltpu.VMEM(late, BF16)]
        out_hbm.update(
            all_feed=shape_of((2,) + feed, BF16),
            all_late=shape_of((2,) + feed, BF16),
            all_last=shape_of((2,) + last, BF16),
            all_prior=shape_of((2,) + last, BF16),
        )
        scratch.update(
            whole_feed=spans,
            sum_feed=spans,
            riding_feed=[sum_scratch(*early[1:]), sum_scratch(*late[1:])],
            sum_late=spans[1],
            whole_last=pltpu.VMEM(last, BF16),
            sum_last=pltpu.VMEM(last, BF16),
            got_last=pltpu.VMEM(last, BF16),
            pieces=pltpu.VMEM((2,) + last, BF16),
            riding_last=sum_scratch(*last[1:]),
            sum_prior=pltpu.VMEM(last, BF16),
        )
    return call_kernel(
        functools.partial(closing_kernel, sums_too),
        given,
        in_hbm,
        results,
        {},
        out_hbm,
        scratch,
        collective_id,
    )


class Line:
    def __init__(self):
        self.last = None

    def run(self, step, *operands):
        if self.last is not None:
            operands, _ = lax.optimization_barrier((operands, self.last))
        results = step(*operands)
        self.last = jax.tree.leaves(results)[0]
        return types.SimpleNamespace(**results) if isinstance(results, dict) else results


def add_low(kept, got):
    return (kept.astype(F32) + got.astype(F32)).astype(BF16)


def pick(cell, low, high):
    first, second = jnp.stack(low), jnp.stack(high)
    return jnp.where(cell == 0, first, second), jnp.where(cell == 0, second, first)


def two_sum(product, left, right):
    return (product(left[0], right[0]) + product(left[1], right[1])).astype(BF16)


def feed_sums(hidden, grad_down, wide_two, pre_grad):
    up, down = two_sum(mm_left, wide_two, pre_grad), two_sum(mm_left, hidden, grad_down)
    return [part for whole in (up, down) for part in jnp.split(whole, 2, axis=0)]


def attention_sums(wide_mid, mixed, wide_one, grads):
    def product(left, right):
        return mm(left.reshape(left.shape[0] * left.shape[1], left.shape[2]), right)

    return [two_sum(product, [grad[j] for grad in grads], wide_one) for j in range(3)] + [
        two_sum(product, mixed, wide_mid)
    ]


def shards(
    tokens,
    out_grad,
    group_order,
    lengths,
    qkv_weight,
    qv_bias,
    out_weight,
    out_bias,
    up_weight,
    up_bias,
    down_weight,
    down_bias,
    norm_gain,
    norm_shift,
):
    layer_count = qkv_weight.shape[0]
    local_width = qkv_weight.shape[3]
    seq_index = lax.axis_index(SEQ)
    cell = lax.axis_index(CELL)
    core = lax.axis_index(TENSOR) % 2
    side = seq_index // 2
    paired_cells = lax.axis_size(CELL) == 2
    gains, shifts = norm_gain.astype(F32), norm_shift.astype(F32)
    row_count = tokens.shape[1]
    head_shape = (local_width // HEAD, HEAD, row_count)
    tokens, out_grad = jnp.swapaxes(tokens, 1, 2), jnp.swapaxes(out_grad, 1, 2)
    qkv_weight = jnp.swapaxes(qkv_weight, 2, 3)
    biases = qv_bias.astype(F32)
    qkv_bias = jnp.stack([biases[:, 0], jnp.zeros_like(biases[:, 0]), biases[:, 1]], axis=1)
    line = Line()

    order = jnp.where(side == 0, group_order[0], group_order[1])
    length = jnp.where(side == 0, lengths[0], lengths[1])
    offsets = jnp.array([0, 2, 0, 2, 1, 3], jnp.int32)
    slots = 2 * (seq_index ^ offsets)[:, None] + (core + jnp.arange(2)[None]) % 2
    wanted = slots.reshape(-1, 1) == jnp.arange(order.shape[0])[None]
    blocks = jnp.sum(jnp.where(wanted, order[None], 0), axis=1)
    info = jnp.concatenate([length[None], blocks]).astype(jnp.int32)

    weights = dict(out_w=out_weight, up_w=up_weight, down_w=down_weight)
    now = line.run(
        lambda *given: start_call(*given, head_shape, 0),
        tokens,
        qkv_weight,
        qkv_bias[0],
        gains[0, :1],
        shifts[0, :1],
    )
    saved = []
    for layer in range(layer_count):
        last = layer == layer_count - 1
        got_pair = swap(now.pair[1], SEQ, 1)
        states = line.run(
            lambda queries, *pairs: attend(info, queries, pairs, 0, None, False),
            now.queries,
            *now.pair,
            now.got_pair,
        )
        mixed = line.run(
            lambda queries, states, pair: attend(info, queries, [pair], 3, states, True),
            now.queries,
            states,
            got_pair,
        )
        rows = [out_bias[layer], gains[layer, 1], shifts[layer, 1], down_bias[layer]]
        given = dict(
            base=now.stream,
            mixed=[mixed[0][0], mixed[1][0]],
            up_b=up_bias[layer].astype(F32)[None],
        )
        in_hbm = dict(weights)
        if not last:
            rows += [gains[layer + 1, 0], shifts[layer + 1, 0]]
            in_hbm.update(qkv_w=qkv_weight, out_grad=out_grad)
            given.update(qkv_b=qkv_bias[layer + 1])
        given.update(vectors=jnp.stack([row.astype(F32) for row in rows]))
        found = line.run(
            lambda given, in_hbm, layer=layer, last=last: forward_call(
                given, in_hbm, layer, last, 1 + layer
            ),
            given,
            in_hbm,
        )
        saved.append(
            types.SimpleNamespace(
                queries=now.queries,
                near_pairs=now.pair,
                far_pairs=[now.got_pair, got_pair],
                wide_one=now.wide_one,
                normed_one=now.normed_one,
                inverse_one=now.inverse_one,
                mixed=[mixed[0][0], mixed[1][0]],
                log_total=[mixed[0][1], mixed[1][1]],
                wide_two=found.wide_two,
                normed_two=found.normed_two,
                inverse_two=found.inverse_two,
                hidden=found.hidden,
                slope=found.slope,
            )
        )
        if not last:
            got_grad = found.got_grad
            now = found

    identity = layer_count + 1
    block_low = found.low
    vectors = []
    halves = {}
    for layer in reversed(range(layer_count + 1)):
        begin, end = layer == layer_count, layer == 0
        given, in_hbm = dict(), dict()
        gain_rows = [gains[0, 0], gains[0, 0]]
        riding = 0
        if begin:
            given.update(got_grad=got_grad, block_low=block_low)
            in_hbm.update(out_grad=out_grad)
        else:
            above = saved[layer]
            given.update(
                grad=found.grad_out,
                query_sum=query_sums,
                pair_sum=near_sums,
                pair_got=far_got,
                normed_one=above.normed_one,
                inverse_one=above.inverse_one,
            )
            in_hbm.update(qkv_w=qkv_weight)
            gain_rows[0] = gains[layer, 0]
            if paired_cells:
                riding = 1 if end else 2
                if end:
                    near_late = line.run(add_low, kept_late, got_late)
                    far_late = swap(near_late, SEQ, 2)
                    given.update(whole=next_whole)
                else:
                    given.update(
                        whole=line.run(add_low, *pending),
                        wide_one=above.wide_one,
                        out_piece=out_piece,
                    )
        if not end:
            below = saved[layer - 1]
            given.update(
                slope=below.slope, normed_two=below.normed_two, inverse_two=below.inverse_two
            )
            in_hbm.update(weights)
            gain_rows[1] = gains[layer - 1, 1]
        given.update(gains=jnp.stack(gain_rows))
        found = line.run(
            lambda given, in_hbm, layer=layer, riding=riding: backward_call(
                given,
                in_hbm,
                layer if layer < layer_count else None,
                layer - 1 if layer > 0 else None,
                riding,
                identity + layer,
            ),
            given,
            in_hbm,
        )
        vectors.append(found.sums)
        if begin:
            block_out = found.block
        else:
            if riding == 2:
                early = found.summed
                got_early = swap(early, CELL, 1)
                next_whole = found.whole_next
                late = line.run(add_low, *late)
                bit = seq_index % 2
                kept_late = jnp.where(bit == 0, late[0], late[1])
                got_late = swap(jnp.where(bit == 0, late[1], late[0]), SEQ, 1)
            elif not paired_cells:
                halves[layer, 1] = line.run(
                    attention_sums, wide_mid, above.mixed, above.wide_one, found.grads
                )
        if end:
            break
        wide_mid = found.wide_mid
        streams = [
            list(members)
            for members in zip(below.queries, found.mixed_grad, below.mixed, below.log_total)
        ]

        def feed_totals():
            return line.run(feed_sums, below.hidden, found.wide, below.wide_two, found.pre)

        if paired_cells:
            sums = feed_totals()
            if begin:
                cut = sums[0].shape[0] // 32 * 16 + 16
                spans = [slice(0, cut), slice(cut, None)]

                def pick_spans(low, high):
                    return [
                        pick(cell, [m[span] for m in low], [m[span] for m in high])
                        for span in spans
                    ]

                pending, late = (
                    [kept, swap(sent, CELL, 1)]
                    for kept, sent in line.run(pick_spans, sums[:2], sums[2:])
                )
            else:
                kept_feed, sent_feed = line.run(
                    functools.partial(pick, cell), sums[:2], sums[2:]
                )
                got_feed = swap(sent_feed, CELL, 1)
            out_piece = line.run(
                lambda mixed, wide: two_sum(
                    lambda left, right: mm(left.reshape(local_width, row_count), right), mixed, wide
                ),
                below.mixed,
                wide_mid,
            )
        else:
            halves[layer - 1, 0] = feed_totals()
        query_sums, far_sums = line.run(
            lambda given, pairs: attend_back(info, given, pairs, 2, False, BF16),
            streams,
            below.far_pairs,
        )
        far_got = [swap(far_sum, SEQ, 1) for far_sum in far_sums]
        streams = [members + [start] for members, start in zip(streams, query_sums)]
        query_sums, near_sums = line.run(
            lambda given, pairs: attend_back(info, given, pairs, 0, True, F32),
            streams,
            below.near_pairs,
        )

    vectors = jnp.stack(vectors)
    if not paired_cells:
        vectors = lax.psum(vectors, CELL)
    given, in_hbm = dict(low=found.low, vectors=vectors), dict()
    if paired_cells:
        given.update(
            kept_feed=kept_feed,
            got_feed=got_feed,
            grads=found.grads,
            wide_one=above.wide_one,
            out_piece=out_piece,
            near_late=near_late,
            far_late=far_late,
            near_prior=found.near_sum,
            far_prior=found.got_far,
        )
        in_hbm.update(early=early, got_early=got_early)
    closing = line.run(
        lambda given, in_hbm: closing_call(given, in_hbm, paired_cells, identity + layer_count + 1),
        given,
        in_hbm,
    )
    if paired_cells:
        feeds = [closing.all_feed, closing.all_late]
        attentions = [closing.all_last, closing.all_prior]
    else:

        def whole(part):
            found = []
            for layer in range(layer_count):
                total = lax.psum(jnp.stack(halves[layer, part]).astype(F32), (CELL, SEQ))
                found.append(total.reshape((2, 2) + total.shape[1:]))
            return found

        feeds, attentions = whole(0), whole(1)

    def final(pieces):
        return jnp.stack([piece.astype(F32) for piece in pieces])

    def quarters(member):
        return member.reshape((4,) + member.shape[2:])

    def square(member):
        return member.reshape(member.shape[0] * member.shape[1], member.shape[2])

    totals = closing.totals
    attention_rows = [totals[layer_count - layer] for layer in range(layer_count)]
    feed_rows = [totals[layer_count - 1 - layer] for layer in range(layer_count)]

    def rows_of(members, *indices):
        return jnp.stack([member[index] for member in members for index in indices])

    gain_grad = jnp.stack([rows_of(attention_rows, 0), rows_of(feed_rows, 3)], axis=1)
    shift_grad = jnp.stack([rows_of(attention_rows, 1), rows_of(feed_rows, 4)], axis=1)
    second = totals.shape[2] // 256 * 128
    qv_rows = rows_of(attention_rows, 7)
    qv_grad = jnp.stack(
        [qv_rows[:, :local_width], qv_rows[:, second : second + local_width]], axis=1
    )
    return (
        jnp.swapaxes(block_out, 1, 2),
        jnp.swapaxes(closing.tokens_grad, 1, 2),
        jnp.swapaxes(
            final([quarters(member)[:3] for member in attentions]), 2, 3
        ),
        qv_grad,
        final([quarters(member)[3] for member in attentions]),
        rows_of(feed_rows, 5),
        final([square(member[0]) for member in feeds]),
        rows_of(feed_rows, 6),
        final([square(member[1]) for member in feeds]),
        rows_of(feed_rows, 2),
        gain_grad,
        shift_grad,
    )


def solution(mesh):
    shared, by_tensor = P(), P(None, TENSOR)
    rows, last = P(CELL, SEQ, None), P(None, None, TENSOR)
    middle = P(None, TENSOR, None)
    weights = (P(None, None, None, TENSOR), last, middle, shared, last, by_tensor, middle)
    norms = (shared, shared, shared)
    return jax.shard_map(
        shards,
        mesh=mesh,
        in_specs=(rows, rows, P(CELL, None), P(CELL)) + weights + norms,
        out_specs=(rows, rows) + weights + norms,
        check_vma=False,
    )
```
